32 devices in a mesh: ctx: 16 (over z, x, core), fsdp: 2 (over y).
Axes of the slice: x: 2, y: 2, z: 4, core: 2. Of those that a mesh axis runs over, the one named last changes fastest.
Arguments:
- tokens: bfloat16 [4, 1024, 768], P('fsdp', 'ctx'), may hold values from -6 to 6
- w_qkv: bfloat16 [2, 768, 2304], P(None, ('ctx', 'fsdp')), may hold values from -0.21875 to 0.21875
- b_qv: bfloat16 [2, 1536], P(None, ('ctx', 'fsdp')), may hold values from -0.75 to 0.75
- w_proj: bfloat16 [2, 768, 768], P(None, ('ctx', 'fsdp')), may hold values from -6 to 6
- b_proj: bfloat16 [2, 768], P(None, ('ctx', 'fsdp')), may hold values from -4 to 4
- ln1_gain: bfloat16 [2, 768], P(None, ('ctx', 'fsdp')), may hold values from 0.5 to 1.5
- ln1_bias: bfloat16 [2, 768], P(None, ('ctx', 'fsdp')), may hold values from -1.5 to 1.5
- ln2_gain: bfloat16 [2, 768], P(None, ('ctx', 'fsdp')), may hold values from 0.5 to 1.5
- ln2_bias: bfloat16 [2, 768], P(None, ('ctx', 'fsdp')), may hold values from -1.5 to 1.5
- w_fc: bfloat16 [2, 768, 3072], P(None, ('ctx', 'fsdp')), may hold values from -0.21875 to 0.21875
- b_fc: bfloat16 [2, 3072], P(None, ('ctx', 'fsdp')), may hold values from -4 to 4
- w_out: bfloat16 [2, 3072, 768], P(None, ('ctx', 'fsdp')), may hold values from -0.109375 to 0.109375
- b_out: bfloat16 [2, 768], P(None, ('ctx', 'fsdp')), may hold values from -4 to 4
- d_out: bfloat16 [4, 1024, 768], P('fsdp', 'ctx'), may hold values from -6 to 6
Outputs:
- output_tokens: bfloat16 [4, 1024, 768], P('fsdp', 'ctx')
- grad_tokens: float32 [4, 1024, 768], P('fsdp', 'ctx')
- grad_w_qkv: float32 [2, 768, 2304], P(None, ('ctx', 'fsdp'))
- grad_b_qv: float32 [2, 1536], P(None, ('ctx', 'fsdp'))
- grad_w_proj: float32 [2, 768, 768], P(None, ('ctx', 'fsdp'))
- grad_b_proj: float32 [2, 768], P(None, ('ctx', 'fsdp'))
- grad_ln1_gain: float32 [2, 768], P(None, ('ctx', 'fsdp'))
- grad_ln1_bias: float32 [2, 768], P(None, ('ctx', 'fsdp'))
- grad_ln2_gain: float32 [2, 768], P(None, ('ctx', 'fsdp'))
- grad_ln2_bias: float32 [2, 768], P(None, ('ctx', 'fsdp'))
- grad_w_fc: float32 [2, 768, 3072], P(None, ('ctx', 'fsdp'))
- grad_b_fc: float32 [2, 3072], P(None, ('ctx', 'fsdp'))
- grad_w_out: float32 [2, 3072, 768], P(None, ('ctx', 'fsdp'))
- grad_b_out: float32 [2, 768], P(None, ('ctx', 'fsdp'))
The draws below stay inside these ranges and needn't reach their ends.
All inputs are finite; a program needn't handle non-finite values.
Results may differ from the reference program's by a relative error of at most 0.025.
Values may be sent and summed in bfloat16 or wider, within the bound.
No kernel may reach another device: no remote copies, remote signals or barrier semaphores. Data moves between devices by JAX's collectives and lax.ppermute only.
A program may use at most 448 MiB of HBM per device.

```python
import math
import jax
import jax.numpy as jnp
from jax import lax

D = 768
H = 12
HD = 64
FF = 3072
LAYERS = 2
LEN = 1024
SEQS = 4


def block_levels(stream_key, dims, pieces, low, largest):
    factor_of, own = 1.0, jax.random.fold_in(stream_key, 6)
    for position, shards_of in pieces:
        steps = jnp.exp(jax.random.uniform(jax.random.fold_in(own, position), (shards_of,), jnp.float32, low / len(pieces), largest / len(pieces)))
        factor_of = factor_of * jnp.repeat(steps, dims[position] // shards_of).reshape([-1 if axis == position else 1 for axis in range(len(dims))])
    return factor_of


def scatter_about(stream_key, dims, width, most, pieces=(), kind=jnp.bfloat16):
    array = jax.random.normal(stream_key, dims, jnp.float32) * width
    if len(pieces) > 0:
        array = block_levels(stream_key, dims, pieces, -0.22, 0.18) * array
    return jnp.clip(array, min=-most, max=most).astype(kind)


def setup_inputs(seed: int = 0) -> dict:
    key_of = jax.random.split(jax.random.key(seed), 15)
    return {
        "tokens": scatter_about(key_of[0], (SEQS, LEN, D), 1.0, 6.0, ((0, 2), (1, 16))),
        "w_qkv": scatter_about(key_of[1], (LAYERS, D, 3 * D), D ** -0.5, 0.21875, ((1, 32),)),
        "b_qv": scatter_about(key_of[2], (LAYERS, 2 * D), 0.05, 0.75, ((1, 32),)),
        "w_proj": scatter_about(key_of[3], (LAYERS, D, D), (max(1, 2 * D // LEN)) ** -0.5, 6.0, ((1, 32),)),
        "b_proj": scatter_about(key_of[4], (LAYERS, D), 0.3, 4.0, ((1, 32),)),
        "ln1_gain": jnp.clip(1.0 + 0.1 * jax.random.normal(key_of[5], (LAYERS, D), jnp.float32), 0.5, 1.5).astype(jnp.bfloat16),
        "ln1_bias": scatter_about(key_of[6], (LAYERS, D), 0.1, 1.5, ((1, 32),)),
        "ln2_gain": jnp.clip(1.0 + 0.1 * jax.random.normal(key_of[7], (LAYERS, D), jnp.float32), 0.5, 1.5).astype(jnp.bfloat16),
        "ln2_bias": scatter_about(key_of[8], (LAYERS, D), 0.1, 1.5, ((1, 32),)),
        "w_fc": scatter_about(key_of[9], (LAYERS, D, FF), D ** -0.5, 0.21875, ((1, 32),)),
        "b_fc": scatter_about(key_of[10], (LAYERS, FF), 0.3, 4.0, ((1, 32),)),
        "w_out": scatter_about(key_of[11], (LAYERS, FF, D), FF ** -0.5, 0.109375, ((1, 32),)),
        "b_out": scatter_about(key_of[12], (LAYERS, D), 0.3, 4.0, ((1, 32),)),
        "d_out": scatter_about(key_of[13], (SEQS, LEN, D), 1.0, 6.0, ((0, 2), (1, 16))),
    }


@jax.custom_vjp
def low(v):
    return lax.optimization_barrier(v.astype(jnp.bfloat16)).astype(jnp.float32)

@jax.custom_vjp
def low_back(v):
    return v

def low_keep(v):
    return (low(v), None)

def low_pass(kept, grad):
    return (grad,)

def back_keep(v):
    return (v, None)

def back_low(kept, grad):
    return (low(grad),)
low.defvjp(low_keep, low_pass)
low_back.defvjp(back_keep, back_low)
highest = lax.Precision.HIGHEST
masked_score = -1e+30

def norm_rows(values, gain, shift):
    center = values - lax.optimization_barrier(jnp.mean(values, -1, keepdims=True))
    spread = lax.optimization_barrier(jnp.mean(center * center, -1, keepdims=True))
    return center * lax.rsqrt(spread + 1e-05) * gain + shift

def attend(queries, keys, values):
    length = queries.shape[0]
    query_block = math.gcd(length, 512)
    positions = jnp.arange(length).astype(jnp.int32)

    def block_out(start):
        chosen = lax.dynamic_slice_in_dim(queries, start, query_block, 0)
        scores = jnp.einsum('qhe,khe->hqk', chosen, keys, precision=highest) * 0.125
        scores = low_back(scores)
        row_pos = start + jnp.arange(query_block).astype(jnp.int32)
        allowed = (positions[None, :] <= row_pos[:, None])[None]
        scores = jnp.where(allowed, scores, masked_score)
        row_top = lax.optimization_barrier(jnp.max(scores, -1, keepdims=True))
        weights = jnp.exp(scores - row_top)
        probs = weights / lax.optimization_barrier(jnp.sum(weights, -1, keepdims=True))
        return jnp.einsum('hqk,khe->qhe', low(probs), values, precision=highest)
    starts = (jnp.arange(length // query_block) * query_block).astype(jnp.int32)
    result = lax.map(jax.checkpoint(block_out), starts)
    return result.reshape(length, H * HD)

def layer(inputs, params):
    w_qkv, b_qv, w_proj, b_proj, gain_one, shift_one, gain_two, shift_two, w_fc, b_fc, w_out, b_out = params
    normed = low(norm_rows(inputs, gain_one, shift_one))
    projected = jnp.dot(normed, w_qkv, precision=highest)
    queries = low(low_back(projected[:, :D] + b_qv[:D])).reshape(-1, H, HD)
    keys = low(low_back(projected[:, D:2 * D])).reshape(-1, H, HD)
    values = low(low_back(projected[:, 2 * D:] + b_qv[D:])).reshape(-1, H, HD)
    attended = low(low_back(attend(queries, keys, values)))
    branch = low_back(jnp.dot(attended, w_proj, precision=highest) + b_proj)
    middle = inputs + branch
    normed_two = low(norm_rows(middle, gain_two, shift_two))
    up_proj = low_back(jnp.dot(normed_two, w_fc, precision=highest) + b_fc)
    activ = low(jax.nn.gelu(up_proj, approximate=True))
    mlp_out = low_back(jnp.dot(activ, w_out, precision=highest) + b_out)
    return middle + mlp_out

def reference(tokens, w_qkv, b_qv, w_proj, b_proj, ln1_gain, ln1_bias, ln2_gain, ln2_bias, w_fc, b_fc, w_out, b_out, d_out):
    params = tuple((item.astype(jnp.float32) for item in (w_qkv, b_qv, w_proj, b_proj, ln1_gain, ln1_bias, ln2_gain, ln2_bias, w_fc, b_fc, w_out, b_out)))

    def network(weights, sequence):
        for layer_no in range(LAYERS):
            sequence = layer(sequence, tuple((item[layer_no] for item in weights)))
        return sequence

    def per_sequence(totals, pair):
        sequence, cotangent = pair
        result, pull = jax.vjp(network, params, sequence)
        grads, grad_seq = pull(cotangent)
        totals = jax.tree.map(jnp.add, totals, grads)
        return (totals, (result.astype(jnp.bfloat16), grad_seq))
    zeros = jax.tree.map(jnp.zeros_like, params)
    totals, (results, grad_seqs) = lax.scan(per_sequence, zeros, (tokens.astype(jnp.float32), d_out.astype(jnp.float32)))
    return (results, grad_seqs, totals[0], totals[1], totals[2], totals[3], totals[4], totals[5], totals[6], totals[7], totals[8], totals[9], totals[10], totals[11])
```

```python
import math

import jax
import jax.numpy as jnp
import numpy as np
from jax import lax
from jax.sharding import Mesh, PartitionSpec as P

D = 768
H = 12
HD = 64
LAYERS = 2
TP = 4
PH = H // TP
PW = PH * HD
EPS = 1e-05
bf16 = jnp.bfloat16
f32 = jnp.float32

ALL = ("s", "g", "p", "c", "f")
REST = ("s", "g", "c", "f")


def dot(a, b, dims=((1,), (0,))):
    return lax.dot_general(a, b, (dims, ((), ())), preferred_element_type=f32)


def swap(value, axis, mask=1):
    size = lax.axis_size(axis)
    return lax.ppermute(value, axis, [(i, i ^ mask) for i in range(size)])


def norm_stats(values):
    center = values - jnp.mean(values, -1, keepdims=True)
    scale = lax.rsqrt(jnp.mean(center * center, -1, keepdims=True) + EPS)
    return center * scale, scale


def norm_low(values, gain, shift):
    unit, _ = norm_stats(values)
    return (unit * gain + shift).astype(bf16)


def norm_back(values, gain, cotangent):
    unit, scale = norm_stats(values)
    inner = cotangent * gain
    grad = scale * (
        inner
        - jnp.mean(inner, -1, keepdims=True)
        - unit * jnp.mean(inner * unit, -1, keepdims=True)
    )
    return grad, jnp.sum(cotangent * unit, 0), jnp.sum(cotangent, 0)


def gelu(u):
    return 0.5 * u * (1.0 + jnp.tanh(math.sqrt(2.0 / math.pi) * (u + 0.044715 * u * u * u)))


def gelu_slope(u):
    root = math.sqrt(2.0 / math.pi)
    t = jnp.tanh(root * (u + 0.044715 * u * u * u))
    return 0.5 * (1.0 + t) + 0.5 * u * (1.0 - t * t) * root * (1.0 + 3 * 0.044715 * u * u)


def attend(qkv, keys_values, mask):
    q, k, v = qkv[:, :PW], keys_values[:, :PW], keys_values[:, PW:]
    q, k, v = (item.reshape(-1, PH, HD) for item in (q, k, v))
    scores = jnp.einsum("qhe,khe->hqk", q, k, preferred_element_type=f32) * 0.125
    scores = jnp.where(mask, scores, -1e30)
    top = jnp.max(scores, -1, keepdims=True)
    weights = jnp.exp(scores - top)
    total = jnp.sum(weights, -1, keepdims=True)
    probs = (weights / total).astype(bf16)
    out = jnp.einsum("hqk,khe->qhe", probs, v, preferred_element_type=f32)
    return out.reshape(-1, PW), top + jnp.log(total)


def attend_back(qkv, keys_values, mask, out, log_total, grad_out):
    q, k, v = qkv[:, :PW], keys_values[:, :PW], keys_values[:, PW:]
    q, k, v, g = (item.reshape(-1, PH, HD) for item in (q, k, v, grad_out))
    scores = jnp.einsum("qhe,khe->hqk", q, k, preferred_element_type=f32) * 0.125
    probs = jnp.where(mask, jnp.exp(scores - log_total), 0.0)
    delta = jnp.sum((grad_out.astype(f32) * out).reshape(-1, PH, HD), -1).T[:, :, None]
    grad_probs = jnp.einsum("qhe,khe->hqk", g, v, preferred_element_type=f32)
    grad_scores = (probs * (grad_probs - delta)).astype(bf16)
    dq = 0.125 * jnp.einsum("hqk,khe->qhe", grad_scores, k, preferred_element_type=f32)
    dk = 0.125 * jnp.einsum("hqk,qhe->khe", grad_scores, q, preferred_element_type=f32)
    dv = jnp.einsum("hqk,qhe->khe", probs.astype(bf16), g, preferred_element_type=f32)
    dkv = jnp.concatenate([dk.reshape(-1, PW), dv.reshape(-1, PW)], 1)
    return dq.reshape(-1, PW), dkv


def share(own):
    return [own] + [swap(own, "p", k) for k in range(1, TP)]


def gather_sum(parts):
    total = parts[0]
    for k in range(1, TP):
        total = total + swap(parts[k].astype(bf16), "p", k).astype(f32)
    return total


def body(tokens, w_qkv, b_qv, w_proj, b_proj, ln1_gain, ln1_bias, ln2_gain, ln2_bias, w_fc, b_fc, w_out, b_out, d_out):
    size = {name: lax.axis_size(name) for name in ALL}
    devices = math.prod(size.values())
    copies = devices // TP
    blocks = devices // size["f"]
    rows = tokens.shape[1]
    shard = w_qkv.shape[1]
    ff = w_fc.shape[2]
    fs = ff // TP
    s, g, p, c = (lax.axis_index(name) for name in ("s", "g", "p", "c"))

    to_chip = []
    for e in range(copies):
        left, fi = divmod(e, size["f"])
        left, ci = divmod(left, size["c"])
        si, gi = divmod(left, size["g"])
        for q in range(TP):
            target = (((si * size["g"] + gi) * TP + q) * size["c"] + ci) * size["f"] + fi
            to_chip.append((q * copies + e, target))
    to_owner = [(b, a) for a, b in to_chip]

    def own_sequence(value):
        kept = lax.dynamic_index_in_dim(value, s, 0, keepdims=False)
        sent = lax.dynamic_index_in_dim(value, 1 - s, 0, keepdims=False)
        got = swap(sent, "s")
        return jnp.where(s == 0, jnp.stack([kept, got]), jnp.stack([got, kept])).reshape(-1, D)

    def back_to_blocks(value):
        value = value.reshape(2, rows, D)
        kept = lax.dynamic_index_in_dim(value, s, 0, keepdims=False)
        sent = lax.dynamic_index_in_dim(value, 1 - s, 0, keepdims=False)
        got = swap(sent, "s")
        return jnp.where(s == 0, jnp.stack([kept, got]), jnp.stack([got, kept]))

    def by_chip(pieces):
        sent = jnp.broadcast_to(
            pieces[None, None, :, None, None],
            (size["s"], size["g"], TP, size["c"], size["f"]) + pieces.shape[1:],
        ).reshape((devices,) + pieces.shape[1:])
        return lax.all_to_all(sent, ALL, 0, 0, tiled=True).reshape(devices * pieces.shape[1], -1)

    small = jnp.concatenate(
        [item.reshape(LAYERS, -1) for item in (b_proj, b_out, ln1_gain, ln1_bias, ln2_gain, ln2_bias, b_qv, b_fc)], 1
    )
    width = small.shape[1]
    small = jnp.broadcast_to(small.reshape(1, -1), (devices, LAYERS * width))
    small = lax.all_to_all(small, ALL, 0, 0, tiled=True).reshape(devices, LAYERS, width)

    qkv_cols = [
        w_qkv[l].reshape(shard, 3, TP, PW).transpose(2, 0, 1, 3).reshape(TP, shard, 3 * PW) for l in range(LAYERS)
    ]
    fc_cols = [w_fc[l].reshape(shard, TP, fs).transpose(1, 0, 2) for l in range(LAYERS)]
    wq = [None] * LAYERS
    wf = [None] * LAYERS
    wq[0] = by_chip(qkv_cols[0])
    x_own = own_sequence(tokens)
    x_all = jnp.concatenate(share(x_own), 0).astype(f32)
    wf[0] = by_chip(fc_cols[0])
    out_rows = lax.ppermute(w_out, ALL, to_chip)
    wo, wp = [], []
    for l in range(LAYERS):
        wp.append(lax.all_gather(w_proj[l], ALL, axis=0, tiled=True))
        wo.append(lax.all_gather(out_rows[l], REST, axis=0, tiled=True))
    for l in range(1, LAYERS):
        wq[l] = by_chip(qkv_cols[l])
        wf[l] = by_chip(fc_cols[l])

    def vector(l, start, count):
        return small[:, l, start : start + count].reshape(-1).astype(f32)

    vec = []
    for l in range(LAYERS):
        at = 0
        names = {}
        for name, count in (
            ("b_proj", shard), ("b_out", shard), ("g1", shard), ("s1", shard), ("g2", shard), ("s2", shard),
            ("b_qv", 2 * shard), ("b_fc", ff // devices),
        ):
            names[name] = vector(l, at, count)
            at += count
        zero = jnp.zeros((PW,), f32)
        names["b_qkv"] = jnp.concatenate(
            [
                lax.dynamic_slice_in_dim(names["b_qv"], p * PW, PW),
                zero,
                lax.dynamic_slice_in_dim(names["b_qv"], D + p * PW, PW),
            ]
        )
        names["b_up"] = lax.dynamic_slice_in_dim(names["b_fc"], p * fs, fs)
        vec.append(names)

    half = jnp.arange(2)[None, :, None]
    inside = jnp.arange(rows)[None, None, :]
    piece = jnp.arange(TP)[:, None, None]

    def positions(group, core):
        return (((group * TP + (p ^ piece)) * 2 + core + half * (blocks // 2)) * rows + inside).reshape(-1)

    q_pos = positions(g, c)
    k_pos = jnp.concatenate([positions(gi, core) for gi in range(size["g"]) for core in (0, 1)])
    mask = (k_pos[None, :] <= q_pos[:, None])[None]

    def all_keys(kv):
        other = swap(kv, "c")
        both = jnp.where(c == 0, jnp.stack([kv, other]), jnp.stack([other, kv])).reshape(-1, kv.shape[1])
        if size["g"] > 1:
            both = lax.all_gather(both, "g", axis=0, tiled=True)
        return both

    def own_keys_grad(dkv):
        if size["g"] > 1:
            dkv = lax.psum_scatter(dkv, "g", scatter_dimension=0, tiled=True)
        dkv = dkv.reshape(2, -1, dkv.shape[1])
        kept = lax.dynamic_index_in_dim(dkv, c, 0, keepdims=False)
        sent = lax.dynamic_index_in_dim(dkv, 1 - c, 0, keepdims=False)
        return kept + swap(sent.astype(bf16), "c").astype(f32)

    saved = []
    for l in range(LAYERS):
        v = vec[l]
        normed = norm_low(x_all, v["g1"], v["s1"])
        qkv = (dot(normed, wq[l]) + v["b_qkv"]).astype(bf16)
        kv = all_keys(qkv[:, PW:])
        out, log_total = attend(qkv, kv, mask)
        low = out.astype(bf16)
        heads = share(low.reshape(TP, -1, PW))
        heads = [jnp.stack([heads[k][m ^ k] for m in range(TP)]).reshape(-1, PW) for k in range(TP)]
        w_rows = [lax.dynamic_slice_in_dim(wp[l], (p ^ k) * PW, PW, 0) for k in range(TP)]
        proj = dot(jnp.concatenate(heads, 1), jnp.concatenate(w_rows, 0))
        mid = x_all + proj + v["b_proj"]
        normed2 = norm_low(mid, v["g2"], v["s2"])
        up = dot(normed2, wf[l]) + v["b_up"]
        act = gelu(up).astype(bf16)
        part = dot(act, wo[l]).reshape(TP, -1, D)
        mlp = gather_sum(part)
        saved.append((x_all, normed, qkv, kv, out, log_total, low, mid, normed2, up, act, w_rows[0]))
        if l + 1 < LAYERS:
            x_all = mid + jnp.concatenate(share(mlp.astype(bf16)), 0).astype(f32) + v["b_out"]
        else:
            tokens_out = mid[: mlp.shape[0]] + mlp + v["b_out"]
    own_rows = tokens_out.shape[0]
    output = back_to_blocks(tokens_out.astype(bf16))

    def send_columns(grad):
        got = lax.all_to_all(grad.astype(bf16).reshape(devices, shard, -1), ALL, 0, 0, tiled=True)
        got = got.reshape(size["s"], size["g"], TP, size["c"], size["f"], shard, -1).astype(f32)
        return jnp.sum(got, (0, 1, 3, 4))

    def send_rows(grad):
        got = lax.all_to_all(grad.astype(bf16).reshape(copies, -1, D), REST, 0, 0, tiled=True)
        return lax.ppermute(jnp.sum(got.astype(f32), 0), ALL, to_owner)

    grads = [None] * LAYERS
    small_grads = [None] * LAYERS
    g_own = own_sequence(d_out)
    g_all = jnp.concatenate(share(g_own), 0)
    g_own = g_own.astype(f32)
    for l in reversed(range(LAYERS)):
        v = vec[l]
        x_all, normed, qkv, kv, out, log_total, low, mid, normed2, up, act, wp_own = saved[l]
        d_b_out = jnp.sum(g_all[:own_rows].astype(f32), 0)
        d_wo = send_rows(dot(act, g_all, ((0,), (0,))))
        g_act = dot(g_all, wo[l], ((1,), (1,)))
        g_up = (gelu_slope(up) * g_act).astype(bf16)
        d_wf = send_columns(dot(normed2, g_up, ((0,), (0,))))
        d_b_fc = jnp.sum(g_up.astype(f32), 0)
        g_norm2 = gather_sum(dot(g_up, wf[l], ((1,), (1,))).reshape(TP, -1, D))
        g_mid, d_g2, d_s2 = norm_back(mid[:own_rows], v["g2"], g_norm2)
        g_mid = g_own + g_mid
        g_attn_own = g_mid.astype(bf16)
        g_attn = jnp.concatenate(share(g_attn_own), 0)
        d_b_proj = jnp.sum(g_attn_own.astype(f32), 0)
        d_wp = send_rows(dot(low, g_attn, ((0,), (0,))))
        g_out = dot(g_attn, wp_own, ((1,), (1,))).astype(bf16)
        dq, dkv = attend_back(qkv, kv, mask, out, log_total, g_out)
        dkv = own_keys_grad(dkv)
        g_qkv = jnp.concatenate([dq, dkv], 1).astype(bf16)
        d_wq = send_columns(dot(normed, g_qkv, ((0,), (0,))))
        d_b_qkv = jnp.sum(g_qkv.astype(f32), 0)
        g_norm = gather_sum(dot(g_qkv, wq[l], ((1,), (1,))).reshape(TP, -1, D))
        g_in, d_g1, d_s1 = norm_back(x_all[:own_rows], v["g1"], g_norm)
        g_own = g_mid + g_in
        if l > 0:
            g_all = jnp.concatenate(share(g_own.astype(bf16)), 0)
        grads[l] = (
            d_wq.reshape(TP, shard, 3, PW).transpose(1, 2, 0, 3).reshape(shard, 3 * D),
            d_wp,
            d_wf.transpose(1, 0, 2).reshape(shard, ff),
            d_wo,
        )
        whole_qv = lax.dynamic_update_slice_in_dim(jnp.zeros((2, D), f32), d_b_qkv.reshape(3, PW)[::2], p * PW, 1)
        whole_fc = lax.dynamic_update_slice_in_dim(jnp.zeros((ff,), f32), d_b_fc, p * fs, 0)
        small_grads[l] = [
            item.reshape(devices, -1)
            for item in (d_b_proj, d_b_out, d_g1, d_s1, d_g2, d_s2, whole_qv, whole_fc)
        ]
    grad_tokens = back_to_blocks(g_own)
    sent = jnp.concatenate([item for l in range(LAYERS) for item in small_grads[l]], 1)
    got = jnp.sum(lax.all_to_all(sent, ALL, 0, 0, tiled=True), 0).reshape(LAYERS, -1)
    parts = []
    at = 0
    for count in [shard] * 6 + [2 * shard, ff // devices]:
        parts.append(got[:, at : at + count])
        at += count
    d_b_proj, d_b_out, d_g1, d_s1, d_g2, d_s2, d_b_qv, d_b_fc = parts
    d_wq, d_wp, d_wf, d_wo = (jnp.stack([grads[l][i] for l in range(LAYERS)]) for i in range(4))
    return (output, grad_tokens, d_wq, d_b_qv, d_wp, d_b_proj, d_g1, d_s1, d_g2, d_s2, d_wf, d_b_fc, d_wo, d_b_out)


def solution(mesh):
    ctx, pair = mesh.shape["ctx"], mesh.shape["fsdp"]
    groups = ctx // (2 * TP * 2)
    view = Mesh(mesh.devices.reshape(2, groups, TP, 2, pair), ALL)
    along = ("s", "g", "p", "c")
    token = P("f", along, None)
    matrix = P(None, ALL, None)
    line = P(None, ALL)
    in_specs = (token, matrix, line, matrix, line, line, line, line, line, matrix, line, matrix, line, token)
    out_specs = (token, token, matrix, line, matrix, line, line, line, line, line, matrix, line, matrix, line)
    return jax.shard_map(body, mesh=view, in_specs=in_specs, out_specs=out_specs, check_vma=False)
```

```python
import functools
import math

import jax
import jax.numpy as jnp
from jax import lax
from jax.experimental import pallas as pl
from jax.experimental.pallas import tpu as pltpu
from jax.sharding import Mesh, PartitionSpec as P

D = 768
H = 12
HD = 64
LAYERS = 2
TP = 4
PH = H // TP
PW = PH * HD
EPS = 1e-05
ROOT = math.sqrt(2.0 / math.pi)
bf16 = jnp.bfloat16
f32 = jnp.float32

ALL = ("h", "g", "x", "c", "f")
COPIES = ("h", "g")
SLOTS = 12


def dot(a, b, dims=((1,), (0,)), precision=None):
    return lax.dot_general(a, b, (dims, ((), ())), preferred_element_type=f32, precision=precision)


NT = ((1,), (1,))
TN = ((0,), (0,))


def swap(value, axis, mask=1):
    names = (axis,) if isinstance(axis, str) else axis
    size = math.prod(lax.axis_size(name) for name in names)
    return lax.ppermute(value, axis, [(i, i ^ mask) for i in range(size)])


def chip_swap(value, mask):
    return swap(value, ("x", "f"), mask % 2 * 2 + mask // 2)


def share(own):
    return [own] + [chip_swap(own, k) for k in range(1, TP)]


def launch(kernel, name, outs, scalars, *args, scratch=(), flops=0):
    shapes = [jax.ShapeDtypeStruct(shape, kind) for shape, kind in outs]
    moved = sum(a.size * a.dtype.itemsize for a in args) + sum(math.prod(o.shape) * o.dtype.itemsize for o in shapes)
    return pl.pallas_call(
        kernel,
        name=name,
        out_shape=shapes,
        in_specs=[pl.BlockSpec(memory_space=pltpu.SMEM)] + [pl.BlockSpec(memory_space=pltpu.VMEM)] * len(args),
        out_specs=[pl.BlockSpec(memory_space=pltpu.VMEM)] * len(shapes),
        scratch_shapes=list(scratch),
        cost_estimate=pl.CostEstimate(flops=flops, bytes_accessed=moved, transcendentals=0),
        compiler_params=pltpu.CompilerParams(vmem_limit_bytes=56 * 1024 * 1024),
    )(scalars, *args)


def unit_rows(values):
    center = values - jnp.mean(values, -1, keepdims=True)
    scale = lax.rsqrt(jnp.mean(center * center, -1, keepdims=True) + EPS)
    return center * scale, scale


def interleave(shard):
    block = D // 2
    per = block // (TP * shard)
    row = lax.broadcasted_iota(jnp.int32, (block, block), 0)
    col = lax.broadcasted_iota(jnp.int32, (block, block), 1)
    chip, rest = lax.div(row, per * shard), lax.rem(row, per * shard)
    target = lax.div(rest, shard) * (TP * shard) + chip * shard + lax.rem(rest, shard)
    return (col == target).astype(bf16)


def first_pieces_kernel(where, w_qkv, *refs):
    small, outs, (lines, cols) = refs[:8], refs[8 : 8 + TP], refs[8 + TP :]
    p = where[1]
    shard = cols.shape[1]
    lines[...] = jnp.zeros_like(lines)
    at = 0
    for l in range(LAYERS):
        for item in small:
            for first in range(0, item.shape[1], shard):
                lines[at : at + 1, :shard] = item[l : l + 1, first : first + shard].astype(f32)
                at += 1
    columns = lines[...].T[:shard, :HD]
    for q in range(TP):
        parts = [w_qkv[0, :, j * D + q * PW : j * D + (q + 1) * PW].astype(f32) for j in range(3)]
        cols[q] = jnp.concatenate(parts + [columns], 1).astype(bf16)
    for k, out in enumerate(outs):
        out[...] = cols[jnp.bitwise_xor(p, k)]


def layer_pieces_kernel(layer, qkv):
    def kernel(where, w_fc, w_out, w_proj, w_qkv, *refs):
        outs, (cols,) = refs[:TP], refs[TP:]
        p = where[1]
        shard = w_proj.shape[1]
        block = D // 2
        order = interleave(shard)
        fc = [dot(w_fc[layer, :, b * block : (b + 1) * block], order, NT) for b in range(w_fc.shape[2] // block)]
        for q in range(TP):
            lanes = slice(q * block // TP, (q + 1) * block // TP)
            cols[q, :, :D] = jnp.concatenate([item[:, lanes] for item in fc], 1).astype(bf16)
            if qkv is not None:
                parts = [w_qkv[qkv, :, j * D + q * PW : j * D + (q + 1) * PW] for j in range(3)]
                cols[q, :, D:] = jnp.concatenate(parts, 1)
        for k, out in enumerate(outs):
            q = jnp.bitwise_xor(p, k)
            out[:, :D] = cols[q, :, :D]
            out[:, D : 2 * D] = w_out[layer, q]
            out[:, 2 * D : 3 * D] = w_proj[layer]
            if qkv is not None:
                out[:, 3 * D :] = cols[q, :, D:]

    return kernel


def arrange_first_kernel(sizes):
    def kernel(where, got, w_out, table, columns, blocks):
        p, c = where[1], where[2]
        devices, shard = w_out.shape[:2]
        groups = sizes["g"]
        columns[...] = jnp.zeros_like(columns)
        for d in range(devices):
            rest, fi = divmod(d, 2)
            rest, ci = divmod(rest, 2)
            rest, xi = divmod(rest, 2)
            copy = jnp.bitwise_xor(c, ci) * sizes["h"] * groups + rest
            one = got[copy * TP + jnp.bitwise_xor(p, 2 * fi + xi)].astype(f32)
            w_out[d] = one[:, : 3 * PW].astype(bf16)
            columns[d * shard : (d + 1) * shard, :HD] = one[:, 3 * PW :]
            blocks[d] = one[:, 3 * PW :]
        lines = columns[...].T
        per = PW // (2 * shard)
        for l in range(LAYERS):
            base = SLOTS * l
            table[8 * l : 8 * l + 6, :] = lines[base : base + 6]
            parts = []
            for first in (0, devices // 2):
                for j in range(per):
                    block = blocks[first + p * per + j]
                    parts += [block[:, base + 6 : base + 7], block[:, base + 7 : base + 8]]
                if first == 0:
                    parts.append(jnp.zeros((PW, 1), f32))
            parts.append(jnp.zeros((D - 3 * PW, 1), f32))
            bias = jnp.broadcast_to(jnp.concatenate(parts, 0), (D, 128)).T
            table[8 * l + 6 : 8 * l + 7, :] = bias[0:1]
            row = lines[base + 8 : base + 9]
            for q in range(1, TP):
                row = jnp.where(p == q, lines[base + 8 + q : base + 9 + q], row)
            table[8 * l + 7 : 8 * l + 8, :] = row

    return kernel


def finish_feed_kernel(where, *refs):
    pieces, (wf_out, wo_out, cols) = refs[: LAYERS * TP], refs[LAYERS * TP :]
    p = where[1]
    shard = wf_out.shape[1]
    block = D // 2
    order = interleave(shard)
    for l in range(LAYERS):
        for k in range(TP):
            cols[jnp.bitwise_xor(p, k)] = pieces[l * TP + k][...]
        fc = [cols[q, :, :D].astype(f32) for q in range(TP)]
        for b in range(wf_out.shape[2] // block):
            lanes = slice(b * block // TP, (b + 1) * block // TP)
            joined = jnp.concatenate([item[:, lanes] for item in fc], 1).astype(bf16)
            wf_out[l, :, b * block : (b + 1) * block] = dot(joined, order)
        for q in range(TP):
            wo_out[l, q] = cols[q, :, D:].astype(f32)


def finish_mixed_kernel(where, last, m0, m1, m2, m3, wq_out, wp_out, *refs):
    small_outs, (cols, square) = refs[:8], refs[8:]
    p = where[1]
    shard = wq_out.shape[1]
    columns = jnp.zeros((shard, 128), f32)
    for q in range(TP):
        total = jnp.zeros((shard, D + 128), f32)
        for copy in range(last.shape[0] // TP):
            total = total + last[(copy * 2 + q % 2) * 2 + q // 2].astype(f32)
        columns = columns + total[:, D:]
        cols[0, q] = total[:, :D]
    for k, m in enumerate((m0, m1, m2, m3)):
        cols[1, jnp.bitwise_xor(p, k)] = m[...].astype(f32)
    for l in range(LAYERS):
        for j in range(3):
            wq_out[l, :, j * D : (j + 1) * D] = jnp.concatenate(
                [cols[l, q, :, j * PW : (j + 1) * PW] for q in range(TP)], 1
            )
        wp_out[l] = jnp.concatenate([cols[l, q, :, 3 * PW :] for q in range(TP)], 1)
    square[...] = jnp.zeros_like(square)
    square[:shard, :] = columns
    lines = square[...].T
    at = 0
    for l in range(LAYERS):
        for out in small_outs:
            for first in range(0, out.shape[1], shard):
                out[l : l + 1, first : first + shard] = lines[at : at + 1, :shard]
                at += 1


def enter_kernel(first, index):
    def kernel(where, table, wq, *refs):
        *inputs, x_out, xo_out, n_out, q_out, kv_out = refs
        if not first:
            mid, *inputs = inputs
        t = table
        gain, shift, bias = (t[8 * index + i : 8 * index + i + 1, :] for i in (2, 3, 6))
        rows = n_out.shape[0] // TP
        for k in range(TP):
            at = slice(k * rows, (k + 1) * rows)
            x = inputs[k][...].astype(f32)
            if not first:
                x = mid[at, :] + x + t[8 * (index - 1) + 1 : 8 * (index - 1) + 2, :]
            x_out[at, :] = x
            if k == 0:
                xo_out[...] = x
            unit, _ = unit_rows(x)
            n_out[at, :] = (unit * gain + shift).astype(bf16)
        got = (dot(n_out[...], wq[...]) + bias[:, : 3 * PW]).astype(bf16)
        q_out[...] = got[:, :PW]
        kv_out[...] = got[:, PW:]

    return kernel


def tile_rows(p, t, size):
    return pl.multiple_of((jnp.bitwise_xor(t % TP, p) * 2 + t // TP) * size, size)


def masks(c, chunk, size):
    a = lax.broadcasted_iota(jnp.int32, (chunk, chunk), 0)
    b = lax.broadcasted_iota(jnp.int32, (chunk, chunk), 1)
    return b <= a, lax.div(b, size) < lax.div(a, size) + c


def attend_kernel(where, q_ref, own_ref, oth_ref, out_ref, lse_ref, qn, kn, on, outn):
    p, c = where[1], where[2]
    count = q_ref.shape[0]
    size = count // (2 * TP)
    chunk = 2 * size
    for t in range(2 * TP):
        at = pl.ds(tile_rows(p, t, size), size)
        here = slice(t * size, (t + 1) * size)
        qn[here, :] = q_ref[at, :]
        kn[here, :] = own_ref[at, :]
        on[here, :] = oth_ref[at, :]
    ok_own, ok_oth = masks(c, chunk, size)
    for j in range(count // chunk):
        rows = slice(j * chunk, (j + 1) * chunk)
        outs = []
        for h in range(PH):
            lanes = slice(h * HD, (h + 1) * HD)
            vlanes = slice(PW + h * HD, PW + (h + 1) * HD)
            q = qn[rows, lanes]
            scores = []
            for keys, ok in ((kn, ok_own), (on, ok_oth)):
                if j > 0:
                    scores.append(dot(q, keys[: j * chunk, lanes], NT) * 0.125)
                scores.append(jnp.where(ok, dot(q, keys[rows, lanes], NT) * 0.125, -1e30))
            top = functools.reduce(jnp.maximum, [jnp.max(v, -1, keepdims=True) for v in scores])
            weights = [jnp.exp(v - top) for v in scores]
            total = sum(jnp.sum(v, -1, keepdims=True) for v in weights)
            low = [v.astype(bf16) for v in weights]
            out = jnp.zeros((chunk, HD), f32)
            for i, keys in enumerate((kn, on)):
                if j > 0:
                    out = out + dot(low[2 * i], keys[: j * chunk, vlanes])
                    out = out + dot(low[2 * i + 1], keys[rows, vlanes])
                else:
                    out = out + dot(low[i], keys[rows, vlanes])
            outs.append(out / total)
            lse_ref[rows, h : h + 1] = top + jnp.log(total)
        outn[rows, :] = jnp.concatenate(outs, 1).astype(bf16)
    for t in range(2 * TP):
        out_ref[pl.ds(tile_rows(p, t, size), size), :] = outn[t * size : (t + 1) * size, :]


def middle_kernel(index):
    def kernel(where, table, x, o0, o1, o2, o3, wp, wf, wo, mid_out, mo_out, heads_out, n_out, up_out, act_out, y0, y1, y2, y3, got):
        p = where[1]
        t = table
        b_proj, gain, shift, b_up = (t[8 * index + i : 8 * index + i + 1, :] for i in (0, 4, 5, 7))
        rows = x.shape[0] // TP
        for k, o in enumerate((o0, o1, o2, o3)):
            for m in range(TP):
                got[k, m * rows : (m + 1) * rows, :] = o[(m ^ k) * rows : ((m ^ k) + 1) * rows, :]
        heads_out[...] = jnp.concatenate([got[jnp.bitwise_xor(p, q)] for q in range(TP)], 1)
        for m, y in enumerate((y0, y1, y2, y3)):
            at = slice(m * rows, (m + 1) * rows)
            mid = x[at, :] + dot(heads_out[at, :], wp[...]) + b_proj
            mid_out[at, :] = mid
            if m == 0:
                mo_out[...] = mid
            unit, _ = unit_rows(mid)
            n_out[at, :] = (unit * gain + shift).astype(bf16)
        up = dot(n_out[...], wf[...]) + b_up
        up_out[...] = up
        act_out[...] = (0.5 * up * (1.0 + jnp.tanh(ROOT * (up + 0.044715 * up * up * up)))).astype(bf16)
        for m, y in enumerate((y0, y1, y2, y3)):
            at = slice(m * rows, (m + 1) * rows)
            y[...] = dot(act_out[at, :], wo[...]).astype(y.dtype)

    return kernel


def part_sums(part, unit, acc):
    acc[0:1, :] += jnp.sum(part * unit, 0, keepdims=True)
    acc[1:2, :] += jnp.sum(part, 0, keepdims=True)


def feed_back_kernel(where, g0, g1, g2, g3, up, mid, wo, wf, g_out, gu_out, bfc_out, sums_out, y0, y1, y2, y3):
    rows = g0.shape[0]
    for k, g in enumerate((g0, g1, g2, g3)):
        g_out[k * rows : (k + 1) * rows, :] = g[...]
    bfc_out[...] = jnp.zeros_like(bfc_out)
    sums_out[...] = jnp.zeros_like(sums_out)
    for k, y in enumerate((y0, y1, y2, y3)):
        at = slice(k * rows, (k + 1) * rows)
        g_act = dot(g_out[at, :], wo[...], NT)
        u = up[at, :]
        t = jnp.tanh(ROOT * (u + 0.044715 * u * u * u))
        slope = 0.5 * (1.0 + t) + 0.5 * u * (1.0 - t * t) * (ROOT * (1.0 + 3 * 0.044715 * u * u))
        g_up = (slope * g_act).astype(bf16)
        gu_out[at, :] = g_up
        bfc_out[0:1, :] += jnp.sum(g_up.astype(f32), 0, keepdims=True)
        part = dot(g_up, wf[...], NT)
        y[...] = part.astype(y.dtype)
        unit, _ = unit_rows(mid[at, :])
        part_sums(part, unit, sums_out)


def norm_back_kernel(index, which):
    def kernel(where, table, grad, value, r0, r1, r2, r3, g_out, low_out, sum_out):
        gain = table[8 * index + which : 8 * index + which + 1, :]
        cot = r0[...] + r1[...].astype(f32) + r2[...].astype(f32) + r3[...].astype(f32)
        unit, scale = unit_rows(value[...])
        inner = cot * gain
        moved = scale * (
            inner - jnp.mean(inner, -1, keepdims=True) - unit * jnp.mean(inner * unit, -1, keepdims=True)
        )
        total = grad[...].astype(f32) + moved
        g_out[...] = total
        low = total.astype(bf16)
        low_out[...] = low
        sum_out[...] = jnp.zeros_like(sum_out)
        sum_out[0:1, :] = jnp.sum(low.astype(f32), 0, keepdims=True)

    return kernel


def attend_back_kernel(where, g0, g1, g2, g3, wp, q_ref, own_ref, oth_ref, lse_ref, ga_out, dq_ref, down_ref, doth_ref, local, gn, qn, kn, on, dqn, dkn, don):
    p, c = where[1], where[2]
    count = q_ref.shape[0]
    size = count // (2 * TP)
    chunk = 2 * size
    rows_of = g0.shape[0]
    for k, g in enumerate((g0, g1, g2, g3)):
        ga_out[k * rows_of : (k + 1) * rows_of, :] = g[...]
    mine = wp[pl.ds(pl.multiple_of(p * PW, PW), PW), :]
    local[...] = dot(ga_out[...], mine, NT)
    for t in range(2 * TP):
        at = pl.ds(tile_rows(p, t, size), size)
        here = slice(t * size, (t + 1) * size)
        gn[here, :] = local[at, :].astype(bf16)
        qn[here, :] = q_ref[at, :]
        kn[here, :] = own_ref[at, :]
        on[here, :] = oth_ref[at, :]
    dkn[...] = jnp.zeros_like(dkn)
    don[...] = jnp.zeros_like(don)
    ok_own, ok_oth = masks(c, chunk, size)
    for j in range(count // chunk):
        rows = slice(j * chunk, (j + 1) * chunk)
        dqs = []
        for h in range(PH):
            lanes = slice(h * HD, (h + 1) * HD)
            vlanes = slice(PW + h * HD, PW + (h + 1) * HD)
            q, g = qn[rows, lanes], gn[rows, lanes]
            lse = lse_ref[rows, h : h + 1]
            work = []
            for keys, sums, ok in ((kn, dkn, ok_own), (on, don, ok_oth)):
                if j > 0:
                    work.append((keys, sums, slice(0, j * chunk), None))
                work.append((keys, sums, rows, ok))
            probs, grads = [], []
            delta = jnp.zeros((chunk, 1), f32)
            for keys, sums, span, ok in work:
                scores = dot(q, keys[span, lanes], NT) * 0.125 - lse
                if ok is not None:
                    scores = jnp.where(ok, scores, -1e30)
                prob = jnp.exp(scores)
                grad = dot(g, keys[span, vlanes], NT)
                delta = delta + jnp.sum(prob * grad, -1, keepdims=True)
                probs.append(prob)
                grads.append(grad)
            dq = jnp.zeros((chunk, HD), f32)
            for (keys, sums, span, ok), prob, grad in zip(work, probs, grads):
                ds = (prob * (grad - delta)).astype(bf16)
                dq = dq + dot(ds, keys[span, lanes])
                sums[span, lanes] += 0.125 * dot(ds, q, TN)
                sums[span, vlanes] += dot(prob.astype(bf16), g, TN)
            dqs.append(0.125 * dq)
        dqn[rows, :] = jnp.concatenate(dqs, 1)
    for t in range(2 * TP):
        at = pl.ds(tile_rows(p, t, size), size)
        here = slice(t * size, (t + 1) * size)
        dq_ref[at, :] = dqn[here, :].astype(bf16)
        down_ref[at, :] = dkn[here, :]
        doth_ref[at, :] = don[here, :].astype(bf16)


def leave_kernel(where, dq, dkv, more, wq, x, gq_out, bq_out, sums_out, y0, y1, y2, y3):
    gq_out[:, :PW] = dq[...]
    gq_out[:, PW:] = (dkv[...] + more[...].astype(f32)).astype(bf16)
    bq_out[...] = jnp.zeros_like(bq_out)
    bq_out[0:1, : 3 * PW] = jnp.sum(gq_out[...].astype(f32), 0, keepdims=True)
    sums_out[...] = jnp.zeros_like(sums_out)
    rows = x.shape[0] // TP
    for k, y in enumerate((y0, y1, y2, y3)):
        at = slice(k * rows, (k + 1) * rows)
        part = dot(gq_out[at, :], wq[...], NT)
        y[...] = part.astype(y.dtype)
        unit, _ = unit_rows(x[at, :])
        part_sums(part, unit, sums_out)


def arrange_kernel(widths):
    def kernel(where, own, oth, *outs):
        p, c = where[1], where[2]
        devices = outs[0].shape[0]

        def one(d, carry):
            core = lax.rem(lax.div(d, 2), 2)
            chip = lax.rem(d, 2) * 2 + lax.rem(lax.div(d, 4), 2)
            block = lax.div(d, 8) * TP + jnp.bitwise_xor(chip, p)
            for source, here in ((own, core == c), (oth, core != c)):

                @pl.when(here)
                def _():
                    at = 0
                    for out, width in zip(outs, widths):
                        out[d] = source[block, :, at : at + width]
                        at += width

            return carry

        lax.fori_loop(0, devices, one, 0)

    return kernel


def scatter_blocks(where, blocks, keep, give):
    p, c = where[1], where[2]
    for i in range(keep.shape[0]):
        copy, k = divmod(i, TP)
        chip = jnp.bitwise_xor(p, k)
        for out, core in ((keep, c), (give, 1 - c)):
            out[i] = blocks[((copy * 2 + lax.rem(chip, 2)) * 2 + core) * 2 + lax.div(chip, 2)]


def feed_weights_kernel(where, act, g, normed, g_up, keep, give, blocks):
    width = normed.shape[1]
    shard = keep.shape[1]
    for at, (a, b) in ((0, (normed, g_up)), (width, (act, g))):
        value = dot(a[...], b[...], TN)
        for d in range(blocks.shape[0]):
            blocks[d, :, at : at + width] = value[d * shard : (d + 1) * shard].astype(bf16)
    scatter_blocks(where, blocks, keep, give)


def mixed_weights(where, normed, g_qkv, heads, g_attn):
    p = where[1]
    value = dot(normed[...], g_qkv[...], TN)
    whole = dot(heads[...], g_attn[...], TN)
    mine = whole[:, :PW]
    for q in range(1, TP):
        mine = jnp.where(p == q, whole[:, q * PW : (q + 1) * PW], mine)
    return jnp.concatenate([value, mine], 1)


def mixed_weights_kernel(where, normed, g_qkv, heads, g_attn, keep, give, blocks):
    value = mixed_weights(where, normed, g_qkv, heads, g_attn)
    shard = blocks.shape[1]
    for d in range(blocks.shape[0]):
        blocks[d] = value[d * shard : (d + 1) * shard].astype(bf16)
    scatter_blocks(where, blocks, keep, give)


def last_weights_kernel(where, normed, g_qkv, heads, g_attn, *refs):
    sums, (keep, give, blocks, lines, more) = refs[: 6 * LAYERS], refs[6 * LAYERS :]
    p, c = where[1], where[2]
    devices, shard = blocks.shape[:2]
    per = PW // (2 * shard)
    lines[...] = jnp.zeros_like(lines)
    more[...] = jnp.zeros_like(more)
    for l in range(LAYERS):
        b_proj, b_out, norm1, norm2, qkv, fc = sums[6 * l : 6 * l + 6]
        base = SLOTS * l
        rows = (b_proj[0:1, :], b_out[0:1, :], norm1[0:1, :], norm1[1:2, :], norm2[0:1, :], norm2[1:2, :])
        for i, row in enumerate(rows):
            lines[base + i : base + i + 1, :] = row
        for q in range(TP):
            lines[base + 8 + q : base + 9 + q, :] = jnp.where(p == q, fc[0:1, :], 0.0)
        bias = jnp.broadcast_to(qkv[0:1, :], (128, D)).T
        for first, start in ((0, 0), (devices // 2, 2 * PW)):
            for j in range(2 * per):
                lane = base + 6 + j % 2
                more[first + p * per + j // 2, :, lane : lane + 1] = bias[
                    start + j * shard : start + (j + 1) * shard, 0:1
                ]
    columns = lines[...].T
    value = mixed_weights(where, normed, g_qkv, heads, g_attn)
    for d in range(devices):
        at = slice(d * shard, (d + 1) * shard)
        blocks[d] = jnp.concatenate([value[at], columns[at] + more[d]], 1).astype(bf16)
    for i in range(keep.shape[0]):
        rest, f = divmod(i, 2)
        keep[i] = blocks[(rest * 2 + c) * 2 + f]
        give[i] = blocks[(rest * 2 + 1 - c) * 2 + f]


def attend(q, keys_values, mask):
    k, v = keys_values[:, :PW], keys_values[:, PW:]
    q, k, v = (item.reshape(-1, PH, HD) for item in (q, k, v))
    scores = jnp.einsum("qhe,khe->hqk", q, k, preferred_element_type=f32) * 0.125
    scores = jnp.where(mask, scores, -1e30)
    top = jnp.max(scores, -1, keepdims=True)
    weights = jnp.exp(scores - top)
    total = jnp.sum(weights, -1, keepdims=True)
    out = jnp.einsum("hqk,khe->qhe", (weights / total).astype(bf16), v, preferred_element_type=f32)
    return out.reshape(-1, PW).astype(bf16), top + jnp.log(total)


def attend_back(q, keys_values, mask, log_total, grad_out):
    k, v = keys_values[:, :PW], keys_values[:, PW:]
    q, k, v, g = (item.reshape(-1, PH, HD) for item in (q, k, v, grad_out))
    scores = jnp.einsum("qhe,khe->hqk", q, k, preferred_element_type=f32) * 0.125
    probs = jnp.where(mask, jnp.exp(scores - log_total), 0.0)
    grad_probs = jnp.einsum("qhe,khe->hqk", g, v, preferred_element_type=f32)
    delta = jnp.sum(probs * grad_probs, -1, keepdims=True)
    grad_scores = (probs * (grad_probs - delta)).astype(bf16)
    dq = 0.125 * jnp.einsum("hqk,khe->qhe", grad_scores, k, preferred_element_type=f32)
    dk = 0.125 * jnp.einsum("hqk,qhe->khe", grad_scores, q, preferred_element_type=f32)
    dv = jnp.einsum("hqk,qhe->khe", probs.astype(bf16), g, preferred_element_type=f32)
    dkv = jnp.concatenate([dk.reshape(-1, PW), dv.reshape(-1, PW)], 1)
    return dq.reshape(-1, PW).astype(bf16), dkv


def body(tokens, w_qkv, b_qv, w_proj, b_proj, ln1_gain, ln1_bias, ln2_gain, ln2_bias, w_fc, b_fc, w_out, b_out, d_out):
    size = {name: lax.axis_size(name) for name in ALL}
    devices = math.prod(size.values())
    rows = tokens.shape[1]
    shard = w_qkv.shape[1]
    ff = w_fc.shape[2]
    h, g, x_at, c, f = (lax.axis_index(name) for name in ALL)
    p = 2 * f + x_at
    where = jnp.stack([h, p, c, g, f]).astype(jnp.int32)
    many = size["g"] > 1

    homes = [(a, b) for a in range(size["h"]) for b in range(size["f"])]
    outward = [
        [(a * 2 + b, (2 * b + (a // 2 + turn) % 2) * 2 + a % 2) for a, b in homes] for turn in range(2)
    ]

    def both_ways(value, low, moves):
        sent = [lax.dynamic_index_in_dim(value, i, 0, keepdims=False) for i in (low, 1 - low)]
        return [lax.ppermute(item, ("h", "f"), move) for item, move in zip(sent, moves)]

    def own_sequence(value):
        one, two = both_ways(value, h // 2, outward)
        return jnp.where(h % 2 == 0, jnp.stack([one, two]), jnp.stack([two, one])).reshape(-1, D)

    def back_to_blocks(value):
        moves = [[(b, a) for a, b in move] for move in outward]
        one, two = both_ways(value.reshape(2, rows, D), h % 2, moves)
        return jnp.where(h // 2 == 0, jnp.stack([one, two]), jnp.stack([two, one]))

    smalls = (b_proj, b_out, ln1_gain, ln1_bias, ln2_gain, ln2_bias, b_qv, b_fc)
    by_part = w_out.reshape(LAYERS, TP, shard, D)

    def plane(pieces):
        return jnp.stack([pieces[0]] + [chip_swap(pieces[k], k) for k in range(1, TP)])

    def layer_pieces(where, layer, qkv):
        extra = 0 if qkv is None else 3 * PW
        pieces = launch(
            layer_pieces_kernel(layer, qkv), f"layer_pieces_{layer}", [((shard, 3 * D + extra), bf16)] * TP,
            where, w_fc, by_part, w_proj, w_qkv,
            scratch=[pltpu.VMEM((TP, shard, D + 3 * PW), bf16)],
        )
        return lax.all_gather(plane(pieces), COPIES, axis=0, tiled=True)

    def arrange(own, *widths):
        return [
            item.reshape(D, -1)
            for item in launch(
                arrange_kernel(widths), "arrange", [((devices, shard, width), bf16) for width in widths],
                where, own, swap(own, "c"),
            )
        ]

    feed = layer_pieces(where, 0, None)
    x_own, later = lax.optimization_barrier((own_sequence(tokens), where))
    first = plane(launch(
        first_pieces_kernel, "first_pieces", [((shard, 3 * PW + HD), bf16)] * TP, later, w_qkv, *smalls,
        scratch=[pltpu.VMEM((128, 128), f32), pltpu.VMEM((TP, shard, 3 * PW + HD), bf16)],
    ))
    first, x_pieces = lax.optimization_barrier((first, share(x_own)))
    first = lax.all_gather(first, COPIES, axis=0, tiled=True)
    first = jnp.concatenate([first, swap(first, "c")], 0)
    wq, table = launch(
        arrange_first_kernel(size), "arrange_first",
        [((devices, shard, 3 * PW), bf16), ((LAYERS * 8, D), f32)], where, first,
        scratch=[pltpu.VMEM((D, 128), f32), pltpu.VMEM((devices, shard, HD), f32)],
    )
    wq = [wq.reshape(D, 3 * PW), None]
    wf, wo, wp = [None] * LAYERS, [None] * LAYERS, [None] * LAYERS
    count = TP * x_pieces[0].shape[0]
    own = count // TP
    if many:
        second = jnp.arange(2)[None, :, None]
        inside = jnp.arange(rows)[None, None, :]
        chip = p ^ jnp.arange(TP)[:, None, None]

        def positions(group, core):
            place = (chip // 2 + 2 * second) * size["g"] + group
            return (((place * 2 + chip % 2) * 2 + core) * rows + inside).reshape(-1)

        q_pos = positions(g, c)
        k_pos = jnp.concatenate([positions(gi, core) for gi in range(size["g"]) for core in (0, 1)])
        mask = (k_pos[None, :] <= q_pos[:, None])[None]

    def all_keys(kv, other):
        both = jnp.where(c == 0, jnp.stack([kv, other]), jnp.stack([other, kv])).reshape(-1, kv.shape[1])
        return lax.all_gather(both, "g", axis=0, tiled=True)

    saved = []
    state = tuple(x_pieces)
    for l in range(LAYERS):
        x, x_own, normed, q, kv = launch(
            enter_kernel(l == 0, l), f"enter_{l}",
            [((count, D), f32), ((own, D), f32), ((count, D), bf16), ((count, PW), bf16), ((count, 2 * PW), bf16)],
            where, table, wq[l], *state, flops=2 * count * D * 3 * PW,
        )
        other = swap(kv, "c")
        if l + 1 == LAYERS:
            g_low, x_own = lax.optimization_barrier((own_sequence(d_out), x_own))
            pieces = share(g_low)
        if l == 0:
            feed, other, later = lax.optimization_barrier((feed, other, where))
        wf[l], wo[l], wp[l] = arrange(feed, D, D, D) if l == 0 else after
        if l == 0:
            feed = layer_pieces(later, 1, 1)
        if many:
            keys = all_keys(kv, other)
            out, lse = attend(q, keys, mask)
        else:
            keys = None
            out, lse = launch(
                attend_kernel, f"attend_{l}", [((count, PW), bf16), ((count, PH), f32)], where, q, kv, other,
                scratch=[pltpu.VMEM((count, PW), bf16), pltpu.VMEM((count, 2 * PW), bf16),
                         pltpu.VMEM((count, 2 * PW), bf16), pltpu.VMEM((count, PW), bf16)],
                flops=4 * count * 2 * count * PW,
            )
        if l + 1 == LAYERS:
            out, pieces = lax.optimization_barrier((out, pieces))
        outs = [out] + [chip_swap(out, k) for k in range(1, TP)]
        mid, mid_own, heads, normed2, up, act, y0, y1, y2, y3 = launch(
            middle_kernel(l), f"middle_{l}",
            [((count, D), f32), ((own, D), f32), ((count, D), bf16), ((count, D), bf16), ((count, D), f32), ((count, D), bf16)]
            + [((own, D), f32)] + [((own, D), bf16)] * 3,
            where, table, x, *outs, wp[l], wf[l], wo[l],
            scratch=[pltpu.VMEM((TP, count, PW), bf16)], flops=6 * count * D * D,
        )
        total = y0
        for k, y in ((1, y1), (2, y2), (3, y3)):
            total = total + chip_swap(y, k).astype(f32)
        saved.append((x, x_own, normed, q, kv, other, keys, lse, heads, mid, mid_own, normed2, up, act))
        if l + 1 < LAYERS:
            state = (mid, *share(total.astype(bf16)))
            feed, state = lax.optimization_barrier((feed, state))
            *after, wq[l + 1] = arrange(feed, D, D, D, 3 * PW)
        else:
            tokens_out = mid_own + total + table[8 * l + 1 : 8 * l + 2]
    output = back_to_blocks(tokens_out.astype(bf16))

    copies = devices // (2 * TP)
    halves = [((copies * TP, shard, 2 * D), bf16)] * 2

    def reduce_copies(keep, give):
        total = (keep.astype(f32) + swap(give, "c").astype(f32)).astype(bf16)
        return lax.psum_scatter(total, COPIES, scatter_dimension=0, tiled=True)

    def by_owner(sums):
        return [sums[0]] + [chip_swap(sums[k], k) for k in range(1, TP)]

    line = ((8, D), f32)
    parts = [((own, D), f32)] + [((own, D), bf16)] * 3
    g_own = g_low
    b_out_sum = jnp.broadcast_to(jnp.sum(g_low.astype(f32), 0, keepdims=True), (8, D))
    sums = [None] * LAYERS
    feed_grads = [None] * LAYERS
    for l in reversed(range(LAYERS)):
        x, x_own, normed, q, kv, other, keys, lse, heads, mid, mid_own, normed2, up, act = saved[l]
        if l + 1 < LAYERS:
            pieces = share(g_low)
        g_all, g_up, b_fc_sum, norm2_sum, y0, y1, y2, y3 = launch(
            feed_back_kernel, f"feed_back_{l}", [((count, D), bf16), ((count, D), bf16), line, line] + parts,
            where, *pieces, up, mid, wo[l], wf[l], flops=4 * count * D * D,
        )
        got = [chip_swap(y, k) for k, y in ((1, y1), (2, y2), (3, y3))]
        keep, give = launch(
            feed_weights_kernel, f"feed_weights_{l}", halves, where, act, g_all, normed2, g_up,
            scratch=[pltpu.VMEM((devices, shard, 2 * D), bf16)], flops=4 * count * D * D,
        )
        if l + 1 == LAYERS:
            got, keep, give, output = lax.optimization_barrier((got, keep, give, output))
        else:
            got, keep, give, mixed = lax.optimization_barrier((got, keep, give, mixed))
        feed = reduce_copies(keep, give)
        g_own, g_low, b_proj_sum = launch(
            norm_back_kernel(l, 4), f"norm2_back_{l}", [((own, D), f32), ((own, D), bf16), line],
            where, table, g_own, mid_own, y0, *got,
        )
        pieces = share(g_low)
        if many:
            g_attn = jnp.concatenate(pieces, 0)
            mine = lax.dynamic_slice_in_dim(wp[l], p * PW, PW, 0)
            dq, dkv = attend_back(q, keys, mask, lse, dot(g_attn, mine, NT).astype(bf16))
            dkv = lax.psum_scatter(dkv, "g", scatter_dimension=0, tiled=True).reshape(2, count, 2 * PW)
            dkv, give = (lax.dynamic_index_in_dim(dkv, i, 0, keepdims=False) for i in (c, 1 - c))
            give = give.astype(bf16)
        else:
            g_attn, dq, dkv, give = launch(
                attend_back_kernel, f"attend_back_{l}",
                [((count, D), bf16), ((count, PW), bf16), ((count, 2 * PW), f32), ((count, 2 * PW), bf16)],
                where, *pieces, wp[l], q, kv, other, lse,
                scratch=[pltpu.VMEM((count, PW), f32), pltpu.VMEM((count, PW), bf16), pltpu.VMEM((count, PW), bf16),
                         pltpu.VMEM((count, 2 * PW), bf16), pltpu.VMEM((count, 2 * PW), bf16),
                         pltpu.VMEM((count, PW), f32), pltpu.VMEM((count, 2 * PW), f32), pltpu.VMEM((count, 2 * PW), f32)],
                flops=10 * count * 2 * count * PW,
            )
        more = swap(give, "c")
        if l == 0:
            more, feed = lax.optimization_barrier((more, feed))
        g_qkv, b_qkv_sum, norm1_sum, y0, y1, y2, y3 = launch(
            leave_kernel, f"leave_{l}", [((count, 3 * PW), bf16), line, line] + parts,
            where, dq, dkv, more, wq[l], x, flops=2 * count * D * 3 * PW,
        )
        got = [chip_swap(y, k) for k, y in ((1, y1), (2, y2), (3, y3))]
        sums[l] = (b_proj_sum, b_out_sum, norm1_sum, norm2_sum, b_qkv_sum, b_fc_sum)
        if l > 0:
            keep, give = launch(
                mixed_weights_kernel, f"mixed_weights_{l}", [((copies * TP, shard, D), bf16)] * 2,
                where, normed, g_qkv, heads, g_attn,
                scratch=[pltpu.VMEM((devices, shard, D), bf16)], flops=4 * count * D * D,
            )
            got, keep, give, feed = lax.optimization_barrier((got, keep, give, feed))
            mixed = reduce_copies(keep, give)
        else:
            keep, give = launch(
                last_weights_kernel, "last_weights", [((copies * TP, shard, D + 128), bf16)] * 2,
                where, normed, g_qkv, heads, g_attn, *[item for per_layer in sums for item in per_layer],
                scratch=[pltpu.VMEM((devices, shard, D + 128), bf16), pltpu.VMEM((128, D), f32),
                         pltpu.VMEM((devices, shard, 128), f32)],
                flops=4 * count * D * D,
            )
            last = (keep.astype(f32) + swap(give, "c").astype(f32)).astype(bf16)
            got, last = lax.optimization_barrier((got, last))
            last = lax.all_to_all(last, ("h", "g", "x", "f"), 0, 0, tiled=True)
        feed_grads[l] = feed
        g_own, g_low, b_out_sum = launch(
            norm_back_kernel(l, 2), f"norm1_back_{l}", [((own, D), f32), ((own, D), bf16), line],
            where, table, g_own, x_own, y0, *got,
        )
    grad_tokens = back_to_blocks(g_own)
    d_wf, d_wo = launch(
        finish_feed_kernel, "finish_feed", [((LAYERS, shard, ff), f32), ((LAYERS, TP, shard, D), f32)],
        where, *[item for l in range(LAYERS) for item in by_owner(feed_grads[l])],
        scratch=[pltpu.VMEM((TP, shard, 2 * D), bf16)],
    )
    d_wo = d_wo.reshape(w_out.shape)
    d_wq, d_wp, d_b_proj, d_b_out, d_g1, d_s1, d_g2, d_s2, d_b_qv, d_b_fc = launch(
        finish_mixed_kernel, "finish_mixed",
        [((LAYERS, shard, 3 * D), f32), ((LAYERS, shard, D), f32)] + [(item.shape, f32) for item in smalls],
        where, last, *by_owner(mixed), scratch=[pltpu.VMEM((LAYERS, TP, shard, D), f32), pltpu.VMEM((128, 128), f32)],
    )
    return (output, grad_tokens, d_wq, d_b_qv, d_wp, d_b_proj, d_g1, d_s1, d_g2, d_s2, d_wf, d_b_fc, d_wo, d_b_out)


def solution(mesh):
    ctx, pair = mesh.shape["ctx"], mesh.shape["fsdp"]
    view = Mesh(mesh.devices.reshape(4, ctx // 16, 2, 2, pair), ALL)
    along = ("h", "g", "x", "c")
    token = P("f", along, None)
    matrix = P(None, ALL, None)
    line = P(None, ALL)
    in_specs = (token, matrix, line, matrix, line, line, line, line, line, matrix, line, matrix, line, token)
    out_specs = (token, token, matrix, line, matrix, line, line, line, line, line, matrix, line, matrix, line)
    return jax.shard_map(body, mesh=view, in_specs=in_specs, out_specs=out_specs, check_vma=False)
```

```python
import functools
import math

import jax
import jax.numpy as jnp
from jax import lax
from jax.experimental import pallas as pl
from jax.experimental.pallas import tpu as pltpu
from jax.sharding import Mesh, PartitionSpec as P

D = 768
H = 12
HD = 64
LAYERS = 2
TP = 4
PH = H // TP
PW = PH * HD
EPS = 1e-05
ROOT = math.sqrt(2.0 / math.pi)
bf16 = jnp.bfloat16
f32 = jnp.float32

ALL = ("h", "g", "x", "c", "f")
COPIES = ("h", "g")
SLOTS = 12


def dot(a, b, dims=((1,), (0,)), precision=None):
    return lax.dot_general(a, b, (dims, ((), ())), preferred_element_type=f32, precision=precision)


NT = ((1,), (1,))
TN = ((0,), (0,))


def swap(value, axis, mask=1):
    names = (axis,) if isinstance(axis, str) else axis
    size = math.prod(lax.axis_size(name) for name in names)
    return lax.ppermute(value, axis, [(i, i ^ mask) for i in range(size)])


def chip_swap(value, mask):
    return swap(value, ("x", "f"), mask % 2 * 2 + mask // 2)


def after(value, event):
    return lax.optimization_barrier((value, event))[0]


def share(own):
    return [own] + [chip_swap(own, k) for k in range(1, TP)]


def launch(kernel, name, outs, scalars, *args, scratch=(), flops=0):
    shapes = [jax.ShapeDtypeStruct(shape, kind) for shape, kind in outs]
    moved = sum(a.size * a.dtype.itemsize for a in args) + sum(math.prod(o.shape) * o.dtype.itemsize for o in shapes)
    return pl.pallas_call(
        kernel,
        name=name,
        out_shape=shapes,
        in_specs=[pl.BlockSpec(memory_space=pltpu.SMEM)] + [pl.BlockSpec(memory_space=pltpu.VMEM)] * len(args),
        out_specs=[pl.BlockSpec(memory_space=pltpu.VMEM)] * len(shapes),
        scratch_shapes=list(scratch),
        cost_estimate=pl.CostEstimate(flops=flops, bytes_accessed=moved, transcendentals=0),
        compiler_params=pltpu.CompilerParams(vmem_limit_bytes=56 * 1024 * 1024),
    )(scalars, *args)


def unit_rows(values):
    center = values - jnp.mean(values, -1, keepdims=True)
    scale = lax.rsqrt(jnp.mean(center * center, -1, keepdims=True) + EPS)
    return center * scale, scale


def interleave(shard):
    block = D // 2
    per = block // (TP * shard)
    row = lax.broadcasted_iota(jnp.int32, (block, block), 0)
    col = lax.broadcasted_iota(jnp.int32, (block, block), 1)
    chip, rest = lax.div(row, per * shard), lax.rem(row, per * shard)
    target = lax.div(rest, shard) * (TP * shard) + chip * shard + lax.rem(rest, shard)
    return (col == target).astype(bf16)


def first_pieces_kernel(where, w_qkv, *refs):
    small, outs, (lines, cols) = refs[:8], refs[8 : 8 + TP], refs[8 + TP :]
    p = where[1]
    shard = cols.shape[1]
    lines[...] = jnp.zeros_like(lines)
    at = 0
    for l in range(LAYERS):
        for item in small:
            for first in range(0, item.shape[1], shard):
                lines[at : at + 1, :shard] = item[l : l + 1, first : first + shard].astype(f32)
                at += 1
    columns = lines[...].T[:shard, :HD]
    for q in range(TP):
        parts = [w_qkv[0, :, j * D + q * PW : j * D + (q + 1) * PW].astype(f32) for j in range(3)]
        cols[q] = jnp.concatenate(parts + [columns], 1).astype(bf16)
    for k, out in enumerate(outs):
        out[...] = cols[jnp.bitwise_xor(p, k)]


def layer_pieces_kernel(layer):
    def kernel(where, w_fc, w_out, w_proj, w_qkv, *refs):
        outs, (cols,) = refs[:TP], refs[TP:]
        p = where[1]
        shard = w_proj.shape[1]
        block = D // 2
        order = interleave(shard)
        fc = [dot(w_fc[layer, :, b * block : (b + 1) * block], order, NT) for b in range(w_fc.shape[2] // block)]
        for q in range(TP):
            lanes = slice(q * block // TP, (q + 1) * block // TP)
            cols[q, :, :D] = jnp.concatenate([item[:, lanes] for item in fc], 1).astype(bf16)
            if layer:
                parts = [w_qkv[layer, :, j * D + q * PW : j * D + (q + 1) * PW] for j in range(3)]
                cols[q, :, D:] = jnp.concatenate(parts + [jnp.zeros((shard, HD), bf16)], 1)
        for k, out in enumerate(outs):
            q = jnp.bitwise_xor(p, k)
            out[:, :D] = cols[q, :, :D]
            out[:, D : 2 * D] = w_out[layer, q]
            out[:, 2 * D : 3 * D] = w_proj[layer]
            if layer:
                out[:, 3 * D :] = cols[q, :, D:]

    return kernel


def arrange_first_kernel(sizes):
    def kernel(where, got, w_first, table, columns, blocks):
        h, p, c = where[0], where[1], where[2]
        devices, shard = w_first.shape[:2]
        groups = sizes["g"]
        columns[...] = jnp.zeros_like(columns)
        for d in range(devices):
            rest, fi = divmod(d, 2)
            rest, ci = divmod(rest, 2)
            rest, xi = divmod(rest, 2)
            hi, gi = divmod(rest, groups)
            copy = (jnp.bitwise_xor(c, ci) * sizes["h"] + jnp.bitwise_xor(h, hi)) * groups + gi
            one = got[copy * TP + jnp.bitwise_xor(p, 2 * fi + xi)].astype(f32)
            w_first[d] = one[:, : 3 * PW].astype(bf16)
            columns[d * shard : (d + 1) * shard, :HD] = one[:, 3 * PW :]
            blocks[d] = one[:, 3 * PW :]
        lines = columns[...].T
        per = PW // (2 * shard)
        for l in range(LAYERS):
            base = SLOTS * l
            table[8 * l : 8 * l + 6, :] = lines[base : base + 6]
            parts = []
            for first in (0, devices // 2):
                for j in range(per):
                    block = blocks[first + p * per + j]
                    parts += [block[:, base + 6 : base + 7], block[:, base + 7 : base + 8]]
                if first == 0:
                    parts.append(jnp.zeros((PW, 1), f32))
            parts.append(jnp.zeros((D - 3 * PW, 1), f32))
            bias = jnp.broadcast_to(jnp.concatenate(parts, 0), (D, 128)).T
            table[8 * l + 6 : 8 * l + 7, :] = bias[0:1]
            row = lines[base + 8 : base + 9]
            for q in range(1, TP):
                row = jnp.where(p == q, lines[base + 8 + q : base + 9 + q], row)
            table[8 * l + 7 : 8 * l + 8, :] = row

    return kernel


def finish_feed_kernel(where, *refs):
    pieces, (wf_out, wo_out, cols) = refs[:TP], refs[TP:]
    p = where[1]
    shard = wf_out.shape[1]
    block = D // 2
    order = interleave(shard)
    for l in range(LAYERS):
        for k in range(TP):
            cols[jnp.bitwise_xor(p, k)] = pieces[k][:, 2 * D * l : 2 * D * (l + 1)]
        fc = [cols[q, :, :D].astype(f32) for q in range(TP)]
        for b in range(wf_out.shape[2] // block):
            lanes = slice(b * block // TP, (b + 1) * block // TP)
            joined = jnp.concatenate([item[:, lanes] for item in fc], 1).astype(bf16)
            wf_out[l, :, b * block : (b + 1) * block] = dot(joined, order)
        for q in range(TP):
            wo_out[l, q] = cols[q, :, D:].astype(f32)


def finish_mixed_kernel(where, last, m0, m1, m2, m3, wq_out, wp_out, *refs):
    small_outs, (cols, square) = refs[:8], refs[8:]
    p = where[1]
    shard = wq_out.shape[1]
    columns = jnp.zeros((shard, 128), f32)
    for q in range(TP):
        total = jnp.zeros((shard, D + 128), f32)
        for copy in range(last.shape[0] // TP):
            total = total + last[(copy * 2 + q % 2) * 2 + q // 2].astype(f32)
        columns = columns + total[:, D:]
        cols[0, q] = total[:, :D]
    for k, m in enumerate((m0, m1, m2, m3)):
        cols[1, jnp.bitwise_xor(p, k)] = m[:, 2 * D * LAYERS :].astype(f32)
    for l in range(LAYERS):
        for j in range(3):
            wq_out[l, :, j * D : (j + 1) * D] = jnp.concatenate(
                [cols[l, q, :, j * PW : (j + 1) * PW] for q in range(TP)], 1
            )
        wp_out[l] = jnp.concatenate([cols[l, q, :, 3 * PW :] for q in range(TP)], 1)
    square[...] = jnp.zeros_like(square)
    square[:shard, :] = columns
    lines = square[...].T
    at = 0
    for l in range(LAYERS):
        for out in small_outs:
            for first in range(0, out.shape[1], shard):
                out[l : l + 1, first : first + shard] = lines[at : at + 1, :shard]
                at += 1


def enter_kernel(first, index):
    def kernel(where, table, wq, *refs):
        *inputs, x_out, xo_out, n_out, q_out, kv_out = refs
        if not first:
            mid, *inputs = inputs
        t = table
        gain, shift, bias = (t[8 * index + i : 8 * index + i + 1, :] for i in (2, 3, 6))
        rows = n_out.shape[0] // TP
        for k in range(TP):
            at = slice(k * rows, (k + 1) * rows)
            x = inputs[k][...].astype(f32)
            if not first:
                x = mid[at, :] + x + t[8 * (index - 1) + 1 : 8 * (index - 1) + 2, :]
            x_out[at, :] = x
            if k == 0:
                xo_out[...] = x
            unit, _ = unit_rows(x)
            n_out[at, :] = (unit * gain + shift).astype(bf16)
        got = (dot(n_out[...], wq[...]) + bias[:, : 3 * PW]).astype(bf16)
        q_out[...] = got[:, :PW]
        kv_out[...] = got[:, PW:]

    return kernel


def tile_rows(p, t, size):
    return pl.multiple_of((jnp.bitwise_xor(t % TP, p) * 2 + t // TP) * size, size)


def masks(c, chunk, size):
    a = lax.broadcasted_iota(jnp.int32, (chunk, chunk), 0)
    b = lax.broadcasted_iota(jnp.int32, (chunk, chunk), 1)
    return b <= a, lax.div(b, size) < lax.div(a, size) + c


def attend_kernel(where, q_ref, own_ref, oth_ref, out_ref, lse_ref, qn, kn, on, outn):
    p, c = where[1], where[2]
    count = q_ref.shape[0]
    size = count // (2 * TP)
    chunk = 2 * size
    for t in range(2 * TP):
        at = pl.ds(tile_rows(p, t, size), size)
        here = slice(t * size, (t + 1) * size)
        qn[here, :] = q_ref[at, :]
        kn[here, :] = own_ref[at, :]
        on[here, :] = oth_ref[at, :]
    ok_own, ok_oth = masks(c, chunk, size)
    for j in range(count // chunk):
        rows = slice(j * chunk, (j + 1) * chunk)
        outs = []
        for h in range(PH):
            lanes = slice(h * HD, (h + 1) * HD)
            vlanes = slice(PW + h * HD, PW + (h + 1) * HD)
            q = qn[rows, lanes]
            scores = []
            for keys, ok in ((kn, ok_own), (on, ok_oth)):
                if j > 0:
                    scores.append(dot(q, keys[: j * chunk, lanes], NT) * 0.125)
                scores.append(jnp.where(ok, dot(q, keys[rows, lanes], NT) * 0.125, -1e30))
            top = functools.reduce(jnp.maximum, [jnp.max(v, -1, keepdims=True) for v in scores])
            weights = [jnp.exp(v - top) for v in scores]
            total = sum(jnp.sum(v, -1, keepdims=True) for v in weights)
            low = [v.astype(bf16) for v in weights]
            out = jnp.zeros((chunk, HD), f32)
            for i, keys in enumerate((kn, on)):
                if j > 0:
                    out = out + dot(low[2 * i], keys[: j * chunk, vlanes])
                    out = out + dot(low[2 * i + 1], keys[rows, vlanes])
                else:
                    out = out + dot(low[i], keys[rows, vlanes])
            outs.append(out / total)
            lse_ref[rows, h : h + 1] = top + jnp.log(total)
        outn[rows, :] = jnp.concatenate(outs, 1).astype(bf16)
    for t in range(2 * TP):
        out_ref[pl.ds(tile_rows(p, t, size), size), :] = outn[t * size : (t + 1) * size, :]


def middle_kernel(index):
    def kernel(where, table, x, o0, o1, o2, o3, wp, wf, wo, mid_out, mo_out, heads_out, n_out, up_out, act_out, y0, y1, y2, y3, got):
        p = where[1]
        t = table
        b_proj, gain, shift, b_up = (t[8 * index + i : 8 * index + i + 1, :] for i in (0, 4, 5, 7))
        rows = x.shape[0] // TP
        for k, o in enumerate((o0, o1, o2, o3)):
            for m in range(TP):
                got[k, m * rows : (m + 1) * rows, :] = o[(m ^ k) * rows : ((m ^ k) + 1) * rows, :]
        heads_out[...] = jnp.concatenate([got[jnp.bitwise_xor(p, q)] for q in range(TP)], 1)
        for m, y in enumerate((y0, y1, y2, y3)):
            at = slice(m * rows, (m + 1) * rows)
            mid = x[at, :] + dot(heads_out[at, :], wp[...]) + b_proj
            mid_out[at, :] = mid
            if m == 0:
                mo_out[...] = mid
            unit, _ = unit_rows(mid)
            n_out[at, :] = (unit * gain + shift).astype(bf16)
        up = dot(n_out[...], wf[...]) + b_up
        up_out[...] = up
        act_out[...] = (0.5 * up * (1.0 + jnp.tanh(ROOT * (up + 0.044715 * up * up * up)))).astype(bf16)
        for m, y in enumerate((y0, y1, y2, y3)):
            at = slice(m * rows, (m + 1) * rows)
            y[...] = dot(act_out[at, :], wo[...]).astype(y.dtype)

    return kernel


def part_sums(part, unit, acc):
    acc[0:1, :] += jnp.sum(part * unit, 0, keepdims=True)
    acc[1:2, :] += jnp.sum(part, 0, keepdims=True)


def feed_back_kernel(where, g0, g1, g2, g3, up, mid, wo, wf, g_out, gu_out, bfc_out, sums_out, y0, y1, y2, y3):
    rows = g0.shape[0]
    for k, g in enumerate((g0, g1, g2, g3)):
        g_out[k * rows : (k + 1) * rows, :] = g[...]
    bfc_out[...] = jnp.zeros_like(bfc_out)
    sums_out[...] = jnp.zeros_like(sums_out)
    sums_out[2:3, :] = jnp.sum(g0[...].astype(f32), 0, keepdims=True)
    for k, y in enumerate((y0, y1, y2, y3)):
        at = slice(k * rows, (k + 1) * rows)
        g_act = dot(g_out[at, :], wo[...], NT)
        u = up[at, :]
        t = jnp.tanh(ROOT * (u + 0.044715 * u * u * u))
        slope = 0.5 * (1.0 + t) + 0.5 * u * (1.0 - t * t) * (ROOT * (1.0 + 3 * 0.044715 * u * u))
        g_up = (slope * g_act).astype(bf16)
        gu_out[at, :] = g_up
        bfc_out[0:1, :] += jnp.sum(g_up.astype(f32), 0, keepdims=True)
        part = dot(g_up, wf[...], NT)
        y[...] = part.astype(y.dtype)
        unit, _ = unit_rows(mid[at, :])
        part_sums(part, unit, sums_out)


def norm_back_kernel(index, which):
    def kernel(where, table, grad, value, r0, r1, r2, r3, g_out, low_out, sum_out):
        gain = table[8 * index + which : 8 * index + which + 1, :]
        cot = r0[...] + r1[...].astype(f32) + r2[...].astype(f32) + r3[...].astype(f32)
        unit, scale = unit_rows(value[...])
        inner = cot * gain
        moved = scale * (
            inner - jnp.mean(inner, -1, keepdims=True) - unit * jnp.mean(inner * unit, -1, keepdims=True)
        )
        total = grad[...].astype(f32) + moved
        g_out[...] = total
        low = total.astype(bf16)
        low_out[...] = low
        sum_out[...] = jnp.zeros_like(sum_out)
        sum_out[0:1, :] = jnp.sum(low.astype(f32), 0, keepdims=True)

    return kernel


def attend_back_kernel(where, g0, g1, g2, g3, wp, q_ref, own_ref, oth_ref, lse_ref, ga_out, dq_ref, down_ref, doth_ref, local, gn, qn, kn, on, dqn, dkn, don):
    p, c = where[1], where[2]
    count = q_ref.shape[0]
    size = count // (2 * TP)
    chunk = 2 * size
    rows_of = g0.shape[0]
    for k, g in enumerate((g0, g1, g2, g3)):
        ga_out[k * rows_of : (k + 1) * rows_of, :] = g[...]
    mine = wp[pl.ds(pl.multiple_of(p * PW, PW), PW), :]
    local[...] = dot(ga_out[...], mine, NT)
    for t in range(2 * TP):
        at = pl.ds(tile_rows(p, t, size), size)
        here = slice(t * size, (t + 1) * size)
        gn[here, :] = local[at, :].astype(bf16)
        qn[here, :] = q_ref[at, :]
        kn[here, :] = own_ref[at, :]
        on[here, :] = oth_ref[at, :]
    dkn[...] = jnp.zeros_like(dkn)
    don[...] = jnp.zeros_like(don)
    ok_own, ok_oth = masks(c, chunk, size)
    for j in range(count // chunk):
        rows = slice(j * chunk, (j + 1) * chunk)
        dqs = []
        for h in range(PH):
            lanes = slice(h * HD, (h + 1) * HD)
            vlanes = slice(PW + h * HD, PW + (h + 1) * HD)
            q, g = qn[rows, lanes], gn[rows, lanes]
            lse = lse_ref[rows, h : h + 1]
            work = []
            for keys, sums, ok in ((kn, dkn, ok_own), (on, don, ok_oth)):
                if j > 0:
                    work.append((keys, sums, slice(0, j * chunk), None))
                work.append((keys, sums, rows, ok))
            probs, grads = [], []
            delta = jnp.zeros((chunk, 1), f32)
            for keys, sums, span, ok in work:
                scores = dot(q, keys[span, lanes], NT) * 0.125 - lse
                if ok is not None:
                    scores = jnp.where(ok, scores, -1e30)
                prob = jnp.exp(scores)
                grad = dot(g, keys[span, vlanes], NT)
                delta = delta + jnp.sum(prob * grad, -1, keepdims=True)
                probs.append(prob)
                grads.append(grad)
            dq = jnp.zeros((chunk, HD), f32)
            for (keys, sums, span, ok), prob, grad in zip(work, probs, grads):
                ds = (prob * (grad - delta)).astype(bf16)
                dq = dq + dot(ds, keys[span, lanes])
                sums[span, lanes] += 0.125 * dot(ds, q, TN)
                sums[span, vlanes] += dot(prob.astype(bf16), g, TN)
            dqs.append(0.125 * dq)
        dqn[rows, :] = jnp.concatenate(dqs, 1)
    for t in range(2 * TP):
        at = pl.ds(tile_rows(p, t, size), size)
        here = slice(t * size, (t + 1) * size)
        dq_ref[at, :] = dqn[here, :].astype(bf16)
        down_ref[at, :] = dkn[here, :]
        doth_ref[at, :] = don[here, :].astype(bf16)


def leave_kernel(where, dq, dkv, more, wq, x, gq_out, bq_out, sums_out, y0, y1, y2, y3):
    gq_out[:, :PW] = dq[...]
    gq_out[:, PW:] = (dkv[...] + more[...].astype(f32)).astype(bf16)
    bq_out[...] = jnp.zeros_like(bq_out)
    bq_out[0:1, : 3 * PW] = jnp.sum(gq_out[...].astype(f32), 0, keepdims=True)
    sums_out[...] = jnp.zeros_like(sums_out)
    rows = x.shape[0] // TP
    for k, y in enumerate((y0, y1, y2, y3)):
        at = slice(k * rows, (k + 1) * rows)
        part = dot(gq_out[at, :], wq[...], NT)
        y[...] = part.astype(y.dtype)
        unit, _ = unit_rows(x[at, :])
        part_sums(part, unit, sums_out)


def arrange_kernel(widths):
    def kernel(where, own, oth, *outs):
        p, c = where[1], where[2]
        devices = outs[0].shape[0]

        def one(d, carry):
            core = lax.rem(lax.div(d, 2), 2)
            chip = lax.rem(d, 2) * 2 + lax.rem(lax.div(d, 4), 2)
            block = lax.div(d, 8) * TP + jnp.bitwise_xor(chip, p)
            for source, here in ((own, core == c), (oth, core != c)):

                @pl.when(here)
                def _():
                    at = 0
                    for out, width in zip(outs, widths):
                        out[d] = source[block, :, at : at + width]
                        at += width

            return carry

        lax.fori_loop(0, devices, one, 0)

    return kernel


def scatter_blocks(where, blocks, keep, give):
    p, c = where[1], where[2]
    for i in range(keep.shape[0]):
        copy, k = divmod(i, TP)
        chip = jnp.bitwise_xor(p, k)
        for out, core in ((keep, c), (give, 1 - c)):
            out[i] = blocks[((copy * 2 + lax.rem(chip, 2)) * 2 + core) * 2 + lax.div(chip, 2)]


def feed_weights_kernel(where, act, g, normed, g_up, keep, give, blocks):
    width = normed.shape[1]
    shard = keep.shape[1]
    for at, (a, b) in ((0, (normed, g_up)), (width, (act, g))):
        value = dot(a[...], b[...], TN)
        for d in range(blocks.shape[0]):
            blocks[d, :, at : at + width] = value[d * shard : (d + 1) * shard].astype(bf16)
    scatter_blocks(where, blocks, keep, give)


def mixed_weights(where, normed, g_qkv, heads, g_attn):
    p = where[1]
    value = dot(normed[...], g_qkv[...], TN)
    whole = dot(heads[...], g_attn[...], TN)
    mine = whole[:, :PW]
    for q in range(1, TP):
        mine = jnp.where(p == q, whole[:, q * PW : (q + 1) * PW], mine)
    return jnp.concatenate([value, mine], 1)


def mixed_weights_kernel(where, normed, g_qkv, heads, g_attn, keep, give, blocks):
    value = mixed_weights(where, normed, g_qkv, heads, g_attn)
    shard = blocks.shape[1]
    for d in range(blocks.shape[0]):
        blocks[d] = value[d * shard : (d + 1) * shard].astype(bf16)
    scatter_blocks(where, blocks, keep, give)


def leave_last_kernel(where, dq, dkv, more_keys, wq, x, normed, heads, g_attn, *refs):
    sums, refs = refs[: 5 * LAYERS - 2], refs[5 * LAYERS - 2 :]
    keep, give, y0, y1, y2, y3, blocks, lines, more, g_qkv, b_qkv, norm1_first = refs
    leave_kernel(where, dq, dkv, more_keys, wq, x, g_qkv, b_qkv, norm1_first, y0, y1, y2, y3)
    p, c = where[1], where[2]
    devices, shard = blocks.shape[:2]
    per = PW // (2 * shard)
    lines[...] = jnp.zeros_like(lines)
    more[...] = jnp.zeros_like(more)
    for l in range(LAYERS):
        b_proj, norm2, fc, norm1, qkv = (tuple(sums[:3]) + (norm1_first, b_qkv)) if l == 0 else sums[3:]
        base = SLOTS * l
        rows = (b_proj[0:1, :], norm2[2:3, :], norm1[0:1, :], norm1[1:2, :], norm2[0:1, :], norm2[1:2, :])
        for i, row in enumerate(rows):
            lines[base + i : base + i + 1, :] = row
        for q in range(TP):
            lines[base + 8 + q : base + 9 + q, :] = jnp.where(p == q, fc[0:1, :], 0.0)
        bias = jnp.broadcast_to(qkv[0:1, :], (128, D)).T
        for first, start in ((0, 0), (devices // 2, 2 * PW)):
            for j in range(2 * per):
                lane = base + 6 + j % 2
                more[first + p * per + j // 2, :, lane : lane + 1] = bias[
                    start + j * shard : start + (j + 1) * shard, 0:1
                ]
    columns = lines[...].T
    value = mixed_weights(where, normed, g_qkv, heads, g_attn)
    for d in range(devices):
        at = slice(d * shard, (d + 1) * shard)
        blocks[d] = jnp.concatenate([value[at], columns[at] + more[d]], 1).astype(bf16)
    for i in range(keep.shape[0]):
        rest, f = divmod(i, 2)
        keep[i] = blocks[(rest * 2 + c) * 2 + f]
        give[i] = blocks[(rest * 2 + 1 - c) * 2 + f]


def attend(q, keys_values, mask):
    k, v = keys_values[:, :PW], keys_values[:, PW:]
    q, k, v = (item.reshape(-1, PH, HD) for item in (q, k, v))
    scores = jnp.einsum("qhe,khe->hqk", q, k, preferred_element_type=f32) * 0.125
    scores = jnp.where(mask, scores, -1e30)
    top = jnp.max(scores, -1, keepdims=True)
    weights = jnp.exp(scores - top)
    total = jnp.sum(weights, -1, keepdims=True)
    out = jnp.einsum("hqk,khe->qhe", (weights / total).astype(bf16), v, preferred_element_type=f32)
    return out.reshape(-1, PW).astype(bf16), top + jnp.log(total)


def attend_back(q, keys_values, mask, log_total, grad_out):
    k, v = keys_values[:, :PW], keys_values[:, PW:]
    q, k, v, g = (item.reshape(-1, PH, HD) for item in (q, k, v, grad_out))
    scores = jnp.einsum("qhe,khe->hqk", q, k, preferred_element_type=f32) * 0.125
    probs = jnp.where(mask, jnp.exp(scores - log_total), 0.0)
    grad_probs = jnp.einsum("qhe,khe->hqk", g, v, preferred_element_type=f32)
    delta = jnp.sum(probs * grad_probs, -1, keepdims=True)
    grad_scores = (probs * (grad_probs - delta)).astype(bf16)
    dq = 0.125 * jnp.einsum("hqk,khe->qhe", grad_scores, k, preferred_element_type=f32)
    dk = 0.125 * jnp.einsum("hqk,qhe->khe", grad_scores, q, preferred_element_type=f32)
    dv = jnp.einsum("hqk,qhe->khe", probs.astype(bf16), g, preferred_element_type=f32)
    dkv = jnp.concatenate([dk.reshape(-1, PW), dv.reshape(-1, PW)], 1)
    return dq.reshape(-1, PW).astype(bf16), dkv


def body(tokens, w_qkv, b_qv, w_proj, b_proj, ln1_gain, ln1_bias, ln2_gain, ln2_bias, w_fc, b_fc, w_out, b_out, d_out):
    size = {name: lax.axis_size(name) for name in ALL}
    devices = math.prod(size.values())
    rows = tokens.shape[1]
    shard = w_qkv.shape[1]
    ff = w_fc.shape[2]
    h, g, x_at, c, f = (lax.axis_index(name) for name in ALL)
    p = 2 * f + x_at
    where = jnp.stack([h, p, c, g, f]).astype(jnp.int32)
    many = size["g"] > 1

    homes = [(a, b) for a in range(size["h"]) for b in range(size["f"])]
    outward = [
        [(a * 2 + b, (2 * ((a // 2 + turn) % 2) + b) * 2 + a % 2) for a, b in homes] for turn in range(2)
    ]

    def both_ways(value, low, moves):
        sent = [lax.dynamic_index_in_dim(value, i, 0, keepdims=False) for i in (low, 1 - low)]
        return [lax.ppermute(item, ("h", "f"), move) for item, move in zip(sent, moves)]

    def own_sequence(value):
        one, two = both_ways(value, h // 2, outward)
        both = jnp.where(h // 2 == 0, jnp.stack([one, two]), jnp.stack([two, one]))
        return [both[:, i].reshape(-1, D) for i in range(2)]

    def back_to_blocks(value):
        moves = [[(b, a) for a, b in move] for move in outward]
        one, two = both_ways(value.reshape(2, rows, -1), h // 2, moves)
        return jnp.where(h // 2 == 0, jnp.stack([one, two]), jnp.stack([two, one]))

    smalls = (b_proj, b_out, ln1_gain, ln1_bias, ln2_gain, ln2_bias, b_qv, b_fc)
    by_part = w_out.reshape(LAYERS, TP, shard, D)

    def plane(pieces):
        return jnp.stack([pieces[0]] + [chip_swap(pieces[k], k) for k in range(1, TP)])

    def layer_pieces(where, layer):
        return launch(
            layer_pieces_kernel(layer), f"layer_pieces_{layer}",
            [((shard, 3 * D + (3 * PW + HD if layer else 0)), bf16)] * TP,
            where, w_fc, by_part, w_proj, w_qkv, scratch=[pltpu.VMEM((TP, shard, D + 3 * PW + HD), bf16)],
        )

    def fetch(pieces):
        return lax.all_gather(pieces, COPIES, axis=0, tiled=True)

    def arrange(own, *widths):
        return [
            item.reshape(D, -1)
            for item in launch(
                arrange_kernel(widths), "arrange", [((devices, shard, width), bf16) for width in widths],
                where, own, swap(own, "c"),
            )
        ]

    feed = layer_pieces(where, 0)
    first = launch(
        first_pieces_kernel, "first_pieces", [((shard, 3 * PW + HD), bf16)] * TP, where, w_qkv, *smalls,
        scratch=[pltpu.VMEM((128, 128), f32), pltpu.VMEM((TP, shard, 3 * PW + HD), bf16)],
    )
    x_own, g_low = own_sequence(jnp.stack([tokens, d_out], 1))
    feed, first, x_own, g_low = lax.optimization_barrier((feed, first, x_own, g_low))
    first, feed, x_own = lax.optimization_barrier((plane(first), feed, x_own))
    x_pieces = share(x_own)
    feed = fetch(plane(feed))
    if many:
        first = lax.all_gather(first, "g", axis=0, tiled=True)
    first = jnp.concatenate([first] + [swap(first, "h", k) for k in range(1, size["h"])], 0)
    later, x_pieces = lax.optimization_barrier((where, x_pieces))
    first, next_feed = lax.optimization_barrier((first, plane(layer_pieces(later, 1))))
    first = jnp.concatenate([first, swap(first, "c")], 0)
    wq, table = launch(
        arrange_first_kernel(size), "arrange_first",
        [((devices, shard, 3 * PW), bf16), ((LAYERS * 8, D), f32)], where, first,
        scratch=[pltpu.VMEM((D, 128), f32), pltpu.VMEM((devices, shard, HD), f32)],
    )
    wq = [wq.reshape(D, 3 * PW), None]
    wf, wo, wp = [None] * LAYERS, [None] * LAYERS, [None] * LAYERS
    count = TP * x_pieces[0].shape[0]
    own = count // TP
    if many:
        second = jnp.arange(2)[None, :, None]
        inside = jnp.arange(rows)[None, None, :]
        chip = p ^ jnp.arange(TP)[:, None, None]

        def positions(group, core):
            place = (chip // 2 + 2 * second) * size["g"] + group
            return (((place * 2 + chip % 2) * 2 + core) * rows + inside).reshape(-1)

        q_pos = positions(g, c)
        k_pos = jnp.concatenate([positions(gi, core) for gi in range(size["g"]) for core in (0, 1)])
        mask = (k_pos[None, :] <= q_pos[:, None])[None]

    def all_keys(kv, other):
        both = jnp.where(c == 0, jnp.stack([kv, other]), jnp.stack([other, kv])).reshape(-1, kv.shape[1])
        return lax.all_gather(both, "g", axis=0, tiled=True)

    saved = []
    state = tuple(x_pieces)
    for l in range(LAYERS):
        x, x_own, normed, q, kv = launch(
            enter_kernel(l == 0, l), f"enter_{l}",
            [((count, D), f32), ((own, D), f32), ((count, D), bf16), ((count, PW), bf16), ((count, 2 * PW), bf16)],
            where, table, wq[l], *state, flops=2 * count * D * 3 * PW,
        )
        other = swap(kv, "c")
        if l + 1 == LAYERS:
            pieces = share(g_low)
            other, next_feed = lax.optimization_barrier((other, next_feed))
            prepared = *arrange(next_feed, D, D), prepared
        if many:
            keys = all_keys(kv, other)
            out, lse = attend(q, keys, mask)
        else:
            keys = None
            out, lse = launch(
                attend_kernel, f"attend_{l}", [((count, PW), bf16), ((count, PH), f32)], where, q, kv, other,
                scratch=[pltpu.VMEM((count, PW), bf16), pltpu.VMEM((count, 2 * PW), bf16),
                         pltpu.VMEM((count, 2 * PW), bf16), pltpu.VMEM((count, PW), bf16)],
                flops=4 * count * 2 * count * PW,
            )
        if l == 0:
            next_mixed, next_feed = fetch(next_feed[..., 2 * D :]), fetch(next_feed[..., : 2 * D])
            prepared = arrange(after(feed, out), D, D, D)
        wf[l], wo[l], wp[l] = prepared
        if l + 1 == LAYERS:
            out, pieces = lax.optimization_barrier((out, pieces))
        outs = [out] + [chip_swap(out, k) for k in range(1, TP)]
        mid, mid_own, heads, normed2, up, act, y0, y1, y2, y3 = launch(
            middle_kernel(l), f"middle_{l}",
            [((count, D), f32), ((own, D), f32), ((count, D), bf16), ((count, D), bf16), ((count, D), f32), ((count, D), bf16)]
            + [((own, D), f32)] + [((own, D), bf16)] * 3,
            where, table, x, *outs, wp[l], wf[l], wo[l],
            scratch=[pltpu.VMEM((TP, count, PW), bf16)], flops=6 * count * D * D,
        )
        if l + 1 < LAYERS:
            total = y0
            for k, y in ((1, y1), (2, y2), (3, y3)):
                total = total + chip_swap(y, k).astype(f32)
        saved.append((x, x_own, normed, q, kv, other, keys, lse, heads, mid, mid_own, normed2, up, act))
        if l + 1 < LAYERS:
            state = (mid, *share(total.astype(bf16)))
            next_mixed, state = lax.optimization_barrier((next_mixed, state))
            prepared, wq[l + 1] = arrange(next_mixed, D, 3 * PW)
    last_parts = [y0, y1, y2, y3]

    copies = devices // (2 * TP)
    halves = [((copies * TP, shard, 2 * D), bf16)] * 2

    def reduce_copies(keep, got):
        total = (keep.astype(f32) + got.astype(f32)).astype(bf16)
        return lax.psum_scatter(total, COPIES, scatter_dimension=0, tiled=True)

    def by_owner(sums):
        return [sums[0]] + [chip_swap(sums[k], k) for k in range(1, TP)]

    line = ((8, D), f32)
    parts = [((own, D), f32)] + [((own, D), bf16)] * 3
    g_own = g_low
    sums = [None] * LAYERS
    for l in reversed(range(LAYERS)):
        x, x_own, normed, q, kv, other, keys, lse, heads, mid, mid_own, normed2, up, act = saved[l]
        g_all, g_up, b_fc_sum, norm2_sum, y0, y1, y2, y3 = launch(
            feed_back_kernel, f"feed_back_{l}", [((count, D), bf16), ((count, D), bf16), line, line] + parts,
            where, *pieces, up, mid, wo[l], wf[l], flops=4 * count * D * D,
        )
        got = [chip_swap(y, k) for k, y in ((1, y1), (2, y2), (3, y3))]
        keep, give = launch(
            feed_weights_kernel, f"feed_weights_{l}", halves, where, act, g_all, normed2, g_up,
            scratch=[pltpu.VMEM((devices, shard, 2 * D), bf16)], flops=4 * count * D * D,
        )
        if l + 1 == LAYERS:
            got, keep, give = lax.optimization_barrier((got, keep, give))
        else:
            got, keep, give, mixed = lax.optimization_barrier((got, keep, give, mixed))
        give = swap(give, "c")
        g_own, g_low, b_proj_sum = launch(
            norm_back_kernel(l, 4), f"norm2_back_{l}", [((own, D), f32), ((own, D), bf16), line],
            where, table, g_own, mid_own, y0, *got,
        )
        give, g_low = lax.optimization_barrier((give, g_low))
        feed = reduce_copies(keep, give)
        pieces = share(g_low)
        if l + 1 == LAYERS:
            last_parts, pieces[1] = lax.optimization_barrier((last_parts, pieces[1]))
            total = last_parts[0]
            for k in range(1, TP):
                total = total + chip_swap(last_parts[k], k).astype(f32)
            meanwhile = (mid_own + total + table[8 * l + 1 : 8 * l + 2]).astype(bf16)
        if many:
            g_attn = jnp.concatenate(pieces, 0)
            mine = lax.dynamic_slice_in_dim(wp[l], p * PW, PW, 0)
            dq, dkv = attend_back(q, keys, mask, lse, dot(g_attn, mine, NT).astype(bf16))
            dkv = lax.psum_scatter(dkv, "g", scatter_dimension=0, tiled=True).reshape(2, count, 2 * PW)
            dkv, give = (lax.dynamic_index_in_dim(dkv, i, 0, keepdims=False) for i in (c, 1 - c))
            give = give.astype(bf16)
        else:
            g_attn, dq, dkv, give = launch(
                attend_back_kernel, f"attend_back_{l}",
                [((count, D), bf16), ((count, PW), bf16), ((count, 2 * PW), f32), ((count, 2 * PW), bf16)],
                where, *pieces, wp[l], q, kv, other, lse,
                scratch=[pltpu.VMEM((count, PW), f32), pltpu.VMEM((count, PW), bf16), pltpu.VMEM((count, PW), bf16),
                         pltpu.VMEM((count, 2 * PW), bf16), pltpu.VMEM((count, 2 * PW), bf16),
                         pltpu.VMEM((count, PW), f32), pltpu.VMEM((count, 2 * PW), f32), pltpu.VMEM((count, 2 * PW), f32)],
                flops=10 * count * 2 * count * PW,
            )
        more = swap(give, "c")
        if l > 0:
            more, output = lax.optimization_barrier((more, meanwhile))
        leave_outs = [((count, 3 * PW), bf16), line, line] + parts
        sums[l] = (b_proj_sum, norm2_sum, b_fc_sum)
        if l > 0:
            g_qkv, b_qkv_sum, norm1_sum, y0, y1, y2, y3 = launch(
                leave_kernel, f"leave_{l}", leave_outs, where, dq, dkv, more, wq[l], x, flops=2 * count * D * 3 * PW,
            )
            got = [chip_swap(y, k) for k, y in ((1, y1), (2, y2), (3, y3))]
            keep, give = launch(
                mixed_weights_kernel, f"mixed_weights_{l}", [((copies * TP, shard, D), bf16)] * 2,
                where, normed, g_qkv, heads, g_attn,
                scratch=[pltpu.VMEM((devices, shard, D), bf16)], flops=4 * count * D * D,
            )
            got, keep, give, feed_last = lax.optimization_barrier((got, keep, give, feed))
            give = swap(give, "c")
            sums[l] = sums[l] + (norm1_sum, b_qkv_sum)
        else:
            keep, give, y0, y1, y2, y3 = launch(
                leave_last_kernel, "leave_last", [((copies * TP, shard, D + 128), bf16)] * 2 + parts,
                where, dq, dkv, more, wq[l], x, normed, heads, g_attn, *sums[0], *sums[1],
                scratch=[pltpu.VMEM((devices, shard, D + 128), bf16), pltpu.VMEM((128, D), f32),
                         pltpu.VMEM((devices, shard, 128), f32), pltpu.VMEM((count, 3 * PW), bf16),
                         pltpu.VMEM((8, D), f32), pltpu.VMEM((8, D), f32)],
                flops=6 * count * D * D,
            )
            give, feed = lax.optimization_barrier((give, feed))
            last = (keep.astype(f32) + swap(give, "c").astype(f32)).astype(bf16)
            got = [chip_swap(y, k) for k, y in ((1, y1), (2, y2), (3, y3))]
            last = lax.all_to_all(after(last, got[0]), ("h", "g", "x", "f"), 0, 0, tiled=True)
            reduced = by_owner(after(jnp.concatenate([feed, feed_last, mixed], 2), got[0]))
        g_own, g_low, _ = launch(
            norm_back_kernel(l, 2), f"norm1_back_{l}", [((own, D), f32), ((own, D), bf16), line],
            where, table, g_own, x_own, y0, *got,
        )
        if l > 0:
            give, g_low = lax.optimization_barrier((give, g_low))
            mixed = reduce_copies(keep, give)
            pieces = share(g_low)
    g_low, reduced = lax.optimization_barrier((g_low, reduced))
    tokens_back = back_to_blocks(jnp.concatenate([output, g_low], 1))
    output, grad_tokens = tokens_back[..., :D], tokens_back[..., D:].astype(f32)
    d_wf, d_wo = launch(
        finish_feed_kernel, "finish_feed", [((LAYERS, shard, ff), f32), ((LAYERS, TP, shard, D), f32)],
        where, *reduced,
        scratch=[pltpu.VMEM((TP, shard, 2 * D), bf16)],
    )
    d_wo = d_wo.reshape(w_out.shape)
    d_wq, d_wp, d_b_proj, d_b_out, d_g1, d_s1, d_g2, d_s2, d_b_qv, d_b_fc = launch(
        finish_mixed_kernel, "finish_mixed",
        [((LAYERS, shard, 3 * D), f32), ((LAYERS, shard, D), f32)] + [(item.shape, f32) for item in smalls],
        where, last, *reduced, scratch=[pltpu.VMEM((LAYERS, TP, shard, D), f32), pltpu.VMEM((128, 128), f32)],
    )
    return (output, grad_tokens, d_wq, d_b_qv, d_wp, d_b_proj, d_g1, d_s1, d_g2, d_s2, d_wf, d_b_fc, d_wo, d_b_out)


def solution(mesh):
    ctx, pair = mesh.shape["ctx"], mesh.shape["fsdp"]
    view = Mesh(mesh.devices.reshape(4, ctx // 16, 2, 2, pair), ALL)
    along = ("h", "g", "x", "c")
    token = P("f", along, None)
    matrix = P(None, ALL, None)
    line = P(None, ALL)
    in_specs = (token, matrix, line, matrix, line, line, line, line, line, matrix, line, matrix, line, token)
    out_specs = (token, token, matrix, line, matrix, line, line, line, line, line, matrix, line, matrix, line)
    return jax.shard_map(body, mesh=view, in_specs=in_specs, out_specs=out_specs, check_vma=False)
```

```python
import functools
import math

import jax
import jax.numpy as jnp
from jax import lax
from jax.experimental import pallas as pl
from jax.experimental.pallas import tpu as pltpu
from jax.sharding import Mesh, PartitionSpec as P

D = 768
H = 12
HD = 64
LAYERS = 2
TP = 4
PH = H // TP
PW = PH * HD
EPS = 1e-05
ROOT = math.sqrt(2.0 / math.pi)
bf16 = jnp.bfloat16
f32 = jnp.float32

ALL = ("h", "g", "x", "c", "f")
COPIES = ("h", "g")
SLOTS = 12


def dot(a, b, dims=((1,), (0,)), precision=None):
    return lax.dot_general(a, b, (dims, ((), ())), preferred_element_type=f32, precision=precision)


NT = ((1,), (1,))
TN = ((0,), (0,))


def swap(value, axis, mask=1):
    names = (axis,) if isinstance(axis, str) else axis
    size = math.prod(lax.axis_size(name) for name in names)
    return lax.ppermute(value, axis, [(i, i ^ mask) for i in range(size)])


def chip_swap(value, mask):
    return swap(value, ("x", "f"), mask % 2 * 2 + mask // 2)


def after(value, event):
    return lax.optimization_barrier((value, event))[0]


def share(own):
    return [own] + [chip_swap(own, k) for k in range(1, TP)]


def launch(kernel, name, outs, scalars, *args, scratch=(), flops=0):
    shapes = [jax.ShapeDtypeStruct(shape, kind) for shape, kind in outs]
    moved = sum(a.size * a.dtype.itemsize for a in args) + sum(math.prod(o.shape) * o.dtype.itemsize for o in shapes)
    return pl.pallas_call(
        kernel,
        name=name,
        out_shape=shapes,
        in_specs=[pl.BlockSpec(memory_space=pltpu.SMEM)] + [pl.BlockSpec(memory_space=pltpu.VMEM)] * len(args),
        out_specs=[pl.BlockSpec(memory_space=pltpu.VMEM)] * len(shapes),
        scratch_shapes=list(scratch),
        cost_estimate=pl.CostEstimate(flops=flops, bytes_accessed=moved, transcendentals=0),
        compiler_params=pltpu.CompilerParams(vmem_limit_bytes=56 * 1024 * 1024),
    )(scalars, *args)


def unit_rows(values):
    center = values - jnp.mean(values, -1, keepdims=True)
    scale = lax.rsqrt(jnp.mean(center * center, -1, keepdims=True) + EPS)
    return center * scale, scale


def interleave(shard):
    block = D // 2
    per = block // (TP * shard)
    row = lax.broadcasted_iota(jnp.int32, (block, block), 0)
    col = lax.broadcasted_iota(jnp.int32, (block, block), 1)
    chip, rest = lax.div(row, per * shard), lax.rem(row, per * shard)
    target = lax.div(rest, shard) * (TP * shard) + chip * shard + lax.rem(rest, shard)
    return (col == target).astype(bf16)


def first_pieces_kernel(where, w_qkv, w_proj, *refs):
    small, outs, (proj, lines, cols) = refs[:8], refs[8 : 8 + TP], refs[8 + TP :]
    p = where[1]
    shard = cols.shape[1]
    lines[...] = jnp.zeros_like(lines)
    at = 0
    for l in range(LAYERS):
        for item in small:
            for first in range(0, item.shape[1], shard):
                lines[at : at + 1, :shard] = item[l : l + 1, first : first + shard].astype(f32)
                at += 1
    columns = lines[...].T[:shard, :HD]
    for q in range(TP):
        parts = [w_qkv[0, :, j * D + q * PW : j * D + (q + 1) * PW].astype(f32) for j in range(3)]
        cols[q] = jnp.concatenate(parts + [columns], 1).astype(bf16)
        proj[q] = w_proj[0, :, q * PW : (q + 1) * PW]
    for k, out in enumerate(outs):
        out[...] = cols[jnp.bitwise_xor(p, k)]


def layer_pieces_kernel(where, w_fc, w_out, w_proj, w_qkv, *refs):
    outs, (cols,) = refs[:TP], refs[TP:]
    p = where[1]
    shard = w_proj.shape[1]
    block = D // 2
    order = interleave(shard)
    for l in range(LAYERS):
        fc = [dot(w_fc[l, :, b * block : (b + 1) * block], order, NT) for b in range(w_fc.shape[2] // block)]
        for q in range(TP):
            lanes = slice(q * block // TP, (q + 1) * block // TP)
            cols[q, :, l * D : (l + 1) * D] = jnp.concatenate([item[:, lanes] for item in fc], 1).astype(bf16)
    for q in range(TP):
        parts = [w_qkv[1, :, j * D + q * PW : j * D + (q + 1) * PW] for j in range(3)]
        cols[q, :, LAYERS * D :] = jnp.concatenate(parts + [jnp.zeros((shard, HD), bf16)], 1)
    for k, out in enumerate(outs):
        q = jnp.bitwise_xor(p, k)
        for l in range(LAYERS):
            out[:, 2 * l * D : (2 * l + 1) * D] = cols[q, :, l * D : (l + 1) * D]
            out[:, (2 * l + 1) * D : (2 * l + 2) * D] = w_out[l, q]
        out[:, 2 * LAYERS * D : (2 * LAYERS + 1) * D] = w_proj[1]
        out[:, (2 * LAYERS + 1) * D :] = cols[q, :, LAYERS * D :]


def arrange_first_kernel(sizes):
    def kernel(where, got, w_first, table, columns, blocks):
        h, p, c = where[0], where[1], where[2]
        devices, shard = w_first.shape[:2]
        groups = sizes["g"]
        columns[...] = jnp.zeros_like(columns)
        for d in range(devices):
            rest, fi = divmod(d, 2)
            rest, ci = divmod(rest, 2)
            rest, xi = divmod(rest, 2)
            hi, gi = divmod(rest, groups)
            copy = (jnp.bitwise_xor(c, ci) * sizes["h"] + jnp.bitwise_xor(h, hi)) * groups + gi
            one = got[copy * TP + jnp.bitwise_xor(p, 2 * fi + xi)].astype(f32)
            w_first[d] = one[:, : 3 * PW].astype(bf16)
            columns[d * shard : (d + 1) * shard, :HD] = one[:, 3 * PW : 3 * PW + HD]
            blocks[d] = one[:, 3 * PW : 3 * PW + HD]
        lines = columns[...].T
        per = PW // (2 * shard)
        for l in range(LAYERS):
            base = SLOTS * l
            table[8 * l : 8 * l + 6, :] = lines[base : base + 6]
            parts = []
            for first in (0, devices // 2):
                for j in range(per):
                    block = blocks[first + p * per + j]
                    parts += [block[:, base + 6 : base + 7], block[:, base + 7 : base + 8]]
                if first == 0:
                    parts.append(jnp.zeros((PW, 1), f32))
            parts.append(jnp.zeros((D - 3 * PW, 1), f32))
            bias = jnp.broadcast_to(jnp.concatenate(parts, 0), (D, 128)).T
            table[8 * l + 6 : 8 * l + 7, :] = bias[0:1]
            row = lines[base + 8 : base + 9]
            for q in range(1, TP):
                row = jnp.where(p == q, lines[base + 8 + q : base + 9 + q], row)
            table[8 * l + 7 : 8 * l + 8, :] = row

    return kernel


def by_core(c, own, oth, work):
    @pl.when(c == 0)
    def _():
        work((own, oth))

    @pl.when(c != 0)
    def _():
        work((oth, own))


def arrange_proj_kernel(sizes):
    def kernel(where, own, oth, out):
        h, p, c = where[0], where[1], where[2]

        def work(cores):
            for d in range(out.shape[0]):
                rest, fi = divmod(d, 2)
                rest, ci = divmod(rest, 2)
                rest, xi = divmod(rest, 2)
                hi, gi = divmod(rest, sizes["g"])
                k = jnp.bitwise_xor(p, 2 * fi + xi)
                place = (jnp.bitwise_xor(h, hi) * sizes["g"] + gi) * TP
                out[d] = jnp.concatenate([cores[ci][k, place + q] for q in range(TP)], 1)

        by_core(c, own, oth, work)

    return kernel


def finish_feed_kernel(where, *refs):
    pieces, (wf_out, wo_out, cols) = refs[:TP], refs[TP:]
    p = where[1]
    shard = wf_out.shape[1]
    block = D // 2
    order = interleave(shard)
    for l in range(LAYERS):
        for k in range(TP):
            cols[jnp.bitwise_xor(p, k)] = pieces[k][:, 2 * D * l : 2 * D * (l + 1)]
        fc = [cols[q, :, :D].astype(f32) for q in range(TP)]
        for b in range(wf_out.shape[2] // block):
            lanes = slice(b * block // TP, (b + 1) * block // TP)
            joined = jnp.concatenate([item[:, lanes] for item in fc], 1).astype(bf16)
            wf_out[l, :, b * block : (b + 1) * block] = dot(joined, order)
        for q in range(TP):
            wo_out[l, q] = cols[q, :, D:].astype(f32)


def finish_mixed_kernel(where, last, m0, m1, m2, m3, wq_out, wp_out, *refs):
    small_outs, (cols, square) = refs[:8], refs[8:]
    p = where[1]
    shard = wq_out.shape[1]
    columns = jnp.zeros((shard, 128), f32)
    for q in range(TP):
        total = jnp.zeros((shard, D + 128), f32)
        for copy in range(last.shape[0] // TP):
            total = total + last[(copy * 2 + q % 2) * 2 + q // 2].astype(f32)
        columns = columns + total[:, D:]
        cols[0, q] = total[:, :D]
    for k, m in enumerate((m0, m1, m2, m3)):
        cols[1, jnp.bitwise_xor(p, k)] = m[:, 2 * D * LAYERS :].astype(f32)
    for l in range(LAYERS):
        for j in range(3):
            wq_out[l, :, j * D : (j + 1) * D] = jnp.concatenate(
                [cols[l, q, :, j * PW : (j + 1) * PW] for q in range(TP)], 1
            )
        wp_out[l] = jnp.concatenate([cols[l, q, :, 3 * PW :] for q in range(TP)], 1)
    square[...] = jnp.zeros_like(square)
    square[:shard, :] = columns
    lines = square[...].T
    at = 0
    for l in range(LAYERS):
        for out in small_outs:
            for first in range(0, out.shape[1], shard):
                out[l : l + 1, first : first + shard] = lines[at : at + 1, :shard]
                at += 1


def enter_kernel(first, index):
    def kernel(where, table, *refs):
        if first:
            *inputs, wq, x_out, xo_out, n_out, q_out, kv_out, u_out = refs
        else:
            mid, *inputs, wq, x_out, xo_out, n_out, q_out, kv_out = refs
        t = table
        gain, shift, bias = (t[8 * index + i : 8 * index + i + 1, :] for i in (2, 3, 6))
        rows = n_out.shape[0] // TP
        for k in range(TP):
            at = slice(k * rows, (k + 1) * rows)
            x = inputs[k][...].astype(f32)
            if not first:
                x = mid[at, :] + x + t[8 * (index - 1) + 1 : 8 * (index - 1) + 2, :]
            x_out[at, :] = x
            if k == 0:
                xo_out[...] = x
            unit, _ = unit_rows(x)
            n_out[at, :] = (unit * gain + shift).astype(bf16)
            if first:
                u_out[at, :] = unit.astype(bf16)
        got = (dot(n_out[...], wq[...]) + bias[:, : 3 * PW]).astype(bf16)
        kv_out[...] = got[:, PW:]
        q_out[...] = got[:, :PW]

    return kernel


def tile_rows(p, t, size):
    return pl.multiple_of((jnp.bitwise_xor(t % TP, p) * 2 + t // TP) * size, size)


def mask_of(c, chunk, size):
    a = lax.broadcasted_iota(jnp.int32, (chunk, 2 * chunk), 0)
    b = lax.broadcasted_iota(jnp.int32, (chunk, 2 * chunk), 1)
    ahead = lax.div(b - chunk, size) < lax.div(a, size) + c
    return jnp.where(b < chunk, b - a, jnp.where(ahead, 0, 1)) <= 0


def by_position(p, count, q_ref, own_ref, oth_ref, qn, kc, vc):
    size = count // (2 * TP)
    for t in range(2 * TP):
        at = pl.ds(tile_rows(p, t, size), size)
        qn[t * size : (t + 1) * size, :] = q_ref[at, :]
        for source, first in ((own_ref, 0), (oth_ref, 2)):
            here = slice((t // 2 * 4 + first + t % 2) * size, (t // 2 * 4 + first + t % 2 + 1) * size)
            both = source[at, :]
            kc[here, :] = both[:, :PW]
            vc[here, :] = both[:, PW:]


def attend_kernel(where, q_ref, own_ref, oth_ref, out_ref, lse_ref, wide_ref, qn, kc, vc):
    p, c = where[1], where[2]
    count = q_ref.shape[0]
    size = count // (2 * TP)
    chunk = 2 * size
    by_position(p, count, q_ref, own_ref, oth_ref, qn, kc, vc)
    allowed = mask_of(c, chunk, size)
    for j in range(count // chunk):
        rows = slice(j * chunk, (j + 1) * chunk)
        past, last = slice(0, 2 * j * chunk), slice(2 * j * chunk, 2 * (j + 1) * chunk)
        outs = []
        for h in range(PH):
            lanes = slice(h * HD, (h + 1) * HD)
            q = qn[rows, lanes]
            scores = [jnp.where(allowed, dot(q, kc[last, lanes], NT) * 0.125, -1e30)]
            if j > 0:
                scores.append(dot(q, kc[past, lanes], NT) * 0.125)
            top = functools.reduce(jnp.maximum, [jnp.max(v, -1, keepdims=True) for v in scores])
            weights = [jnp.exp(v - top) for v in scores]
            total = sum(jnp.sum(v, -1, keepdims=True) for v in weights)
            out = dot(weights[0].astype(bf16), vc[last, lanes])
            if j > 0:
                out = out + dot(weights[1].astype(bf16), vc[past, lanes])
            outs.append(out / total)
            lse_ref[rows, h : h + 1] = top + jnp.log(total)
        out = jnp.concatenate(outs, 1)
        wide_ref[rows, :] = out
        low = out.astype(bf16)
        for t in (2 * j, 2 * j + 1):
            out_ref[pl.ds(tile_rows(p, t, size), size), :] = low[(t - 2 * j) * size : (t - 2 * j + 1) * size]


def middle_kernel(index):
    def kernel(where, table, o0, o1, o2, o3, wp, x, wf, wo, mid_out, mo_out, heads_out, n_out, slope_out, act_out, y0, y1, y2, y3, got):
        p = where[1]
        t = table
        b_proj, gain, shift, b_up = (t[8 * index + i : 8 * index + i + 1, :] for i in (0, 4, 5, 7))
        rows = x.shape[0] // TP
        for k, o in enumerate((o0, o1, o2, o3)):
            for m in range(TP):
                got[k, m * rows : (m + 1) * rows, :] = o[(m ^ k) * rows : ((m ^ k) + 1) * rows, :]
        heads_out[...] = jnp.concatenate([got[jnp.bitwise_xor(p, q)] for q in range(TP)], 1)
        for m, y in enumerate((y0, y1, y2, y3)):
            at = slice(m * rows, (m + 1) * rows)
            mid = x[at, :] + dot(heads_out[at, :], wp[...]) + b_proj
            mid_out[at, :] = mid
            if m == 0:
                mo_out[...] = mid
            unit, _ = unit_rows(mid)
            n_out[at, :] = (unit * gain + shift).astype(bf16)
        up = dot(n_out[...], wf[...]) + b_up
        square = up * up
        bent = jnp.tanh(ROOT * up * (1.0 + 0.044715 * square))
        half = 0.5 * (1.0 + bent)
        act_out[...] = (up * half).astype(bf16)
        slope_out[...] = (half + up * half * (1.0 - bent) * (ROOT * (1.0 + 3 * 0.044715 * square))).astype(bf16)
        for m, y in ((3, y3), (2, y2), (1, y1), (0, y0)):
            at = slice(m * rows, (m + 1) * rows)
            y[...] = dot(act_out[at, :], wo[...]).astype(y.dtype)

    return kernel


def part_sums(parts, values, acc):
    acc[...] = jnp.zeros(acc.shape, f32)
    rows = parts[0].shape[0]
    for k, part in enumerate(parts):
        unit, _ = unit_rows(values[k * rows : (k + 1) * rows, :])
        part = part[...].astype(f32)
        acc[0:1, :] += jnp.sum(part * unit, 0, keepdims=True)
        acc[1:2, :] += jnp.sum(part, 0, keepdims=True)


def feed_back_kernel(where, g0, g1, g2, g3, slope, wo, wf, g_out, gu_out, y0, y1, y2, y3):
    rows = g0.shape[0]
    for k, (g, y) in enumerate(((g0, y0), (g1, y1), (g2, y2), (g3, y3))):
        at = slice(k * rows, (k + 1) * rows)
        g_out[at, :] = g[...]
        g_up = (slope[at, :].astype(f32) * dot(g_out[at, :], wo[...], NT)).astype(bf16)
        gu_out[at, :] = g_up
        y[...] = dot(g_up, wf[...], NT).astype(y.dtype)


def norm_back_kernel(index, which):
    def kernel(where, value, grad, table, r0, r1, r2, r3, g_out, low_out, sum_out):
        gain = table[8 * index + which : 8 * index + which + 1, :]
        unit, scale = unit_rows(value[...])
        cot = r0[...] + r1[...].astype(f32) + r2[...].astype(f32) + r3[...].astype(f32)
        inner = cot * gain
        moved = scale * (
            inner - jnp.mean(inner, -1, keepdims=True) - unit * jnp.mean(inner * unit, -1, keepdims=True)
        )
        total = grad[...].astype(f32) + moved
        g_out[...] = total
        low = total.astype(bf16)
        low_out[...] = low
        sum_out[...] = jnp.zeros(sum_out.shape, f32)
        sum_out[0:1, :] = jnp.sum(low.astype(f32), 0, keepdims=True)

    return kernel


def attend_back_kernel(where, q_ref, own_ref, oth_ref, wide_ref, lse_ref, wp, g0, g1, g2, g3, ga_out, dq_ref, down_ref, doth_ref, local, gn, qn, kc, vc, dqn, dkc, dvc):
    p, c = where[1], where[2]
    count = q_ref.shape[0]
    size = count // (2 * TP)
    chunk = 2 * size
    rows_of = g0.shape[0]
    by_position(p, count, q_ref, own_ref, oth_ref, qn, kc, vc)
    for k, g in enumerate((g0, g1, g2, g3)):
        ga_out[k * rows_of : (k + 1) * rows_of, :] = g[...]
    mine = wp[pl.ds(pl.multiple_of(p * PW, PW), PW), :]
    local[...] = dot(ga_out[...], mine, NT)
    for t in range(2 * TP):
        gn[t * size : (t + 1) * size, :] = local[pl.ds(tile_rows(p, t, size), size), :].astype(bf16)
    product = gn[...].astype(f32) * wide_ref[...]
    delta = [jnp.sum(product[:, h * HD : (h + 1) * HD], -1, keepdims=True) for h in range(PH)]
    allowed = mask_of(c, chunk, size)
    dqn[...] = jnp.zeros_like(dqn)
    for b in range(count // chunk):
        rows, keys = slice(b * chunk, count), slice(2 * b * chunk, 2 * (b + 1) * chunk)
        dqs, dks, dvs = [], [], []
        for h in range(PH):
            lanes = slice(h * HD, (h + 1) * HD)
            q, g, k = qn[rows, lanes], gn[rows, lanes], kc[keys, lanes]
            scores = dot(q, k, NT) * 0.125 - lse_ref[rows, h : h + 1]
            first = jnp.where(allowed, scores[:chunk], -1e30)
            if b + 1 < count // chunk:
                first = jnp.concatenate([first, scores[chunk:]], 0)
            probs = jnp.exp(first)
            grad = dot(g, vc[keys, lanes], NT)
            ds = (probs * (grad - delta[h][b * chunk :])).astype(bf16)
            dqs.append(dot(ds, k))
            dks.append(dot(ds, q, TN))
            dvs.append(dot(probs.astype(bf16), g, TN))
        dqn[rows, :] += jnp.concatenate(dqs, 1)
        dkc[keys, :] = jnp.concatenate(dks, 1) * 0.125
        dvc[keys, :] = jnp.concatenate(dvs, 1)
    for t in range(2 * TP):
        at = pl.ds(tile_rows(p, t, size), size)
        for out, first in ((doth_ref, 2), (down_ref, 0)):
            here = slice((t // 2 * 4 + first + t % 2) * size, (t // 2 * 4 + first + t % 2 + 1) * size)
            out[at, :] = jnp.concatenate([dkc[here, :], dvc[here, :]], 1).astype(out.dtype)
        dq_ref[at, :] = (dqn[t * size : (t + 1) * size, :] * 0.125).astype(bf16)


def leave_kernel(where, dq, dkv, more, wq, gq_out, y0, y1, y2, y3):
    gq_out[:, :PW] = dq[...]
    gq_out[:, PW:] = (dkv[...] + more[...].astype(f32)).astype(bf16)
    rows = y0.shape[0]
    for k, y in ((3, y3), (2, y2), (1, y1), (0, y0)):
        y[...] = dot(gq_out[k * rows : (k + 1) * rows, :], wq[...], NT).astype(y.dtype)


def arrange_kernel(widths):
    def kernel(where, own, oth, *outs):
        p, c = where[1], where[2]

        def work(cores):
            for d in range(outs[0].shape[0]):
                rest, f = divmod(d, 2)
                rest, core = divmod(rest, 2)
                copy, x = divmod(rest, 2)
                block = copy * TP + jnp.bitwise_xor(2 * f + x, p)
                at = 0
                for out, width in zip(outs, widths):
                    out[d] = cores[core][block, :, at : at + width]
                    at += width

        by_core(c, own, oth, work)

    return kernel


def scatter_blocks(where, blocks, keep, give):
    p, c = where[1], where[2]
    for i in range(keep.shape[0]):
        copy, k = divmod(i, TP)
        chip = jnp.bitwise_xor(p, k)
        for out, core in ((keep, c), (give, 1 - c)):
            out[i] = blocks[((copy * 2 + lax.rem(chip, 2)) * 2 + core) * 2 + lax.div(chip, 2)]


def feed_weights_kernel(where, normed, g_up, act, g, mid, y0, y1, y2, y3, keep, give, b_out, sums, blocks):
    part_sums((y0, y1, y2, y3), mid, sums)
    sums[2:3, :] = jnp.sum(g[: y0.shape[0], :].astype(f32), 0, keepdims=True)
    b_out[...] = jnp.zeros(b_out.shape, f32)
    b_out[0:1, :] = jnp.sum(g_up[...].astype(f32), 0, keepdims=True)
    width = normed.shape[1]
    shard = keep.shape[1]
    for at, (a, b) in ((0, (normed, g_up)), (width, (act, g))):
        value = dot(a[...], b[...], TN)
        for d in range(blocks.shape[0]):
            blocks[d, :, at : at + width] = value[d * shard : (d + 1) * shard].astype(bf16)
    scatter_blocks(where, blocks, keep, give)


def mixed_weights(where, normed, g_qkv, heads, g_attn):
    p = where[1]
    value = dot(normed[...], g_qkv[...], TN)
    whole = dot(heads[...], g_attn[...], TN)
    mine = whole[:, :PW]
    for q in range(1, TP):
        mine = jnp.where(p == q, whole[:, q * PW : (q + 1) * PW], mine)
    return jnp.concatenate([value, mine], 1)


def mixed_weights_kernel(where, normed, g_qkv, heads, g_attn, x, y0, y1, y2, y3, keep, give, b_out, sums, blocks):
    part_sums((y0, y1, y2, y3), x, sums)
    b_out[...] = jnp.zeros(b_out.shape, f32)
    b_out[0:1, : 3 * PW] = jnp.sum(g_qkv[...].astype(f32), 0, keepdims=True)
    value = mixed_weights(where, normed, g_qkv, heads, g_attn)
    shard = blocks.shape[1]
    for d in range(blocks.shape[0]):
        blocks[d] = value[d * shard : (d + 1) * shard].astype(bf16)
    scatter_blocks(where, blocks, keep, give)


def leave_last_kernel(where, dq, dkv, more_keys, wq, unit, normed, heads, g_attn, *refs):
    sums, refs = refs[: 5 * LAYERS - 2], refs[5 * LAYERS - 2 :]
    keep, give, y0, y1, y2, y3, blocks, lines, more, g_qkv = refs
    leave_kernel(where, dq, dkv, more_keys, wq, g_qkv, y0, y1, y2, y3)
    part = jnp.concatenate([y[...].astype(f32) for y in (y0, y1, y2, y3)], 0)
    norm1_first = [jnp.sum(part * unit[...].astype(f32), 0, keepdims=True), jnp.sum(part, 0, keepdims=True)]
    b_qkv = jnp.sum(g_qkv[...].astype(f32), 0, keepdims=True)
    p, c = where[1], where[2]
    devices, shard = blocks.shape[:2]
    per = PW // (2 * shard)
    lines[...] = jnp.zeros_like(lines)
    more[...] = jnp.zeros_like(more)
    for l in range(LAYERS):
        b_proj, norm2, fc = sums[3 * l : 3 * l + 3]
        if l == 0:
            (gain, shift), qkv = norm1_first, jnp.concatenate([b_qkv, jnp.zeros((1, D - 3 * PW), f32)], 1)
        else:
            gain, shift, qkv = sums[6][0:1, :], sums[6][1:2, :], sums[7][0:1, :]
        base = SLOTS * l
        rows = (b_proj[0:1, :], norm2[2:3, :], gain, shift, norm2[0:1, :], norm2[1:2, :])
        for i, row in enumerate(rows):
            lines[base + i : base + i + 1, :] = row
        for q in range(TP):
            lines[base + 8 + q : base + 9 + q, :] = jnp.where(p == q, fc[0:1, :], 0.0)
        bias = jnp.broadcast_to(qkv, (128, D)).T
        for first, start in ((0, 0), (devices // 2, 2 * PW)):
            for j in range(2 * per):
                lane = base + 6 + j % 2
                more[first + p * per + j // 2, :, lane : lane + 1] = bias[
                    start + j * shard : start + (j + 1) * shard, 0:1
                ]
    columns = lines[...].T
    value = mixed_weights(where, normed, g_qkv, heads, g_attn)
    for d in range(devices):
        at = slice(d * shard, (d + 1) * shard)
        blocks[d] = jnp.concatenate([value[at], columns[at] + more[d]], 1).astype(bf16)
    for i in range(keep.shape[0]):
        rest, f = divmod(i, 2)
        keep[i] = blocks[(rest * 2 + c) * 2 + f]
        give[i] = blocks[(rest * 2 + 1 - c) * 2 + f]


def attend(q, keys_values, mask):
    k, v = keys_values[:, :PW], keys_values[:, PW:]
    q, k, v = (item.reshape(-1, PH, HD) for item in (q, k, v))
    scores = jnp.einsum("qhe,khe->hqk", q, k, preferred_element_type=f32) * 0.125
    scores = jnp.where(mask, scores, -1e30)
    top = jnp.max(scores, -1, keepdims=True)
    weights = jnp.exp(scores - top)
    total = jnp.sum(weights, -1, keepdims=True)
    out = jnp.einsum("hqk,khe->qhe", (weights / total).astype(bf16), v, preferred_element_type=f32)
    return out.reshape(-1, PW).astype(bf16), top + jnp.log(total)


def attend_back(q, keys_values, mask, log_total, grad_out):
    k, v = keys_values[:, :PW], keys_values[:, PW:]
    q, k, v, g = (item.reshape(-1, PH, HD) for item in (q, k, v, grad_out))
    scores = jnp.einsum("qhe,khe->hqk", q, k, preferred_element_type=f32) * 0.125
    probs = jnp.where(mask, jnp.exp(scores - log_total), 0.0)
    grad_probs = jnp.einsum("qhe,khe->hqk", g, v, preferred_element_type=f32)
    delta = jnp.sum(probs * grad_probs, -1, keepdims=True)
    grad_scores = (probs * (grad_probs - delta)).astype(bf16)
    dq = 0.125 * jnp.einsum("hqk,khe->qhe", grad_scores, k, preferred_element_type=f32)
    dk = 0.125 * jnp.einsum("hqk,qhe->khe", grad_scores, q, preferred_element_type=f32)
    dv = jnp.einsum("hqk,qhe->khe", probs.astype(bf16), g, preferred_element_type=f32)
    dkv = jnp.concatenate([dk.reshape(-1, PW), dv.reshape(-1, PW)], 1)
    return dq.reshape(-1, PW).astype(bf16), dkv


def body(tokens, w_qkv, b_qv, w_proj, b_proj, ln1_gain, ln1_bias, ln2_gain, ln2_bias, w_fc, b_fc, w_out, b_out, d_out):
    size = {name: lax.axis_size(name) for name in ALL}
    devices = math.prod(size.values())
    rows = tokens.shape[1]
    shard = w_qkv.shape[1]
    ff = w_fc.shape[2]
    h, g, x_at, c, f = (lax.axis_index(name) for name in ALL)
    p = 2 * f + x_at
    where = jnp.stack([h, p, c, g, f]).astype(jnp.int32)
    many = size["g"] > 1

    homes = [(a, b) for a in range(size["h"]) for b in range(size["f"])]
    outward = [
        [(a * 2 + b, (2 * ((a // 2 + turn) % 2) + b) * 2 + a % 2) for a, b in homes] for turn in range(2)
    ]

    def both_ways(value, low, moves):
        sent = [lax.dynamic_index_in_dim(value, i, 0, keepdims=False) for i in (low, 1 - low)]
        return [lax.ppermute(item, ("h", "f"), move) for item, move in zip(sent, moves)]

    def own_sequence(value):
        one, two = both_ways(value, h // 2, outward)
        both = jnp.where(h // 2 == 0, jnp.stack([one, two]), jnp.stack([two, one]))
        return [both[:, i].reshape(-1, D) for i in range(2)]

    def back_to_blocks(value):
        moves = [[(b, a) for a, b in move] for move in outward]
        one, two = both_ways(value.reshape(2, rows, -1), h // 2, moves)
        return jnp.where(h // 2 == 0, jnp.stack([one, two]), jnp.stack([two, one]))

    smalls = (b_proj, b_out, ln1_gain, ln1_bias, ln2_gain, ln2_bias, b_qv, b_fc)
    by_part = w_out.reshape(LAYERS, TP, shard, D)

    def plane(pieces):
        return jnp.stack([pieces[0]] + [chip_swap(pieces[k], k) for k in range(1, TP)])

    def fetch(pieces):
        return lax.all_gather(pieces, COPIES, axis=0, tiled=True)

    def arrange(own, *widths):
        return [
            item.reshape(D, -1)
            for item in launch(
                arrange_kernel(widths), "arrange", [((devices, shard, width), bf16) for width in widths],
                where, own, swap(own, "c"),
            )
        ]

    *first, proj = launch(
        first_pieces_kernel, "first_pieces",
        [((shard, 3 * PW + HD), bf16)] * TP + [((TP, shard, PW), bf16)], where, w_qkv, w_proj, *smalls,
        scratch=[pltpu.VMEM((128, 128), f32), pltpu.VMEM((TP, shard, 3 * PW + HD), bf16)],
    )
    feed = launch(
        layer_pieces_kernel, "layer_pieces", [((shard, (2 * LAYERS + 1) * D + 3 * PW + HD), bf16)] * TP,
        where, w_fc, by_part, w_proj, w_qkv, scratch=[pltpu.VMEM((TP, shard, LAYERS * D + 3 * PW + HD), bf16)],
    )
    x_own, g_low = own_sequence(jnp.stack([tokens, d_out], 1))
    feed, first, x_own, g_low = lax.optimization_barrier((feed, first, x_own, g_low))
    first, feed, x_own = lax.optimization_barrier((plane(first), feed, x_own))
    first = jnp.concatenate([first, proj], 2)
    if many:
        first = lax.all_gather(first, "g", axis=0, tiled=True)
    first = jnp.concatenate([first] + [swap(first, "h", k) for k in range(1, size["h"])], 0)
    feed = [feed[0]] + [chip_swap(feed[k], k) for k in range(1, TP)]
    x_pieces = share(after(x_own, feed[1]))

    def part_of(start, stop):
        return jnp.stack([item[:, start:stop] for item in feed])

    next_feed, next_mixed = part_of(2 * D, 4 * D), part_of(4 * D, feed[0].shape[1])
    feed = fetch(part_of(0, 2 * D))
    proj = after(first[:, :, 3 * PW + HD :], x_pieces)
    proj = [proj] + [chip_swap(proj, k) for k in range(1, TP)]
    first = jnp.concatenate([first, swap(first, "c")], 0)
    wq, table = launch(
        arrange_first_kernel(size), "arrange_first",
        [((devices, shard, 3 * PW), bf16), ((LAYERS * 8, D), f32)], where, first, flops=1 << 34,
        scratch=[pltpu.VMEM((D, 128), f32), pltpu.VMEM((devices, shard, HD), f32)],
    )
    wq = [wq.reshape(D, 3 * PW), None]
    wf, wo, wp = [None] * LAYERS, [None] * LAYERS, [None] * LAYERS
    count = TP * x_pieces[0].shape[0]
    own = count // TP
    if many:
        second = jnp.arange(2)[None, :, None]
        inside = jnp.arange(rows)[None, None, :]
        chip = p ^ jnp.arange(TP)[:, None, None]

        def positions(group, core):
            place = (chip // 2 + 2 * second) * size["g"] + group
            return (((place * 2 + chip % 2) * 2 + core) * rows + inside).reshape(-1)

        q_pos = positions(g, c)
        k_pos = jnp.concatenate([positions(gi, core) for gi in range(size["g"]) for core in (0, 1)])
        mask = (k_pos[None, :] <= q_pos[:, None])[None]

    def all_keys(kv, other):
        both = jnp.where(c == 0, jnp.stack([kv, other]), jnp.stack([other, kv])).reshape(-1, kv.shape[1])
        return lax.all_gather(both, "g", axis=0, tiled=True)

    saved = []
    state = tuple(x_pieces)
    for l in range(LAYERS):
        x, x_own, normed, q, kv, *unit = launch(
            enter_kernel(l == 0, l), f"enter_{l}",
            [((count, D), f32), ((own, D), f32), ((count, D), bf16), ((count, PW), bf16), ((count, 2 * PW), bf16)]
            + [((count, D), bf16)] * (l == 0),
            where, table, *state, wq[l], flops=2 * count * D * 3 * PW,
        )
        other = swap(kv, "c")
        if many:
            keys = all_keys(kv, other)
            out, lse = attend(q, keys, mask)
            wide = None
        else:
            keys = None
            out, lse, wide = launch(
                attend_kernel, f"attend_{l}", [((count, PW), bf16), ((count, PH), f32), ((count, PW), f32)],
                where, q, kv, other,
                scratch=[pltpu.VMEM((count, PW), bf16)] + [pltpu.VMEM((2 * count, PW), bf16)] * 2,
                flops=4 * count * 2 * count * PW,
            )
        if l == 0:
            next_mixed, next_feed = fetch(next_mixed), fetch(next_feed)
        if l == 0:
            out, proj = lax.optimization_barrier((out, proj))
        outs = [out] + [chip_swap(out, k) for k in range(1, TP)]
        if l == 0:
            proj = jnp.stack(proj)
            (proj,) = launch(
                arrange_proj_kernel(size), "arrange_proj", [((devices, shard, D), bf16)],
                where, proj, swap(proj, "c"),
            )
            prepared = *arrange(after(feed, out), D, D), proj.reshape(D, D)
        if l + 1 == LAYERS:
            pieces = share(after(g_low, outs[1]))
            prepared = *arrange(after(next_feed, out), D, D), prepared
        wf[l], wo[l], wp[l] = prepared
        mid, mid_own, heads, normed2, slope, act, y0, y1, y2, y3 = launch(
            middle_kernel(l), f"middle_{l}",
            [((count, D), f32), ((own, D), f32), ((count, D), bf16), ((count, D), bf16), ((count, D), bf16), ((count, D), bf16)]
            + [((own, D), f32)] + [((own, D), bf16)] * 3,
            where, table, *outs, wp[l], x, wf[l], wo[l],
            scratch=[pltpu.VMEM((TP, count, PW), bf16)], flops=6 * count * D * D,
        )
        if l + 1 < LAYERS:
            total = y0
            for k, y in ((1, y1), (2, y2), (3, y3)):
                total = total + chip_swap(y, k).astype(f32)
        saved.append((x, x_own, normed, q, kv, other, keys, lse, wide, heads, mid, mid_own, normed2, slope, act, unit))
        if l + 1 < LAYERS:
            next_mixed, total = lax.optimization_barrier((next_mixed, total))
            state = (mid, *share(total.astype(bf16)))
            prepared, wq[l + 1] = arrange(next_mixed, D, 3 * PW)
    last_parts = [y0, y1, y2, y3]

    copies = devices // (2 * TP)
    halves = [((copies * TP, shard, 2 * D), bf16)] * 2

    def reduce_copies(keep, got):
        total = (keep.astype(f32) + got.astype(f32)).astype(bf16)
        return lax.psum_scatter(total, COPIES, scatter_dimension=0, tiled=True)

    def by_owner(sums):
        return [sums[0]] + [chip_swap(sums[k], k) for k in range(1, TP)]

    line = ((8, D), f32)
    parts = [((own, D), f32)] + [((own, D), bf16)] * 3
    g_own = g_low
    sums = [None] * LAYERS
    for l in reversed(range(LAYERS)):
        x, x_own, normed, q, kv, other, keys, lse, wide, heads, mid, mid_own, normed2, slope, act, unit = saved[l]
        g_all, g_up, y0, y1, y2, y3 = launch(
            feed_back_kernel, f"feed_back_{l}", [((count, D), bf16), ((count, D), bf16)] + parts,
            where, *pieces, slope, wo[l], wf[l], flops=4 * count * D * D,
        )
        got = [chip_swap(y, k) for k, y in ((1, y1), (2, y2), (3, y3))]
        keep, give, b_fc_sum, norm2_sum = launch(
            feed_weights_kernel, f"feed_weights_{l}", halves + [line, line],
            where, normed2, g_up, act, g_all, mid, y0, y1, y2, y3,
            scratch=[pltpu.VMEM((devices, shard, 2 * D), bf16)], flops=4 * count * D * D,
        )
        if l + 1 == LAYERS:
            got, keep, give = lax.optimization_barrier((got, keep, give))
        else:
            got, keep, give, mixed, output = lax.optimization_barrier((got, keep, give, mixed, output))
        give = swap(give, "c")
        g_own, g_low, b_proj_sum = launch(
            norm_back_kernel(l, 4), f"norm2_back_{l}", [((own, D), f32), ((own, D), bf16), line],
            where, mid_own, g_own, table, y0, *got,
        )
        give, g_low = lax.optimization_barrier((give, g_low))
        feed = reduce_copies(keep, give)
        pieces = share(g_low)
        if l + 1 == LAYERS:
            last_parts, pieces[1] = lax.optimization_barrier((last_parts, pieces[1]))
            total = last_parts[0]
            for k in range(1, TP):
                total = total + chip_swap(last_parts[k], k).astype(f32)
            meanwhile = (mid_own + total + table[8 * l + 1 : 8 * l + 2]).astype(bf16)
        if many:
            g_attn = jnp.concatenate(pieces, 0)
            mine = lax.dynamic_slice_in_dim(wp[l], p * PW, PW, 0)
            dq, dkv = attend_back(q, keys, mask, lse, dot(g_attn, mine, NT).astype(bf16))
            dkv = lax.psum_scatter(dkv, "g", scatter_dimension=0, tiled=True).reshape(2, count, 2 * PW)
            dkv, give = (lax.dynamic_index_in_dim(dkv, i, 0, keepdims=False) for i in (c, 1 - c))
            give = give.astype(bf16)
        else:
            g_attn, dq, dkv, give = launch(
                attend_back_kernel, f"attend_back_{l}",
                [((count, D), bf16), ((count, PW), bf16), ((count, 2 * PW), f32), ((count, 2 * PW), bf16)],
                where, q, kv, other, wide, lse, wp[l], *pieces,
                scratch=[pltpu.VMEM((count, PW), f32), pltpu.VMEM((count, PW), bf16), pltpu.VMEM((count, PW), bf16)]
                + [pltpu.VMEM((2 * count, PW), bf16)] * 2 + [pltpu.VMEM((count, PW), f32)]
                + [pltpu.VMEM((2 * count, PW), f32)] * 2,
                flops=10 * count * 2 * count * PW,
            )
        more = swap(give, "c")
        if l > 0:
            more, output = lax.optimization_barrier((more, meanwhile))
            output = back_to_blocks(output)
        sums[l] = (b_proj_sum, norm2_sum, b_fc_sum)
        if l > 0:
            g_qkv, y0, y1, y2, y3 = launch(
                leave_kernel, f"leave_{l}", [((count, 3 * PW), bf16)] + parts,
                where, dq, dkv, more, wq[l], flops=2 * count * D * 3 * PW,
            )
            got = [chip_swap(y, k) for k, y in ((1, y1), (2, y2), (3, y3))]
            keep, give, b_qkv_sum, norm1_sum = launch(
                mixed_weights_kernel, f"mixed_weights_{l}", [((copies * TP, shard, D), bf16)] * 2 + [line, line],
                where, normed, g_qkv, heads, g_attn, x, y0, y1, y2, y3,
                scratch=[pltpu.VMEM((devices, shard, D), bf16)], flops=4 * count * D * D,
            )
            got, keep, give, feed_last = lax.optimization_barrier((got, keep, give, feed))
            give = swap(give, "c")
            sums[l] = sums[l] + (norm1_sum, b_qkv_sum)
        else:
            keep, give, y0, y1, y2, y3 = launch(
                leave_last_kernel, "leave_last", [((copies * TP, shard, D + 128), bf16)] * 2 + parts,
                where, dq, dkv, more, wq[l], *unit, normed, heads, g_attn, *sums[0], *sums[1],
                scratch=[pltpu.VMEM((devices, shard, D + 128), bf16), pltpu.VMEM((128, D), f32),
                         pltpu.VMEM((devices, shard, 128), f32), pltpu.VMEM((count, 3 * PW), bf16)],
                flops=6 * count * D * D,
            )
            give, feed = lax.optimization_barrier((give, feed))
            last = (keep.astype(f32) + swap(give, "c").astype(f32)).astype(bf16)
            got = [chip_swap(y, k) for k, y in ((1, y1), (2, y2), (3, y3))]
            last = after(last, got[0])
            reduced = by_owner(after(jnp.concatenate([feed, feed_last, mixed], 2), last))
            last = lax.all_to_all(last, ("h", "g", "x", "f"), 0, 0, tiled=True)
        g_own, g_low, _ = launch(
            norm_back_kernel(l, 2), f"norm1_back_{l}", [((own, D), f32), ((own, D), bf16), line],
            where, x_own, g_own, table, y0, *got,
        )
        if l > 0:
            give, g_low = lax.optimization_barrier((give, g_low))
            mixed = reduce_copies(keep, give)
            pieces = share(g_low)
    g_low, reduced = lax.optimization_barrier((g_low, reduced))
    grad_tokens = back_to_blocks(g_low).astype(f32)
    d_wf, d_wo = launch(
        finish_feed_kernel, "finish_feed", [((LAYERS, shard, ff), f32), ((LAYERS, TP, shard, D), f32)],
        where, *reduced,
        scratch=[pltpu.VMEM((TP, shard, 2 * D), bf16)],
    )
    d_wo = d_wo.reshape(w_out.shape)
    d_wq, d_wp, d_b_proj, d_b_out, d_g1, d_s1, d_g2, d_s2, d_b_qv, d_b_fc = launch(
        finish_mixed_kernel, "finish_mixed",
        [((LAYERS, shard, 3 * D), f32), ((LAYERS, shard, D), f32)] + [(item.shape, f32) for item in smalls],
        where, last, *reduced, scratch=[pltpu.VMEM((LAYERS, TP, shard, D), f32), pltpu.VMEM((128, 128), f32)],
    )
    return (output, grad_tokens, d_wq, d_b_qv, d_wp, d_b_proj, d_g1, d_s1, d_g2, d_s2, d_wf, d_b_fc, d_wo, d_b_out)


def solution(mesh):
    ctx, pair = mesh.shape["ctx"], mesh.shape["fsdp"]
    view = Mesh(mesh.devices.reshape(4, ctx // 16, 2, 2, pair), ALL)
    along = ("h", "g", "x", "c")
    token = P("f", along, None)
    matrix = P(None, ALL, None)
    line = P(None, ALL)
    in_specs = (token, matrix, line, matrix, line, line, line, line, line, matrix, line, matrix, line, token)
    out_specs = (token, token, matrix, line, matrix, line, line, line, line, line, matrix, line, matrix, line)
    return jax.shard_map(body, mesh=view, in_specs=in_specs, out_specs=out_specs, check_vma=False)
```

```python
import functools
import math

import jax
import jax.numpy as jnp
from jax import lax
from jax.experimental import pallas as pl
from jax.experimental.pallas import tpu as pltpu
from jax.sharding import Mesh, PartitionSpec as P

D = 768
H = 12
HD = 64
LAYERS = 2
TP = 4
PH = H // TP
PW = PH * HD
EPS = 1e-05
ROOT = math.sqrt(2.0 / math.pi)
bf16 = jnp.bfloat16
f32 = jnp.float32

ALL = ("h", "g", "x", "c", "f")
COPIES = ("h", "g")
SLOTS = 12


def dot(a, b, dims=((1,), (0,)), precision=None):
    return lax.dot_general(a, b, (dims, ((), ())), preferred_element_type=f32, precision=precision)


NT = ((1,), (1,))
TN = ((0,), (0,))


def swap(value, axis, mask=1):
    names = (axis,) if isinstance(axis, str) else axis
    size = math.prod(lax.axis_size(name) for name in names)
    return lax.ppermute(value, axis, [(i, i ^ mask) for i in range(size)])


def chip_swap(value, mask):
    return swap(value, ("x", "f"), mask % 2 * 2 + mask // 2)


def after(value, event):
    return lax.optimization_barrier((value, event))[0]


def share(own):
    far = [chip_swap(own, k) for k in reversed(range(1, TP))]
    return [own] + far[::-1]


def launch(kernel, name, outs, scalars, *args, scratch=(), flops=0):
    shapes = [jax.ShapeDtypeStruct(shape, kind) for shape, kind in outs]
    moved = sum(a.size * a.dtype.itemsize for a in args) + sum(math.prod(o.shape) * o.dtype.itemsize for o in shapes)
    return pl.pallas_call(
        kernel,
        name=name,
        out_shape=shapes,
        in_specs=[pl.BlockSpec(memory_space=pltpu.SMEM)] + [pl.BlockSpec(memory_space=pltpu.VMEM)] * len(args),
        out_specs=[pl.BlockSpec(memory_space=pltpu.VMEM)] * len(shapes),
        scratch_shapes=list(scratch),
        cost_estimate=pl.CostEstimate(flops=flops, bytes_accessed=moved, transcendentals=0),
        compiler_params=pltpu.CompilerParams(vmem_limit_bytes=56 * 1024 * 1024),
    )(scalars, *args)


def unit_rows(values):
    center = values - jnp.mean(values, -1, keepdims=True)
    scale = lax.rsqrt(jnp.mean(center * center, -1, keepdims=True) + EPS)
    return center * scale, scale


def interleave(shard):
    block = D // 2
    per = block // (TP * shard)
    row = lax.broadcasted_iota(jnp.int32, (block, block), 0)
    col = lax.broadcasted_iota(jnp.int32, (block, block), 1)
    chip, rest = lax.div(row, per * shard), lax.rem(row, per * shard)
    target = lax.div(rest, shard) * (TP * shard) + chip * shard + lax.rem(rest, shard)
    return (col == target).astype(bf16)


def first_pieces_kernel(where, w_qkv, w_proj, *refs):
    small, outs, (proj, lines, cols) = refs[:8], refs[8 : 8 + TP], refs[8 + TP :]
    p = where[1]
    shard = cols.shape[1]
    lines[...] = jnp.zeros_like(lines)
    at = 0
    for l in range(LAYERS):
        for item in small:
            for first in range(0, item.shape[1], shard):
                lines[at : at + 1, :shard] = item[l : l + 1, first : first + shard].astype(f32)
                at += 1
    columns = lines[...].T[:shard, :HD]
    for q in range(TP):
        parts = [w_qkv[0, :, j * D + q * PW : j * D + (q + 1) * PW].astype(f32) for j in range(3)]
        cols[q] = jnp.concatenate(parts + [columns], 1).astype(bf16)
        proj[q] = w_proj[0, :, q * PW : (q + 1) * PW]
    for k, out in enumerate(outs):
        out[...] = cols[jnp.bitwise_xor(p, k)]


def layer_pieces_kernel(where, w_fc, w_out, w_proj, w_qkv, *refs):
    outs, (cols,) = refs[:TP], refs[TP:]
    p = where[1]
    shard = w_proj.shape[1]
    block = D // 2
    order = interleave(shard)
    for l in range(LAYERS):
        fc = [dot(w_fc[l, :, b * block : (b + 1) * block], order, NT) for b in range(w_fc.shape[2] // block)]
        for q in range(TP):
            lanes = slice(q * block // TP, (q + 1) * block // TP)
            cols[q, :, l * D : (l + 1) * D] = jnp.concatenate([item[:, lanes] for item in fc], 1).astype(bf16)
    for q in range(TP):
        parts = [w_qkv[1, :, j * D + q * PW : j * D + (q + 1) * PW] for j in range(3)]
        cols[q, :, LAYERS * D :] = jnp.concatenate(parts + [jnp.zeros((shard, HD), bf16)], 1)
    for k, out in enumerate(outs):
        q = jnp.bitwise_xor(p, k)
        for l in range(LAYERS):
            out[:, 2 * l * D : (2 * l + 1) * D] = cols[q, :, l * D : (l + 1) * D]
            out[:, (2 * l + 1) * D : (2 * l + 2) * D] = w_out[l, q]
        out[:, 2 * LAYERS * D : (2 * LAYERS + 1) * D] = w_proj[1]
        out[:, (2 * LAYERS + 1) * D :] = cols[q, :, LAYERS * D :]


def arrange_first_kernel(sizes):
    def kernel(where, got, w_first, table, columns, blocks):
        h, p, c = where[0], where[1], where[2]
        devices, shard = w_first.shape[:2]
        groups = sizes["g"]
        columns[...] = jnp.zeros_like(columns)
        for d in range(devices):
            rest, fi = divmod(d, 2)
            rest, ci = divmod(rest, 2)
            rest, xi = divmod(rest, 2)
            hi, gi = divmod(rest, groups)
            copy = (jnp.bitwise_xor(c, ci) * sizes["h"] + jnp.bitwise_xor(h, hi)) * groups + gi
            one = got[copy * TP + jnp.bitwise_xor(p, 2 * fi + xi)].astype(f32)
            w_first[d] = one[:, : 3 * PW].astype(bf16)
            columns[d * shard : (d + 1) * shard, :HD] = one[:, 3 * PW : 3 * PW + HD]
            blocks[d] = one[:, 3 * PW : 3 * PW + HD]
        lines = columns[...].T
        per = PW // (2 * shard)
        for l in range(LAYERS):
            base = SLOTS * l
            table[8 * l : 8 * l + 6, :] = lines[base : base + 6]
            parts = []
            for first in (0, devices // 2):
                for j in range(per):
                    block = blocks[first + p * per + j]
                    parts += [block[:, base + 6 : base + 7], block[:, base + 7 : base + 8]]
                if first == 0:
                    parts.append(jnp.zeros((PW, 1), f32))
            parts.append(jnp.zeros((D - 3 * PW, 1), f32))
            bias = jnp.broadcast_to(jnp.concatenate(parts, 0), (D, 128)).T
            table[8 * l + 6 : 8 * l + 7, :] = bias[0:1]
            row = lines[base + 8 : base + 9]
            for q in range(1, TP):
                row = jnp.where(p == q, lines[base + 8 + q : base + 9 + q], row)
            table[8 * l + 7 : 8 * l + 8, :] = row

    return kernel


def by_core(c, own, oth, work):
    @pl.when(c == 0)
    def _():
        work((own, oth))

    @pl.when(c != 0)
    def _():
        work((oth, own))


def arrange_proj_kernel(sizes):
    def kernel(where, own, oth, out):
        h, p, c = where[0], where[1], where[2]

        def work(cores):
            for d in range(out.shape[0]):
                rest, fi = divmod(d, 2)
                rest, ci = divmod(rest, 2)
                rest, xi = divmod(rest, 2)
                hi, gi = divmod(rest, sizes["g"])
                k = jnp.bitwise_xor(p, 2 * fi + xi)
                place = (jnp.bitwise_xor(h, hi) * sizes["g"] + gi) * TP
                out[d] = jnp.concatenate([cores[ci][k, place + q] for q in range(TP)], 1)

        by_core(c, own, oth, work)

    return kernel


def finish_feed_kernel(where, *refs):
    pieces, (wf_out, wo_out, cols) = refs[:TP], refs[TP:]
    p = where[1]
    shard = wf_out.shape[1]
    block = D // 2
    order = interleave(shard)
    for l in range(LAYERS):
        for k in range(TP):
            cols[jnp.bitwise_xor(p, k)] = pieces[k][:, 2 * D * l : 2 * D * (l + 1)]
        fc = [cols[q, :, :D].astype(f32) for q in range(TP)]
        for b in range(wf_out.shape[2] // block):
            lanes = slice(b * block // TP, (b + 1) * block // TP)
            joined = jnp.concatenate([item[:, lanes] for item in fc], 1).astype(bf16)
            wf_out[l, :, b * block : (b + 1) * block] = dot(joined, order)
        for q in range(TP):
            wo_out[l, q] = cols[q, :, D:].astype(f32)


def finish_mixed_kernel(where, last, m0, m1, m2, m3, wq_out, wp_out, *refs):
    small_outs, (cols, square) = refs[:8], refs[8:]
    p = where[1]
    shard = wq_out.shape[1]
    columns = jnp.zeros((shard, 128), f32)
    for q in range(TP):
        total = jnp.zeros((shard, D + 128), f32)
        for copy in range(last.shape[0] // TP):
            total = total + last[(copy * 2 + q % 2) * 2 + q // 2].astype(f32)
        columns = columns + total[:, D:]
        cols[0, q] = total[:, :D]
    for k, m in enumerate((m0, m1, m2, m3)):
        cols[1, jnp.bitwise_xor(p, k)] = m[:, 2 * D * LAYERS :].astype(f32)
    for l in range(LAYERS):
        for j in range(3):
            wq_out[l, :, j * D : (j + 1) * D] = jnp.concatenate(
                [cols[l, q, :, j * PW : (j + 1) * PW] for q in range(TP)], 1
            )
        wp_out[l] = jnp.concatenate([cols[l, q, :, 3 * PW :] for q in range(TP)], 1)
    square[...] = jnp.zeros_like(square)
    square[:shard, :] = columns
    lines = square[...].T
    at = 0
    for l in range(LAYERS):
        for out in small_outs:
            for first in range(0, out.shape[1], shard):
                out[l : l + 1, first : first + shard] = lines[at : at + 1, :shard]
                at += 1


def enter_kernel(first, index):
    def kernel(where, table, *refs):
        if first:
            *inputs, wq, x_out, xo_out, n_out, q_out, kv_out, u_out = refs
        else:
            mid, *inputs, wq, x_out, xo_out, n_out, q_out, kv_out = refs
        t = table
        gain, shift, bias = (t[8 * index + i : 8 * index + i + 1, :] for i in (2, 3, 6))
        rows = n_out.shape[0] // TP
        for k in range(TP):
            at = slice(k * rows, (k + 1) * rows)
            x = inputs[k][...].astype(f32)
            if not first:
                x = mid[at, :] + x + t[8 * (index - 1) + 1 : 8 * (index - 1) + 2, :]
            x_out[at, :] = x
            if k == 0:
                xo_out[...] = x
            unit, _ = unit_rows(x)
            n_out[at, :] = (unit * gain + shift).astype(bf16)
            if first:
                u_out[at, :] = unit.astype(bf16)
        got = (dot(n_out[...], wq[...]) + bias[:, : 3 * PW]).astype(bf16)
        kv_out[...] = got[:, PW:]
        q_out[...] = got[:, :PW]

    return kernel


def tile_rows(p, t, size):
    return pl.multiple_of((jnp.bitwise_xor(t % TP, p) * 2 + t // TP) * size, size)


def mask_of(c, chunk, size):
    a = lax.broadcasted_iota(jnp.int32, (chunk, 2 * chunk), 0)
    b = lax.broadcasted_iota(jnp.int32, (chunk, 2 * chunk), 1)
    ahead = lax.div(b - chunk, size) < lax.div(a, size) + c
    return jnp.where(b < chunk, b - a, jnp.where(ahead, 0, 1)) <= 0


def by_position(p, count, q_ref, own_ref, oth_ref, qn, kc, vc):
    size = count // (2 * TP)
    for t in range(2 * TP):
        at = pl.ds(tile_rows(p, t, size), size)
        qn[t * size : (t + 1) * size, :] = q_ref[at, :]
        for source, first in ((own_ref, 0), (oth_ref, 2)):
            here = slice((t // 2 * 4 + first + t % 2) * size, (t // 2 * 4 + first + t % 2 + 1) * size)
            both = source[at, :]
            kc[here, :] = both[:, :PW]
            vc[here, :] = both[:, PW:]


def attend_kernel(where, q_ref, own_ref, oth_ref, out_ref, lse_ref, wide_ref, qn, kc, vc):
    p, c = where[1], where[2]
    count = q_ref.shape[0]
    size = count // (2 * TP)
    chunk = 2 * size
    by_position(p, count, q_ref, own_ref, oth_ref, qn, kc, vc)
    allowed = mask_of(c, chunk, size)
    for j in range(count // chunk):
        rows = slice(j * chunk, (j + 1) * chunk)
        past, last = slice(0, 2 * j * chunk), slice(2 * j * chunk, 2 * (j + 1) * chunk)
        outs = []
        for h in range(PH):
            lanes = slice(h * HD, (h + 1) * HD)
            q = qn[rows, lanes]
            scores = [jnp.where(allowed, dot(q, kc[last, lanes], NT) * 0.125, -1e30)]
            if j > 0:
                scores.append(dot(q, kc[past, lanes], NT) * 0.125)
            top = functools.reduce(jnp.maximum, [jnp.max(v, -1, keepdims=True) for v in scores])
            weights = [jnp.exp(v - top) for v in scores]
            total = sum(jnp.sum(v, -1, keepdims=True) for v in weights)
            out = dot(weights[0].astype(bf16), vc[last, lanes])
            if j > 0:
                out = out + dot(weights[1].astype(bf16), vc[past, lanes])
            outs.append(out / total)
            lse_ref[rows, h : h + 1] = top + jnp.log(total)
        out = jnp.concatenate(outs, 1)
        wide_ref[rows, :] = out
        low = out.astype(bf16)
        for t in (2 * j, 2 * j + 1):
            out_ref[pl.ds(tile_rows(p, t, size), size), :] = low[(t - 2 * j) * size : (t - 2 * j + 1) * size]


def middle_kernel(index):
    def kernel(where, table, o0, o1, o2, o3, wp, x, wf, wo, mid_out, mo_out, heads_out, n_out, slope_out, act_out, y0, y1, y2, y3, got):
        p = where[1]
        t = table
        b_proj, gain, shift, b_up = (t[8 * index + i : 8 * index + i + 1, :] for i in (0, 4, 5, 7))
        rows = x.shape[0] // TP
        for k, o in enumerate((o0, o1, o2, o3)):
            for m in range(TP):
                got[k, m * rows : (m + 1) * rows, :] = o[(m ^ k) * rows : ((m ^ k) + 1) * rows, :]
        heads_out[...] = jnp.concatenate([got[jnp.bitwise_xor(p, q)] for q in range(TP)], 1)
        for m, y in enumerate((y0, y1, y2, y3)):
            at = slice(m * rows, (m + 1) * rows)
            mid = x[at, :] + dot(heads_out[at, :], wp[...]) + b_proj
            mid_out[at, :] = mid
            if m == 0:
                mo_out[...] = mid
            unit, _ = unit_rows(mid)
            n_out[at, :] = (unit * gain + shift).astype(bf16)
        up = dot(n_out[...], wf[...]) + b_up
        square = up * up
        bent = jnp.tanh(ROOT * up * (1.0 + 0.044715 * square))
        half = 0.5 * (1.0 + bent)
        act_out[...] = (up * half).astype(bf16)
        slope_out[...] = (half + up * half * (1.0 - bent) * (ROOT * (1.0 + 3 * 0.044715 * square))).astype(bf16)
        for m, y in ((3, y3), (2, y2), (1, y1), (0, y0)):
            at = slice(m * rows, (m + 1) * rows)
            y[...] = dot(act_out[at, :], wo[...]).astype(y.dtype)

    return kernel


def part_sums(parts, values, acc):
    acc[...] = jnp.zeros(acc.shape, f32)
    rows = parts[0].shape[0]
    for k, part in enumerate(parts):
        unit, _ = unit_rows(values[k * rows : (k + 1) * rows, :])
        part = part[...].astype(f32)
        acc[0:1, :] += jnp.sum(part * unit, 0, keepdims=True)
        acc[1:2, :] += jnp.sum(part, 0, keepdims=True)


def feed_back_kernel(where, g0, g1, g2, g3, slope, wo, wf, g_out, gu_out, y0, y1, y2, y3):
    rows = g0.shape[0]
    for k, (g, y) in enumerate(((g0, y0), (g1, y1), (g2, y2), (g3, y3))):
        at = slice(k * rows, (k + 1) * rows)
        g_out[at, :] = g[...]
        g_up = (slope[at, :].astype(f32) * dot(g_out[at, :], wo[...], NT)).astype(bf16)
        gu_out[at, :] = g_up
        y[...] = dot(g_up, wf[...], NT).astype(y.dtype)


def norm_back_kernel(index, which):
    def kernel(where, value, grad, table, r0, r1, r2, r3, g_out, low_out, sum_out):
        gain = table[8 * index + which : 8 * index + which + 1, :]
        unit, scale = unit_rows(value[...])
        cot = r0[...] + r1[...].astype(f32) + r2[...].astype(f32) + r3[...].astype(f32)
        inner = cot * gain
        moved = scale * (
            inner - jnp.mean(inner, -1, keepdims=True) - unit * jnp.mean(inner * unit, -1, keepdims=True)
        )
        total = grad[...].astype(f32) + moved
        g_out[...] = total
        low = total.astype(bf16)
        low_out[...] = low
        sum_out[...] = jnp.zeros(sum_out.shape, f32)
        sum_out[0:1, :] = jnp.sum(low.astype(f32), 0, keepdims=True)

    return kernel


def attend_back_kernel(where, q_ref, own_ref, oth_ref, wide_ref, lse_ref, wp, g0, g1, g2, g3, ga_out, dq_ref, down_ref, doth_ref, local, gn, qn, kc, vc, dqn, dkc, dvc):
    p, c = where[1], where[2]
    count = q_ref.shape[0]
    size = count // (2 * TP)
    chunk = 2 * size
    rows_of = g0.shape[0]
    by_position(p, count, q_ref, own_ref, oth_ref, qn, kc, vc)
    for k, g in enumerate((g0, g1, g2, g3)):
        ga_out[k * rows_of : (k + 1) * rows_of, :] = g[...]
    mine = wp[pl.ds(pl.multiple_of(p * PW, PW), PW), :]
    local[...] = dot(ga_out[...], mine, NT)
    for t in range(2 * TP):
        gn[t * size : (t + 1) * size, :] = local[pl.ds(tile_rows(p, t, size), size), :].astype(bf16)
    product = gn[...].astype(f32) * wide_ref[...]
    delta = [jnp.sum(product[:, h * HD : (h + 1) * HD], -1, keepdims=True) for h in range(PH)]
    allowed = mask_of(c, chunk, size)
    dqn[...] = jnp.zeros_like(dqn)
    for b in range(count // chunk):
        rows, keys = slice(b * chunk, count), slice(2 * b * chunk, 2 * (b + 1) * chunk)
        dqs, dks, dvs = [], [], []
        for h in range(PH):
            lanes = slice(h * HD, (h + 1) * HD)
            q, g, k = qn[rows, lanes], gn[rows, lanes], kc[keys, lanes]
            scores = dot(q, k, NT) * 0.125 - lse_ref[rows, h : h + 1]
            first = jnp.where(allowed, scores[:chunk], -1e30)
            if b + 1 < count // chunk:
                first = jnp.concatenate([first, scores[chunk:]], 0)
            probs = jnp.exp(first)
            grad = dot(g, vc[keys, lanes], NT)
            ds = (probs * (grad - delta[h][b * chunk :])).astype(bf16)
            dqs.append(dot(ds, k))
            dks.append(dot(ds, q, TN))
            dvs.append(dot(probs.astype(bf16), g, TN))
        dqn[rows, :] += jnp.concatenate(dqs, 1)
        dkc[keys, :] = jnp.concatenate(dks, 1) * 0.125
        dvc[keys, :] = jnp.concatenate(dvs, 1)
    for t in range(2 * TP):
        at = pl.ds(tile_rows(p, t, size), size)
        for out, first in ((doth_ref, 2), (down_ref, 0)):
            here = slice((t // 2 * 4 + first + t % 2) * size, (t // 2 * 4 + first + t % 2 + 1) * size)
            out[at, :] = jnp.concatenate([dkc[here, :], dvc[here, :]], 1).astype(out.dtype)
        dq_ref[at, :] = (dqn[t * size : (t + 1) * size, :] * 0.125).astype(bf16)


def leave_kernel(where, dq, dkv, more, wq, gq_out, y0, y1, y2, y3):
    gq_out[:, :PW] = dq[...]
    gq_out[:, PW:] = (dkv[...] + more[...].astype(f32)).astype(bf16)
    rows = y0.shape[0]
    for k, y in ((3, y3), (2, y2), (1, y1), (0, y0)):
        y[...] = dot(gq_out[k * rows : (k + 1) * rows, :], wq[...], NT).astype(y.dtype)


def arrange_kernel(widths):
    def kernel(where, own, oth, *outs):
        p, c = where[1], where[2]

        def work(cores):
            for d in range(outs[0].shape[0]):
                rest, f = divmod(d, 2)
                rest, core = divmod(rest, 2)
                copy, x = divmod(rest, 2)
                block = copy * TP + jnp.bitwise_xor(2 * f + x, p)
                at = 0
                for out, width in zip(outs, widths):
                    out[d] = cores[core][block, :, at : at + width]
                    at += width

        by_core(c, own, oth, work)

    return kernel


def scatter_blocks(where, blocks, keep, give):
    p, c = where[1], where[2]
    for i in range(keep.shape[0]):
        copy, k = divmod(i, TP)
        chip = jnp.bitwise_xor(p, k)
        for out, core in ((keep, c), (give, 1 - c)):
            out[i] = blocks[((copy * 2 + lax.rem(chip, 2)) * 2 + core) * 2 + lax.div(chip, 2)]


def feed_weights_kernel(where, normed, g_up, act, g, mid, y0, y1, y2, y3, keep, give, b_out, sums, blocks):
    part_sums((y0, y1, y2, y3), mid, sums)
    sums[2:3, :] = jnp.sum(g[: y0.shape[0], :].astype(f32), 0, keepdims=True)
    b_out[...] = jnp.zeros(b_out.shape, f32)
    b_out[0:1, :] = jnp.sum(g_up[...].astype(f32), 0, keepdims=True)
    width = normed.shape[1]
    shard = keep.shape[1]
    for at, (a, b) in ((0, (normed, g_up)), (width, (act, g))):
        value = dot(a[...], b[...], TN)
        for d in range(blocks.shape[0]):
            blocks[d, :, at : at + width] = value[d * shard : (d + 1) * shard].astype(bf16)
    scatter_blocks(where, blocks, keep, give)


def mixed_weights(where, normed, g_qkv, heads, g_attn):
    p = where[1]
    value = dot(normed[...], g_qkv[...], TN)
    whole = dot(heads[...], g_attn[...], TN)
    mine = whole[:, :PW]
    for q in range(1, TP):
        mine = jnp.where(p == q, whole[:, q * PW : (q + 1) * PW], mine)
    return jnp.concatenate([value, mine], 1)


def mixed_weights_kernel(where, normed, g_qkv, heads, g_attn, x, y0, y1, y2, y3, keep, give, b_out, sums, blocks):
    part_sums((y0, y1, y2, y3), x, sums)
    b_out[...] = jnp.zeros(b_out.shape, f32)
    b_out[0:1, : 3 * PW] = jnp.sum(g_qkv[...].astype(f32), 0, keepdims=True)
    value = mixed_weights(where, normed, g_qkv, heads, g_attn)
    shard = blocks.shape[1]
    for d in range(blocks.shape[0]):
        blocks[d] = value[d * shard : (d + 1) * shard].astype(bf16)
    scatter_blocks(where, blocks, keep, give)


def leave_last_kernel(where, dq, dkv, more_keys, wq, unit, normed, heads, g_attn, *refs):
    sums, refs = refs[: 5 * LAYERS - 2], refs[5 * LAYERS - 2 :]
    keep, give, y0, y1, y2, y3, blocks, lines, more, g_qkv = refs
    leave_kernel(where, dq, dkv, more_keys, wq, g_qkv, y0, y1, y2, y3)
    part = jnp.concatenate([y[...].astype(f32) for y in (y0, y1, y2, y3)], 0)
    norm1_first = [jnp.sum(part * unit[...].astype(f32), 0, keepdims=True), jnp.sum(part, 0, keepdims=True)]
    b_qkv = jnp.sum(g_qkv[...].astype(f32), 0, keepdims=True)
    p, c = where[1], where[2]
    devices, shard = blocks.shape[:2]
    per = PW // (2 * shard)
    lines[...] = jnp.zeros_like(lines)
    more[...] = jnp.zeros_like(more)
    for l in range(LAYERS):
        b_proj, norm2, fc = sums[3 * l : 3 * l + 3]
        if l == 0:
            (gain, shift), qkv = norm1_first, jnp.concatenate([b_qkv, jnp.zeros((1, D - 3 * PW), f32)], 1)
        else:
            gain, shift, qkv = sums[6][0:1, :], sums[6][1:2, :], sums[7][0:1, :]
        base = SLOTS * l
        rows = (b_proj[0:1, :], norm2[2:3, :], gain, shift, norm2[0:1, :], norm2[1:2, :])
        for i, row in enumerate(rows):
            lines[base + i : base + i + 1, :] = row
        for q in range(TP):
            lines[base + 8 + q : base + 9 + q, :] = jnp.where(p == q, fc[0:1, :], 0.0)
        bias = jnp.broadcast_to(qkv, (128, D)).T
        for first, start in ((0, 0), (devices // 2, 2 * PW)):
            for j in range(2 * per):
                lane = base + 6 + j % 2
                more[first + p * per + j // 2, :, lane : lane + 1] = bias[
                    start + j * shard : start + (j + 1) * shard, 0:1
                ]
    columns = lines[...].T
    value = mixed_weights(where, normed, g_qkv, heads, g_attn)
    for d in range(devices):
        at = slice(d * shard, (d + 1) * shard)
        blocks[d] = jnp.concatenate([value[at], columns[at] + more[d]], 1).astype(bf16)
    for i in range(keep.shape[0]):
        rest, f = divmod(i, 2)
        keep[i] = blocks[(rest * 2 + c) * 2 + f]
        give[i] = blocks[(rest * 2 + 1 - c) * 2 + f]


def attend(q, keys_values, mask):
    k, v = keys_values[:, :PW], keys_values[:, PW:]
    q, k, v = (item.reshape(-1, PH, HD) for item in (q, k, v))
    scores = jnp.einsum("qhe,khe->hqk", q, k, preferred_element_type=f32) * 0.125
    scores = jnp.where(mask, scores, -1e30)
    top = jnp.max(scores, -1, keepdims=True)
    weights = jnp.exp(scores - top)
    total = jnp.sum(weights, -1, keepdims=True)
    out = jnp.einsum("hqk,khe->qhe", (weights / total).astype(bf16), v, preferred_element_type=f32)
    return out.reshape(-1, PW).astype(bf16), top + jnp.log(total)


def attend_back(q, keys_values, mask, log_total, grad_out):
    k, v = keys_values[:, :PW], keys_values[:, PW:]
    q, k, v, g = (item.reshape(-1, PH, HD) for item in (q, k, v, grad_out))
    scores = jnp.einsum("qhe,khe->hqk", q, k, preferred_element_type=f32) * 0.125
    probs = jnp.where(mask, jnp.exp(scores - log_total), 0.0)
    grad_probs = jnp.einsum("qhe,khe->hqk", g, v, preferred_element_type=f32)
    delta = jnp.sum(probs * grad_probs, -1, keepdims=True)
    grad_scores = (probs * (grad_probs - delta)).astype(bf16)
    dq = 0.125 * jnp.einsum("hqk,khe->qhe", grad_scores, k, preferred_element_type=f32)
    dk = 0.125 * jnp.einsum("hqk,qhe->khe", grad_scores, q, preferred_element_type=f32)
    dv = jnp.einsum("hqk,qhe->khe", probs.astype(bf16), g, preferred_element_type=f32)
    dkv = jnp.concatenate([dk.reshape(-1, PW), dv.reshape(-1, PW)], 1)
    return dq.reshape(-1, PW).astype(bf16), dkv


def body(tokens, w_qkv, b_qv, w_proj, b_proj, ln1_gain, ln1_bias, ln2_gain, ln2_bias, w_fc, b_fc, w_out, b_out, d_out):
    size = {name: lax.axis_size(name) for name in ALL}
    devices = math.prod(size.values())
    rows = tokens.shape[1]
    shard = w_qkv.shape[1]
    ff = w_fc.shape[2]
    h, g, x_at, c, f = (lax.axis_index(name) for name in ALL)
    p = 2 * f + x_at
    where = jnp.stack([h, p, c, g, f]).astype(jnp.int32)
    many = size["g"] > 1

    homes = [(a, b) for a in range(size["h"]) for b in range(size["f"])]
    outward = [
        [(a * 2 + b, (2 * ((a // 2 + turn) % 2) + b) * 2 + a % 2) for a, b in homes] for turn in range(2)
    ]

    def both_ways(value, low, moves):
        sent = [lax.dynamic_index_in_dim(value, i, 0, keepdims=False) for i in (low, 1 - low)]
        return [lax.ppermute(item, ("h", "f"), move) for item, move in zip(sent, moves)]

    def own_sequence(value):
        one, two = both_ways(value, h // 2, outward)
        both = jnp.where(h // 2 == 0, jnp.stack([one, two]), jnp.stack([two, one]))
        return [both[:, i].reshape(-1, D) for i in range(2)]

    def back_to_blocks(value):
        moves = [[(b, a) for a, b in move] for move in outward]
        one, two = both_ways(value.reshape(2, rows, -1), h // 2, moves)
        return jnp.where(h // 2 == 0, jnp.stack([one, two]), jnp.stack([two, one]))

    smalls = (b_proj, b_out, ln1_gain, ln1_bias, ln2_gain, ln2_bias, b_qv, b_fc)
    by_part = w_out.reshape(LAYERS, TP, shard, D)

    def plane(pieces):
        return jnp.stack([pieces[0]] + [chip_swap(pieces[k], k) for k in range(1, TP)])

    def fetch(pieces):
        return lax.all_gather(pieces, COPIES, axis=0, tiled=True)

    def arrange(own, *widths):
        return [
            item.reshape(D, -1)
            for item in launch(
                arrange_kernel(widths), "arrange", [((devices, shard, width), bf16) for width in widths],
                where, own, swap(own, "c"),
            )
        ]

    *first, proj = launch(
        first_pieces_kernel, "first_pieces",
        [((shard, 3 * PW + HD), bf16)] * TP + [((TP, shard, PW), bf16)], where, w_qkv, w_proj, *smalls,
        scratch=[pltpu.VMEM((128, 128), f32), pltpu.VMEM((TP, shard, 3 * PW + HD), bf16)],
    )
    feed = launch(
        layer_pieces_kernel, "layer_pieces", [((shard, (2 * LAYERS + 1) * D + 3 * PW + HD), bf16)] * TP,
        where, w_fc, by_part, w_proj, w_qkv, scratch=[pltpu.VMEM((TP, shard, LAYERS * D + 3 * PW + HD), bf16)],
    )
    x_own, g_low = own_sequence(jnp.stack([tokens, d_out], 1))
    feed, first, x_own, g_low = lax.optimization_barrier((feed, first, x_own, g_low))
    first, feed, x_own = lax.optimization_barrier((plane(first), feed, x_own))
    feed = [feed[0]] + [chip_swap(feed[k], k) for k in range(1, TP)]
    first = after(jnp.concatenate([first, proj], 2), feed[1])
    if many:
        first = lax.all_gather(first, "g", axis=0, tiled=True)
    first = jnp.concatenate([first] + [swap(first, "h", k) for k in range(1, size["h"])], 0)

    def part_of(start, stop):
        return jnp.stack([item[:, start:stop] for item in feed])

    next_feed, next_mixed = part_of(2 * D, 4 * D), part_of(4 * D, feed[0].shape[1])
    feed = part_of(0, 2 * D)
    x_pieces = share(after(x_own, feed))
    feed = fetch(feed)
    proj = after(first[:, :, 3 * PW + HD :], x_pieces)
    proj = [proj] + [chip_swap(proj, k) for k in range(1, TP)]
    first = jnp.concatenate([first, swap(first, "c")], 0)
    wq, table = launch(
        arrange_first_kernel(size), "arrange_first",
        [((devices, shard, 3 * PW), bf16), ((LAYERS * 8, D), f32)], where, first, flops=1 << 34,
        scratch=[pltpu.VMEM((D, 128), f32), pltpu.VMEM((devices, shard, HD), f32)],
    )
    wq = [wq.reshape(D, 3 * PW), None]
    wf, wo, wp = [None] * LAYERS, [None] * LAYERS, [None] * LAYERS
    count = TP * x_pieces[0].shape[0]
    own = count // TP
    if many:
        second = jnp.arange(2)[None, :, None]
        inside = jnp.arange(rows)[None, None, :]
        chip = p ^ jnp.arange(TP)[:, None, None]

        def positions(group, core):
            place = (chip // 2 + 2 * second) * size["g"] + group
            return (((place * 2 + chip % 2) * 2 + core) * rows + inside).reshape(-1)

        q_pos = positions(g, c)
        k_pos = jnp.concatenate([positions(gi, core) for gi in range(size["g"]) for core in (0, 1)])
        mask = (k_pos[None, :] <= q_pos[:, None])[None]

    def all_keys(kv, other):
        both = jnp.where(c == 0, jnp.stack([kv, other]), jnp.stack([other, kv])).reshape(-1, kv.shape[1])
        return lax.all_gather(both, "g", axis=0, tiled=True)

    saved = []
    state = tuple(x_pieces)
    for l in range(LAYERS):
        x, x_own, normed, q, kv, *unit = launch(
            enter_kernel(l == 0, l), f"enter_{l}",
            [((count, D), f32), ((own, D), f32), ((count, D), bf16), ((count, PW), bf16), ((count, 2 * PW), bf16)]
            + [((count, D), bf16)] * (l == 0),
            where, table, *state, wq[l], flops=2 * count * D * 3 * PW,
        )
        other = swap(kv, "c")
        if many:
            keys = all_keys(kv, other)
            out, lse = attend(q, keys, mask)
            wide = None
        else:
            keys = None
            out, lse, wide = launch(
                attend_kernel, f"attend_{l}", [((count, PW), bf16), ((count, PH), f32), ((count, PW), f32)],
                where, q, kv, other,
                scratch=[pltpu.VMEM((count, PW), bf16)] + [pltpu.VMEM((2 * count, PW), bf16)] * 2,
                flops=4 * count * 2 * count * PW,
            )
        if l == 0:
            next_mixed, next_feed = fetch(next_mixed), fetch(next_feed)
        if l == 0:
            out, proj = lax.optimization_barrier((out, proj))
        outs = share(out)
        if l == 0:
            proj = jnp.stack(proj)
            (proj,) = launch(
                arrange_proj_kernel(size), "arrange_proj", [((devices, shard, D), bf16)],
                where, proj, swap(proj, "c"),
            )
            prepared = *arrange(after(feed, out), D, D), proj.reshape(D, D)
        if l + 1 == LAYERS:
            pieces = share(after(g_low, outs[1]))
            prepared = *arrange(after(next_feed, out), D, D), prepared
        wf[l], wo[l], wp[l] = prepared
        mid, mid_own, heads, normed2, slope, act, y0, y1, y2, y3 = launch(
            middle_kernel(l), f"middle_{l}",
            [((count, D), f32), ((own, D), f32), ((count, D), bf16), ((count, D), bf16), ((count, D), bf16), ((count, D), bf16)]
            + [((own, D), f32)] + [((own, D), bf16)] * 3,
            where, table, *outs, wp[l], x, wf[l], wo[l],
            scratch=[pltpu.VMEM((TP, count, PW), bf16)], flops=6 * count * D * D,
        )
        if l + 1 < LAYERS:
            total = y0
            for k, y in ((1, y1), (2, y2), (3, y3)):
                total = total + chip_swap(y, k).astype(f32)
        saved.append((x, x_own, normed, q, kv, other, keys, lse, wide, heads, mid, mid_own, normed2, slope, act, unit))
        if l + 1 < LAYERS:
            next_mixed, total = lax.optimization_barrier((next_mixed, total))
            state = (mid, *share(total.astype(bf16)))
            prepared, wq[l + 1] = arrange(next_mixed, D, 3 * PW)
    last_parts = [y0, y1, y2, y3]

    copies = devices // (2 * TP)
    halves = [((copies * TP, shard, 2 * D), bf16)] * 2

    def reduce_copies(keep, got):
        total = (keep.astype(f32) + got.astype(f32)).astype(bf16)
        return lax.psum_scatter(total, COPIES, scatter_dimension=0, tiled=True)

    def by_owner(sums):
        return [sums[0]] + [chip_swap(sums[k], k) for k in range(1, TP)]

    line = ((8, D), f32)
    parts = [((own, D), f32)] + [((own, D), bf16)] * 3
    g_own = g_low
    sums = [None] * LAYERS
    for l in reversed(range(LAYERS)):
        x, x_own, normed, q, kv, other, keys, lse, wide, heads, mid, mid_own, normed2, slope, act, unit = saved[l]
        g_all, g_up, y0, y1, y2, y3 = launch(
            feed_back_kernel, f"feed_back_{l}", [((count, D), bf16), ((count, D), bf16)] + parts,
            where, *pieces, slope, wo[l], wf[l], flops=4 * count * D * D,
        )
        got = [chip_swap(y, k) for k, y in ((3, y3), (2, y2), (1, y1))][::-1]
        keep, give, b_fc_sum, norm2_sum = launch(
            feed_weights_kernel, f"feed_weights_{l}", halves + [line, line],
            where, normed2, g_up, act, g_all, mid, y0, y1, y2, y3,
            scratch=[pltpu.VMEM((devices, shard, 2 * D), bf16)], flops=4 * count * D * D,
        )
        if l + 1 == LAYERS:
            got, keep, give = lax.optimization_barrier((got, keep, give))
        else:
            got, keep, give, mixed, output = lax.optimization_barrier((got, keep, give, mixed, output))
        give = swap(give, "c")
        g_own, g_low, b_proj_sum = launch(
            norm_back_kernel(l, 4), f"norm2_back_{l}", [((own, D), f32), ((own, D), bf16), line],
            where, mid_own, g_own, table, y0, *got,
        )
        give, g_low = lax.optimization_barrier((give, g_low))
        feed = reduce_copies(keep, give)
        pieces = share(g_low)
        if l + 1 == LAYERS:
            last_parts, pieces[1] = lax.optimization_barrier((last_parts, pieces[1]))
            total = last_parts[0]
            for k in range(1, TP):
                total = total + chip_swap(last_parts[k], k).astype(f32)
            meanwhile = (mid_own + total + table[8 * l + 1 : 8 * l + 2]).astype(bf16)
        if many:
            g_attn = jnp.concatenate(pieces, 0)
            mine = lax.dynamic_slice_in_dim(wp[l], p * PW, PW, 0)
            dq, dkv = attend_back(q, keys, mask, lse, dot(g_attn, mine, NT).astype(bf16))
            dkv = lax.psum_scatter(dkv, "g", scatter_dimension=0, tiled=True).reshape(2, count, 2 * PW)
            dkv, give = (lax.dynamic_index_in_dim(dkv, i, 0, keepdims=False) for i in (c, 1 - c))
            give = give.astype(bf16)
        else:
            g_attn, dq, dkv, give = launch(
                attend_back_kernel, f"attend_back_{l}",
                [((count, D), bf16), ((count, PW), bf16), ((count, 2 * PW), f32), ((count, 2 * PW), bf16)],
                where, q, kv, other, wide, lse, wp[l], *pieces,
                scratch=[pltpu.VMEM((count, PW), f32), pltpu.VMEM((count, PW), bf16), pltpu.VMEM((count, PW), bf16)]
                + [pltpu.VMEM((2 * count, PW), bf16)] * 2 + [pltpu.VMEM((count, PW), f32)]
                + [pltpu.VMEM((2 * count, PW), f32)] * 2,
                flops=10 * count * 2 * count * PW,
            )
        more = swap(give, "c")
        if l > 0:
            more, output = lax.optimization_barrier((more, meanwhile))
            output = back_to_blocks(output)
        sums[l] = (b_proj_sum, norm2_sum, b_fc_sum)
        if l > 0:
            g_qkv, y0, y1, y2, y3 = launch(
                leave_kernel, f"leave_{l}", [((count, 3 * PW), bf16)] + parts,
                where, dq, dkv, more, wq[l], flops=2 * count * D * 3 * PW,
            )
            got = [chip_swap(y, k) for k, y in ((3, y3), (2, y2), (1, y1))][::-1]
            keep, give, b_qkv_sum, norm1_sum = launch(
                mixed_weights_kernel, f"mixed_weights_{l}", [((copies * TP, shard, D), bf16)] * 2 + [line, line],
                where, normed, g_qkv, heads, g_attn, x, y0, y1, y2, y3,
                scratch=[pltpu.VMEM((devices, shard, D), bf16)], flops=4 * count * D * D,
            )
            got, keep, give, feed_last = lax.optimization_barrier((got, keep, give, feed))
            give = swap(give, "c")
            sums[l] = sums[l] + (norm1_sum, b_qkv_sum)
        else:
            keep, give, y0, y1, y2, y3 = launch(
                leave_last_kernel, "leave_last", [((copies * TP, shard, D + 128), bf16)] * 2 + parts,
                where, dq, dkv, more, wq[l], *unit, normed, heads, g_attn, *sums[0], *sums[1],
                scratch=[pltpu.VMEM((devices, shard, D + 128), bf16), pltpu.VMEM((128, D), f32),
                         pltpu.VMEM((devices, shard, 128), f32), pltpu.VMEM((count, 3 * PW), bf16)],
                flops=6 * count * D * D,
            )
            give, feed = lax.optimization_barrier((give, feed))
            last = (keep.astype(f32) + swap(give, "c").astype(f32)).astype(bf16)
            got = [chip_swap(y, k) for k, y in ((3, y3), (2, y2), (1, y1))][::-1]
            last = after(last, got[0])
            reduced = by_owner(after(jnp.concatenate([feed, feed_last, mixed], 2), last))
            last = lax.all_to_all(last, ("h", "g", "x", "f"), 0, 0, tiled=True)
        g_own, g_low, _ = launch(
            norm_back_kernel(l, 2), f"norm1_back_{l}", [((own, D), f32), ((own, D), bf16), line],
            where, x_own, g_own, table, y0, *got,
        )
        if l > 0:
            give, g_low = lax.optimization_barrier((give, g_low))
            mixed = reduce_copies(keep, give)
            pieces = share(g_low)
    g_low, reduced[1] = lax.optimization_barrier((g_low, reduced[1]))
    grad_tokens = back_to_blocks(g_low).astype(f32)
    d_wf, d_wo = launch(
        finish_feed_kernel, "finish_feed", [((LAYERS, shard, ff), f32), ((LAYERS, TP, shard, D), f32)],
        where, *reduced,
        scratch=[pltpu.VMEM((TP, shard, 2 * D), bf16)],
    )
    d_wo = d_wo.reshape(w_out.shape)
    d_wq, d_wp, d_b_proj, d_b_out, d_g1, d_s1, d_g2, d_s2, d_b_qv, d_b_fc = launch(
        finish_mixed_kernel, "finish_mixed",
        [((LAYERS, shard, 3 * D), f32), ((LAYERS, shard, D), f32)] + [(item.shape, f32) for item in smalls],
        where, last, *reduced, scratch=[pltpu.VMEM((LAYERS, TP, shard, D), f32), pltpu.VMEM((128, 128), f32)],
    )
    return (output, grad_tokens, d_wq, d_b_qv, d_wp, d_b_proj, d_g1, d_s1, d_g2, d_s2, d_wf, d_b_fc, d_wo, d_b_out)


def solution(mesh):
    ctx, pair = mesh.shape["ctx"], mesh.shape["fsdp"]
    view = Mesh(mesh.devices.reshape(4, ctx // 16, 2, 2, pair), ALL)
    along = ("h", "g", "x", "c")
    token = P("f", along, None)
    matrix = P(None, ALL, None)
    line = P(None, ALL)
    in_specs = (token, matrix, line, matrix, line, line, line, line, line, matrix, line, matrix, line, token)
    out_specs = (token, token, matrix, line, matrix, line, line, line, line, line, matrix, line, matrix, line)
    return jax.shard_map(body, mesh=view, in_specs=in_specs, out_specs=out_specs, check_vma=False)
```

```python
import functools
import math

import jax
import jax.numpy as jnp
from jax import lax
from jax.experimental import pallas as pl
from jax.experimental.pallas import tpu as pltpu
from jax.sharding import Mesh, PartitionSpec as P

D = 768
H = 12
HD = 64
LAYERS = 2
TP = 4
PH = H // TP
PW = PH * HD
EPS = 1e-05
ROOT = math.sqrt(2.0 / math.pi)
bf16 = jnp.bfloat16
f32 = jnp.float32

ALL = ("h", "g", "x", "c", "f")
COPIES = ("h", "g")
SLOTS = 12


def dot(a, b, dims=((1,), (0,)), precision=None):
    return lax.dot_general(a, b, (dims, ((), ())), preferred_element_type=f32, precision=precision)


NT = ((1,), (1,))
TN = ((0,), (0,))


def swap(value, axis, mask=1):
    names = (axis,) if isinstance(axis, str) else axis
    size = math.prod(lax.axis_size(name) for name in names)
    return lax.ppermute(value, axis, [(i, i ^ mask) for i in range(size)])


def chip_swap(value, mask):
    return swap(value, ("x", "f"), mask % 2 * 2 + mask // 2)


def after(value, event):
    return lax.optimization_barrier((value, event))[0]


def share(own):
    far = [chip_swap(own, k) for k in reversed(range(1, TP))]
    return [own] + far[::-1]


def launch(kernel, name, outs, scalars, *args, scratch=(), flops=0):
    shapes = [jax.ShapeDtypeStruct(shape, kind) for shape, kind in outs]
    moved = sum(a.size * a.dtype.itemsize for a in args) + sum(math.prod(o.shape) * o.dtype.itemsize for o in shapes)
    return pl.pallas_call(
        kernel,
        name=name,
        out_shape=shapes,
        in_specs=[pl.BlockSpec(memory_space=pltpu.SMEM)] + [pl.BlockSpec(memory_space=pltpu.VMEM)] * len(args),
        out_specs=[pl.BlockSpec(memory_space=pltpu.VMEM)] * len(shapes),
        scratch_shapes=list(scratch),
        cost_estimate=pl.CostEstimate(flops=flops, bytes_accessed=moved, transcendentals=0),
        compiler_params=pltpu.CompilerParams(vmem_limit_bytes=56 * 1024 * 1024),
    )(scalars, *args)


def unit_rows(values):
    center = values - jnp.mean(values, -1, keepdims=True)
    scale = lax.rsqrt(jnp.mean(center * center, -1, keepdims=True) + EPS)
    return center * scale, scale


def interleave(shard):
    block = D // 2
    per = block // (TP * shard)
    row = lax.broadcasted_iota(jnp.int32, (block, block), 0)
    col = lax.broadcasted_iota(jnp.int32, (block, block), 1)
    chip, rest = lax.div(row, per * shard), lax.rem(row, per * shard)
    target = lax.div(rest, shard) * (TP * shard) + chip * shard + lax.rem(rest, shard)
    return (col == target).astype(bf16)


def first_pieces_kernel(where, w_qkv, w_proj, *refs):
    small, outs, (proj, lines, cols) = refs[:8], refs[8 : 8 + TP], refs[8 + TP :]
    p = where[1]
    shard = cols.shape[1]
    lines[...] = jnp.zeros_like(lines)
    at = 0
    for l in range(LAYERS):
        for item in small:
            for first in range(0, item.shape[1], shard):
                lines[at : at + 1, :shard] = item[l : l + 1, first : first + shard].astype(f32)
                at += 1
    columns = lines[...].T[:shard, :HD]
    for q in range(TP):
        parts = [w_qkv[0, :, j * D + q * PW : j * D + (q + 1) * PW].astype(f32) for j in range(3)]
        cols[q] = jnp.concatenate(parts + [columns], 1).astype(bf16)
        proj[q] = w_proj[0, :, q * PW : (q + 1) * PW]
    for k, out in enumerate(outs):
        out[...] = cols[jnp.bitwise_xor(p, k)]


def layer_pieces_kernel(where, w_fc, w_out, w_proj, w_qkv, *refs):
    outs, (cols,) = refs[:TP], refs[TP:]
    p = where[1]
    shard = w_proj.shape[1]
    block = D // 2
    order = interleave(shard)
    for l in range(LAYERS):
        fc = [dot(w_fc[l, :, b * block : (b + 1) * block], order, NT) for b in range(w_fc.shape[2] // block)]
        for q in range(TP):
            lanes = slice(q * block // TP, (q + 1) * block // TP)
            cols[q, :, l * D : (l + 1) * D] = jnp.concatenate([item[:, lanes] for item in fc], 1).astype(bf16)
    for q in range(TP):
        parts = [w_qkv[1, :, j * D + q * PW : j * D + (q + 1) * PW] for j in range(3)]
        cols[q, :, LAYERS * D :] = jnp.concatenate(parts + [jnp.zeros((shard, HD), bf16)], 1)
    for k, out in enumerate(outs):
        q = jnp.bitwise_xor(p, k)
        for l in range(LAYERS):
            out[:, 2 * l * D : (2 * l + 1) * D] = cols[q, :, l * D : (l + 1) * D]
            out[:, (2 * l + 1) * D : (2 * l + 2) * D] = w_out[l, q]
        out[:, 2 * LAYERS * D : (2 * LAYERS + 1) * D] = w_proj[1]
        out[:, (2 * LAYERS + 1) * D :] = cols[q, :, LAYERS * D :]


def arrange_first_kernel(sizes):
    def kernel(where, got, w_first, table, columns, blocks):
        h, p, c = where[0], where[1], where[2]
        devices, shard = w_first.shape[:2]
        groups = sizes["g"]
        columns[...] = jnp.zeros_like(columns)
        for d in range(devices):
            rest, fi = divmod(d, 2)
            rest, ci = divmod(rest, 2)
            rest, xi = divmod(rest, 2)
            hi, gi = divmod(rest, groups)
            copy = (jnp.bitwise_xor(c, ci) * sizes["h"] + jnp.bitwise_xor(h, hi)) * groups + gi
            one = got[copy * TP + jnp.bitwise_xor(p, 2 * fi + xi)].astype(f32)
            w_first[d] = one[:, : 3 * PW].astype(bf16)
            columns[d * shard : (d + 1) * shard, :HD] = one[:, 3 * PW : 3 * PW + HD]
            blocks[d] = one[:, 3 * PW : 3 * PW + HD]
        lines = columns[...].T
        per = PW // (2 * shard)
        for l in range(LAYERS):
            base = SLOTS * l
            table[8 * l : 8 * l + 6, :] = lines[base : base + 6]
            parts = []
            for first in (0, devices // 2):
                for j in range(per):
                    block = blocks[first + p * per + j]
                    parts += [block[:, base + 6 : base + 7], block[:, base + 7 : base + 8]]
                if first == 0:
                    parts.append(jnp.zeros((PW, 1), f32))
            parts.append(jnp.zeros((D - 3 * PW, 1), f32))
            bias = jnp.broadcast_to(jnp.concatenate(parts, 0), (D, 128)).T
            table[8 * l + 6 : 8 * l + 7, :] = bias[0:1]
            row = lines[base + 8 : base + 9]
            for q in range(1, TP):
                row = jnp.where(p == q, lines[base + 8 + q : base + 9 + q], row)
            table[8 * l + 7 : 8 * l + 8, :] = row

    return kernel


def by_core(c, own, oth, work):
    @pl.when(c == 0)
    def _():
        work((own, oth))

    @pl.when(c != 0)
    def _():
        work((oth, own))


def arrange_proj_kernel(sizes):
    def kernel(where, own, oth, out):
        h, p, c = where[0], where[1], where[2]

        def work(cores):
            for d in range(out.shape[0]):
                rest, fi = divmod(d, 2)
                rest, ci = divmod(rest, 2)
                rest, xi = divmod(rest, 2)
                hi, gi = divmod(rest, sizes["g"])
                k = jnp.bitwise_xor(p, 2 * fi + xi)
                place = (jnp.bitwise_xor(h, hi) * sizes["g"] + gi) * TP
                out[d] = jnp.concatenate([cores[ci][k, place + q] for q in range(TP)], 1)

        by_core(c, own, oth, work)

    return kernel


def finish_feed_kernel(where, *refs):
    pieces, (wf_out, wo_out, cols) = refs[:TP], refs[TP:]
    p = where[1]
    shard = wf_out.shape[1]
    block = D // 2
    order = interleave(shard)
    for l in range(LAYERS):
        for k in range(TP):
            cols[jnp.bitwise_xor(p, k)] = pieces[k][:, 2 * D * l : 2 * D * (l + 1)]
        fc = [cols[q, :, :D].astype(f32) for q in range(TP)]
        for b in range(wf_out.shape[2] // block):
            lanes = slice(b * block // TP, (b + 1) * block // TP)
            joined = jnp.concatenate([item[:, lanes] for item in fc], 1).astype(bf16)
            wf_out[l, :, b * block : (b + 1) * block] = dot(joined, order)
        for q in range(TP):
            wo_out[l, q] = cols[q, :, D:].astype(f32)


def finish_mixed_kernel(where, last, m0, m1, m2, m3, wq_out, wp_out, *refs):
    small_outs, (cols, square) = refs[:8], refs[8:]
    p = where[1]
    shard = wq_out.shape[1]
    columns = jnp.zeros((shard, 128), f32)
    for q in range(TP):
        total = jnp.zeros((shard, D + 128), f32)
        for copy in range(last.shape[0] // TP):
            total = total + last[(copy * 2 + q % 2) * 2 + q // 2].astype(f32)
        columns = columns + total[:, D:]
        cols[0, q] = total[:, :D]
    for k, m in enumerate((m0, m1, m2, m3)):
        cols[1, jnp.bitwise_xor(p, k)] = m[:, 2 * D * LAYERS :].astype(f32)
    for l in range(LAYERS):
        for j in range(3):
            wq_out[l, :, j * D : (j + 1) * D] = jnp.concatenate(
                [cols[l, q, :, j * PW : (j + 1) * PW] for q in range(TP)], 1
            )
        wp_out[l] = jnp.concatenate([cols[l, q, :, 3 * PW :] for q in range(TP)], 1)
    square[...] = jnp.zeros_like(square)
    square[:shard, :] = columns
    lines = square[...].T
    at = 0
    for l in range(LAYERS):
        for out in small_outs:
            for first in range(0, out.shape[1], shard):
                out[l : l + 1, first : first + shard] = lines[at : at + 1, :shard]
                at += 1


def enter_kernel(first, index):
    def kernel(where, table, *refs):
        if first:
            *inputs, wq, x_out, xo_out, n_out, q_out, kv_out, u_out = refs
        else:
            mid, *inputs, wq, x_out, xo_out, n_out, q_out, kv_out = refs
        t = table
        gain, shift, bias = (t[8 * index + i : 8 * index + i + 1, :] for i in (2, 3, 6))
        rows = n_out.shape[0] // TP
        for k in range(TP):
            at = slice(k * rows, (k + 1) * rows)
            x = inputs[k][...].astype(f32)
            if not first:
                x = mid[at, :] + x + t[8 * (index - 1) + 1 : 8 * (index - 1) + 2, :]
            x_out[at, :] = x
            if k == 0:
                xo_out[...] = x
            unit, _ = unit_rows(x)
            n_out[at, :] = (unit * gain + shift).astype(bf16)
            if first:
                u_out[at, :] = unit.astype(bf16)
        got = (dot(n_out[...], wq[...]) + bias[:, : 3 * PW]).astype(bf16)
        kv_out[...] = got[:, PW:]
        q_out[...] = got[:, :PW]

    return kernel


def tile_rows(p, t, size):
    return pl.multiple_of((jnp.bitwise_xor(t % TP, p) * 2 + t // TP) * size, size)


def mask_of(c, chunk, size):
    a = lax.broadcasted_iota(jnp.int32, (chunk, 2 * chunk), 0)
    b = lax.broadcasted_iota(jnp.int32, (chunk, 2 * chunk), 1)
    ahead = lax.div(b - chunk, size) < lax.div(a, size) + c
    return jnp.where(b < chunk, b - a, jnp.where(ahead, 0, 1)) <= 0


def by_position(p, count, q_ref, own_ref, oth_ref, qn, kc, vc):
    size = count // (2 * TP)
    for t in range(2 * TP):
        at = pl.ds(tile_rows(p, t, size), size)
        qn[t * size : (t + 1) * size, :] = q_ref[at, :]
        for source, first in ((own_ref, 0), (oth_ref, 2)):
            here = slice((t // 2 * 4 + first + t % 2) * size, (t // 2 * 4 + first + t % 2 + 1) * size)
            both = source[at, :]
            kc[here, :] = both[:, :PW]
            vc[here, :] = both[:, PW:]


def attend_kernel(where, q_ref, own_ref, oth_ref, out_ref, lse_ref, wide_ref, qn, kc, vc):
    p, c = where[1], where[2]
    count = q_ref.shape[0]
    size = count // (2 * TP)
    chunk = 2 * size
    by_position(p, count, q_ref, own_ref, oth_ref, qn, kc, vc)
    allowed = mask_of(c, chunk, size)
    for j in range(count // chunk):
        rows = slice(j * chunk, (j + 1) * chunk)
        past, last = slice(0, 2 * j * chunk), slice(2 * j * chunk, 2 * (j + 1) * chunk)
        outs = []
        for h in range(PH):
            lanes = slice(h * HD, (h + 1) * HD)
            q = qn[rows, lanes]
            scores = [jnp.where(allowed, dot(q, kc[last, lanes], NT) * 0.125, -1e30)]
            if j > 0:
                scores.append(dot(q, kc[past, lanes], NT) * 0.125)
            top = functools.reduce(jnp.maximum, [jnp.max(v, -1, keepdims=True) for v in scores])
            weights = [jnp.exp(v - top) for v in scores]
            total = sum(jnp.sum(v, -1, keepdims=True) for v in weights)
            out = dot(weights[0].astype(bf16), vc[last, lanes])
            if j > 0:
                out = out + dot(weights[1].astype(bf16), vc[past, lanes])
            outs.append(out / total)
            lse_ref[rows, h : h + 1] = top + jnp.log(total)
        out = jnp.concatenate(outs, 1)
        wide_ref[rows, :] = out
        low = out.astype(bf16)
        for t in (2 * j, 2 * j + 1):
            out_ref[pl.ds(tile_rows(p, t, size), size), :] = low[(t - 2 * j) * size : (t - 2 * j + 1) * size]


def middle_kernel(index):
    def kernel(where, table, o0, o1, o2, o3, wp, x, wf, wo, mid_out, mo_out, heads_out, n_out, slope_out, act_out, y0, y1, y2, y3, got):
        p = where[1]
        t = table
        b_proj, gain, shift, b_up = (t[8 * index + i : 8 * index + i + 1, :] for i in (0, 4, 5, 7))
        rows = x.shape[0] // TP
        for k, o in enumerate((o0, o1, o2, o3)):
            for m in range(TP):
                got[k, m * rows : (m + 1) * rows, :] = o[(m ^ k) * rows : ((m ^ k) + 1) * rows, :]
        heads_out[...] = jnp.concatenate([got[jnp.bitwise_xor(p, q)] for q in range(TP)], 1)
        for m, y in enumerate((y0, y1, y2, y3)):
            at = slice(m * rows, (m + 1) * rows)
            mid = x[at, :] + dot(heads_out[at, :], wp[...]) + b_proj
            mid_out[at, :] = mid
            if m == 0:
                mo_out[...] = mid
            unit, _ = unit_rows(mid)
            n_out[at, :] = (unit * gain + shift).astype(bf16)
        up = dot(n_out[...], wf[...]) + b_up
        square = up * up
        bent = jnp.tanh(ROOT * up * (1.0 + 0.044715 * square))
        half = 0.5 * (1.0 + bent)
        act_out[...] = (up * half).astype(bf16)
        slope_out[...] = (half + up * half * (1.0 - bent) * (ROOT * (1.0 + 3 * 0.044715 * square))).astype(bf16)
        for m, y in ((3, y3), (2, y2), (1, y1), (0, y0)):
            at = slice(m * rows, (m + 1) * rows)
            y[...] = dot(act_out[at, :], wo[...]).astype(y.dtype)

    return kernel


def part_sums(parts, values, acc):
    acc[...] = jnp.zeros(acc.shape, f32)
    rows = parts[0].shape[0]
    for k, part in enumerate(parts):
        unit, _ = unit_rows(values[k * rows : (k + 1) * rows, :])
        part = part[...].astype(f32)
        acc[0:1, :] += jnp.sum(part * unit, 0, keepdims=True)
        acc[1:2, :] += jnp.sum(part, 0, keepdims=True)


def feed_back_kernel(where, g0, g1, g2, g3, slope, wo, wf, gu_out, y0, y1, y2, y3):
    rows = g0.shape[0]
    for k, (g, y) in enumerate(((g0, y0), (g1, y1), (g2, y2), (g3, y3))):
        at = slice(k * rows, (k + 1) * rows)
        g_up = (slope[at, :].astype(f32) * dot(g[...], wo[...], NT)).astype(bf16)
        gu_out[at, :] = g_up
        y[...] = dot(g_up, wf[...], NT).astype(y.dtype)


def norm_back_kernel(index, which):
    def kernel(where, value, grad, table, r0, r1, r2, r3, g_out, low_out, sum_out):
        gain = table[8 * index + which : 8 * index + which + 1, :]
        unit, scale = unit_rows(value[...])
        cot = r0[...] + r1[...].astype(f32) + r2[...].astype(f32) + r3[...].astype(f32)
        inner = cot * gain
        moved = scale * (
            inner - jnp.mean(inner, -1, keepdims=True) - unit * jnp.mean(inner * unit, -1, keepdims=True)
        )
        total = grad[...].astype(f32) + moved
        g_out[...] = total
        low = total.astype(bf16)
        low_out[...] = low
        sum_out[...] = jnp.zeros(sum_out.shape, f32)
        sum_out[0:1, :] = jnp.sum(low.astype(f32), 0, keepdims=True)

    return kernel


def attend_back_kernel(where, q_ref, own_ref, oth_ref, wide_ref, lse_ref, wp, g0, g1, g2, g3, dq_ref, down_ref, doth_ref, local, gn, qn, kc, vc, dqn, dkc, dvc):
    p, c = where[1], where[2]
    count = q_ref.shape[0]
    size = count // (2 * TP)
    chunk = 2 * size
    rows_of = g0.shape[0]
    by_position(p, count, q_ref, own_ref, oth_ref, qn, kc, vc)
    mine = wp[pl.ds(pl.multiple_of(p * PW, PW), PW), :]
    for k, g in enumerate((g0, g1, g2, g3)):
        local[k * rows_of : (k + 1) * rows_of, :] = dot(g[...], mine, NT)
    for t in range(2 * TP):
        gn[t * size : (t + 1) * size, :] = local[pl.ds(tile_rows(p, t, size), size), :].astype(bf16)
    product = gn[...].astype(f32) * wide_ref[...]
    delta = [jnp.sum(product[:, h * HD : (h + 1) * HD], -1, keepdims=True) for h in range(PH)]
    allowed = mask_of(c, chunk, size)
    dqn[...] = jnp.zeros_like(dqn)
    for b in range(count // chunk):
        rows, keys = slice(b * chunk, count), slice(2 * b * chunk, 2 * (b + 1) * chunk)
        dqs, dks, dvs = [], [], []
        for h in range(PH):
            lanes = slice(h * HD, (h + 1) * HD)
            q, g, k = qn[rows, lanes], gn[rows, lanes], kc[keys, lanes]
            scores = dot(q, k, NT) * 0.125 - lse_ref[rows, h : h + 1]
            first = jnp.where(allowed, scores[:chunk], -1e30)
            if b + 1 < count // chunk:
                first = jnp.concatenate([first, scores[chunk:]], 0)
            probs = jnp.exp(first)
            grad = dot(g, vc[keys, lanes], NT)
            ds = (probs * (grad - delta[h][b * chunk :])).astype(bf16)
            dqs.append(dot(ds, k))
            dks.append(dot(ds, q, TN))
            dvs.append(dot(probs.astype(bf16), g, TN))
        dqn[rows, :] += jnp.concatenate(dqs, 1)
        dkc[keys, :] = jnp.concatenate(dks, 1) * 0.125
        dvc[keys, :] = jnp.concatenate(dvs, 1)
    for t in range(2 * TP):
        at = pl.ds(tile_rows(p, t, size), size)
        for out, first in ((doth_ref, 2), (down_ref, 0)):
            here = slice((t // 2 * 4 + first + t % 2) * size, (t // 2 * 4 + first + t % 2 + 1) * size)
            out[at, :] = jnp.concatenate([dkc[here, :], dvc[here, :]], 1).astype(out.dtype)
        dq_ref[at, :] = (dqn[t * size : (t + 1) * size, :] * 0.125).astype(bf16)


def leave_kernel(where, dq, dkv, more, wq, gq_out, y0, y1, y2, y3):
    gq_out[:, :PW] = dq[...]
    gq_out[:, PW:] = (dkv[...] + more[...].astype(f32)).astype(bf16)
    rows = y0.shape[0]
    for k, y in ((3, y3), (2, y2), (1, y1), (0, y0)):
        y[...] = dot(gq_out[k * rows : (k + 1) * rows, :], wq[...], NT).astype(y.dtype)


def arrange_kernel(widths):
    def kernel(where, own, oth, *outs):
        p, c = where[1], where[2]

        def work(cores):
            for d in range(outs[0].shape[0]):
                rest, f = divmod(d, 2)
                rest, core = divmod(rest, 2)
                copy, x = divmod(rest, 2)
                block = copy * TP + jnp.bitwise_xor(2 * f + x, p)
                at = 0
                for out, width in zip(outs, widths):
                    out[d] = cores[core][block, :, at : at + width]
                    at += width

        by_core(c, own, oth, work)

    return kernel


def scatter_blocks(where, blocks, keep, give):
    p, c = where[1], where[2]
    for i in range(keep.shape[0]):
        copy, k = divmod(i, TP)
        chip = jnp.bitwise_xor(p, k)
        for out, core in ((keep, c), (give, 1 - c)):
            out[i] = blocks[((copy * 2 + lax.rem(chip, 2)) * 2 + core) * 2 + lax.div(chip, 2)]


def feed_weights_kernel(where, normed, g_up, act, g0, g1, g2, g3, mid, y0, y1, y2, y3, keep, give, b_out, sums, blocks):
    part_sums((y0, y1, y2, y3), mid, sums)
    sums[2:3, :] = jnp.sum(g0[...].astype(f32), 0, keepdims=True)
    b_out[...] = jnp.zeros(b_out.shape, f32)
    b_out[0:1, :] = jnp.sum(g_up[...].astype(f32), 0, keepdims=True)
    width = normed.shape[1]
    shard = keep.shape[1]
    g = jnp.concatenate([g0[...], g1[...], g2[...], g3[...]], 0)
    for at, (a, b) in ((0, (normed, g_up[...])), (width, (act, g))):
        value = dot(a[...], b, TN)
        for d in range(blocks.shape[0]):
            blocks[d, :, at : at + width] = value[d * shard : (d + 1) * shard].astype(bf16)
    scatter_blocks(where, blocks, keep, give)


def mixed_weights(where, normed, g_qkv, heads, g_attn):
    p = where[1]
    value = dot(normed[...], g_qkv[...], TN)
    whole = dot(heads[...], jnp.concatenate([g[...] for g in g_attn], 0), TN)
    mine = whole[:, :PW]
    for q in range(1, TP):
        mine = jnp.where(p == q, whole[:, q * PW : (q + 1) * PW], mine)
    return jnp.concatenate([value, mine], 1)


def mixed_weights_kernel(where, normed, g_qkv, heads, g0, g1, g2, g3, x, y0, y1, y2, y3, keep, give, b_out, sums, blocks):
    part_sums((y0, y1, y2, y3), x, sums)
    b_out[...] = jnp.zeros(b_out.shape, f32)
    b_out[0:1, : 3 * PW] = jnp.sum(g_qkv[...].astype(f32), 0, keepdims=True)
    value = mixed_weights(where, normed, g_qkv, heads, (g0, g1, g2, g3))
    shard = blocks.shape[1]
    for d in range(blocks.shape[0]):
        blocks[d] = value[d * shard : (d + 1) * shard].astype(bf16)
    scatter_blocks(where, blocks, keep, give)


def leave_last_kernel(where, dq, dkv, more_keys, wq, unit, normed, heads, g0, g1, g2, g3, *refs):
    sums, refs = refs[: 5 * LAYERS - 2], refs[5 * LAYERS - 2 :]
    keep, give, y0, y1, y2, y3, blocks, lines, more, g_qkv = refs
    leave_kernel(where, dq, dkv, more_keys, wq, g_qkv, y0, y1, y2, y3)
    part = jnp.concatenate([y[...].astype(f32) for y in (y0, y1, y2, y3)], 0)
    norm1_first = [jnp.sum(part * unit[...].astype(f32), 0, keepdims=True), jnp.sum(part, 0, keepdims=True)]
    b_qkv = jnp.sum(g_qkv[...].astype(f32), 0, keepdims=True)
    p, c = where[1], where[2]
    devices, shard = blocks.shape[:2]
    per = PW // (2 * shard)
    lines[...] = jnp.zeros_like(lines)
    more[...] = jnp.zeros_like(more)
    for l in range(LAYERS):
        b_proj, norm2, fc = sums[3 * l : 3 * l + 3]
        if l == 0:
            (gain, shift), qkv = norm1_first, jnp.concatenate([b_qkv, jnp.zeros((1, D - 3 * PW), f32)], 1)
        else:
            gain, shift, qkv = sums[6][0:1, :], sums[6][1:2, :], sums[7][0:1, :]
        base = SLOTS * l
        rows = (b_proj[0:1, :], norm2[2:3, :], gain, shift, norm2[0:1, :], norm2[1:2, :])
        for i, row in enumerate(rows):
            lines[base + i : base + i + 1, :] = row
        for q in range(TP):
            lines[base + 8 + q : base + 9 + q, :] = jnp.where(p == q, fc[0:1, :], 0.0)
        bias = jnp.broadcast_to(qkv, (128, D)).T
        for first, start in ((0, 0), (devices // 2, 2 * PW)):
            for j in range(2 * per):
                lane = base + 6 + j % 2
                more[first + p * per + j // 2, :, lane : lane + 1] = bias[
                    start + j * shard : start + (j + 1) * shard, 0:1
                ]
    columns = lines[...].T
    value = mixed_weights(where, normed, g_qkv, heads, (g0, g1, g2, g3))
    for d in range(devices):
        at = slice(d * shard, (d + 1) * shard)
        blocks[d] = jnp.concatenate([value[at], columns[at] + more[d]], 1).astype(bf16)
    for i in range(keep.shape[0]):
        rest, f = divmod(i, 2)
        keep[i] = blocks[(rest * 2 + c) * 2 + f]
        give[i] = blocks[(rest * 2 + 1 - c) * 2 + f]


def attend(q, keys_values, mask):
    k, v = keys_values[:, :PW], keys_values[:, PW:]
    q, k, v = (item.reshape(-1, PH, HD) for item in (q, k, v))
    scores = jnp.einsum("qhe,khe->hqk", q, k, preferred_element_type=f32) * 0.125
    scores = jnp.where(mask, scores, -1e30)
    top = jnp.max(scores, -1, keepdims=True)
    weights = jnp.exp(scores - top)
    total = jnp.sum(weights, -1, keepdims=True)
    out = jnp.einsum("hqk,khe->qhe", (weights / total).astype(bf16), v, preferred_element_type=f32)
    return out.reshape(-1, PW).astype(bf16), top + jnp.log(total)


def attend_back(q, keys_values, mask, log_total, grad_out):
    k, v = keys_values[:, :PW], keys_values[:, PW:]
    q, k, v, g = (item.reshape(-1, PH, HD) for item in (q, k, v, grad_out))
    scores = jnp.einsum("qhe,khe->hqk", q, k, preferred_element_type=f32) * 0.125
    probs = jnp.where(mask, jnp.exp(scores - log_total), 0.0)
    grad_probs = jnp.einsum("qhe,khe->hqk", g, v, preferred_element_type=f32)
    delta = jnp.sum(probs * grad_probs, -1, keepdims=True)
    grad_scores = (probs * (grad_probs - delta)).astype(bf16)
    dq = 0.125 * jnp.einsum("hqk,khe->qhe", grad_scores, k, preferred_element_type=f32)
    dk = 0.125 * jnp.einsum("hqk,qhe->khe", grad_scores, q, preferred_element_type=f32)
    dv = jnp.einsum("hqk,qhe->khe", probs.astype(bf16), g, preferred_element_type=f32)
    dkv = jnp.concatenate([dk.reshape(-1, PW), dv.reshape(-1, PW)], 1)
    return dq.reshape(-1, PW).astype(bf16), dkv


def body(tokens, w_qkv, b_qv, w_proj, b_proj, ln1_gain, ln1_bias, ln2_gain, ln2_bias, w_fc, b_fc, w_out, b_out, d_out):
    size = {name: lax.axis_size(name) for name in ALL}
    devices = math.prod(size.values())
    rows = tokens.shape[1]
    shard = w_qkv.shape[1]
    ff = w_fc.shape[2]
    h, g, x_at, c, f = (lax.axis_index(name) for name in ALL)
    p = 2 * f + x_at
    where = jnp.stack([h, p, c, g, f]).astype(jnp.int32)
    many = size["g"] > 1

    homes = [(a, b) for a in range(size["h"]) for b in range(size["f"])]
    outward = [
        [(a * 2 + b, (2 * ((a // 2 + turn) % 2) + b) * 2 + a % 2) for a, b in homes] for turn in range(2)
    ]

    def both_ways(value, low, moves):
        sent = [lax.dynamic_index_in_dim(value, i, 0, keepdims=False) for i in (low, 1 - low)]
        return [lax.ppermute(item, ("h", "f"), move) for item, move in zip(sent, moves)]

    def own_sequence(value):
        one, two = both_ways(value, h // 2, outward)
        both = jnp.where(h // 2 == 0, jnp.stack([one, two]), jnp.stack([two, one]))
        return [both[:, i].reshape(-1, D) for i in range(2)]

    def back_to_blocks(value):
        moves = [[(b, a) for a, b in move] for move in outward]
        one, two = both_ways(value.reshape(2, rows, -1), h // 2, moves)
        return jnp.where(h // 2 == 0, jnp.stack([one, two]), jnp.stack([two, one]))

    smalls = (b_proj, b_out, ln1_gain, ln1_bias, ln2_gain, ln2_bias, b_qv, b_fc)
    by_part = w_out.reshape(LAYERS, TP, shard, D)

    def plane(pieces):
        return jnp.stack([pieces[0]] + [chip_swap(pieces[k], k) for k in range(1, TP)])

    def fetch(pieces):
        return lax.all_gather(pieces, COPIES, axis=0, tiled=True)

    def arrange(own, *widths):
        return [
            item.reshape(D, -1)
            for item in launch(
                arrange_kernel(widths), "arrange", [((devices, shard, width), bf16) for width in widths],
                where, own, swap(own, "c"),
            )
        ]

    *first, proj = launch(
        first_pieces_kernel, "first_pieces",
        [((shard, 3 * PW + HD), bf16)] * TP + [((TP, shard, PW), bf16)], where, w_qkv, w_proj, *smalls,
        scratch=[pltpu.VMEM((128, 128), f32), pltpu.VMEM((TP, shard, 3 * PW + HD), bf16)],
    )
    feed = launch(
        layer_pieces_kernel, "layer_pieces", [((shard, (2 * LAYERS + 1) * D + 3 * PW + HD), bf16)] * TP,
        where, w_fc, by_part, w_proj, w_qkv, scratch=[pltpu.VMEM((TP, shard, LAYERS * D + 3 * PW + HD), bf16)],
    )
    x_own, g_low = own_sequence(jnp.stack([tokens, d_out], 1))
    feed, first, x_own, g_low = lax.optimization_barrier((feed, first, x_own, g_low))
    first, feed, x_own = lax.optimization_barrier((plane(first), feed, x_own))
    feed = [feed[0]] + [chip_swap(feed[k], k) for k in range(1, TP)]
    first = after(jnp.concatenate([first, proj], 2), feed[1])
    if many:
        first = lax.all_gather(first, "g", axis=0, tiled=True)
    first = jnp.concatenate([first] + [swap(first, "h", k) for k in range(1, size["h"])], 0)

    def part_of(start, stop):
        return jnp.stack([item[:, start:stop] for item in feed])

    next_feed, next_mixed = part_of(2 * D, 4 * D), part_of(4 * D, feed[0].shape[1])
    feed = part_of(0, 2 * D)
    x_pieces = share(after(x_own, feed))
    feed = fetch(feed)
    proj = after(first[:, :, 3 * PW + HD :], x_pieces)
    proj = [proj] + [chip_swap(proj, k) for k in range(1, TP)]
    first = jnp.concatenate([first, swap(first, "c")], 0)
    wq, table = launch(
        arrange_first_kernel(size), "arrange_first",
        [((devices, shard, 3 * PW), bf16), ((LAYERS * 8, D), f32)], where, first, flops=1 << 34,
        scratch=[pltpu.VMEM((D, 128), f32), pltpu.VMEM((devices, shard, HD), f32)],
    )
    wq = [wq.reshape(D, 3 * PW), None]
    wf, wo, wp = [None] * LAYERS, [None] * LAYERS, [None] * LAYERS
    count = TP * x_pieces[0].shape[0]
    own = count // TP
    if many:
        second = jnp.arange(2)[None, :, None]
        inside = jnp.arange(rows)[None, None, :]
        chip = p ^ jnp.arange(TP)[:, None, None]

        def positions(group, core):
            place = (chip // 2 + 2 * second) * size["g"] + group
            return (((place * 2 + chip % 2) * 2 + core) * rows + inside).reshape(-1)

        q_pos = positions(g, c)
        k_pos = jnp.concatenate([positions(gi, core) for gi in range(size["g"]) for core in (0, 1)])
        mask = (k_pos[None, :] <= q_pos[:, None])[None]

    def all_keys(kv, other):
        both = jnp.where(c == 0, jnp.stack([kv, other]), jnp.stack([other, kv])).reshape(-1, kv.shape[1])
        return lax.all_gather(both, "g", axis=0, tiled=True)

    saved = []
    state = tuple(x_pieces)
    for l in range(LAYERS):
        x, x_own, normed, q, kv, *unit = launch(
            enter_kernel(l == 0, l), f"enter_{l}",
            [((count, D), f32), ((own, D), f32), ((count, D), bf16), ((count, PW), bf16), ((count, 2 * PW), bf16)]
            + [((count, D), bf16)] * (l == 0),
            where, table, *state, wq[l], flops=2 * count * D * 3 * PW,
        )
        other = swap(kv, "c")
        if many:
            keys = all_keys(kv, other)
            out, lse = attend(q, keys, mask)
            wide = None
        else:
            keys = None
            out, lse, wide = launch(
                attend_kernel, f"attend_{l}", [((count, PW), bf16), ((count, PH), f32), ((count, PW), f32)],
                where, q, kv, other,
                scratch=[pltpu.VMEM((count, PW), bf16)] + [pltpu.VMEM((2 * count, PW), bf16)] * 2,
                flops=4 * count * 2 * count * PW,
            )
        if l == 0:
            next_mixed, next_feed = fetch(next_mixed), fetch(next_feed)
        if l == 0:
            out, proj = lax.optimization_barrier((out, proj))
        outs = share(out)
        if l == 0:
            proj = jnp.stack(proj)
            (proj,) = launch(
                arrange_proj_kernel(size), "arrange_proj", [((devices, shard, D), bf16)],
                where, proj, swap(proj, "c"),
            )
            prepared = *arrange(after(feed, out), D, D), proj.reshape(D, D)
        if l + 1 == LAYERS:
            pieces = share(after(g_low, outs[1]))
            prepared = *arrange(after(next_feed, out), D, D), prepared
        wf[l], wo[l], wp[l] = prepared
        mid, mid_own, heads, normed2, slope, act, y0, y1, y2, y3 = launch(
            middle_kernel(l), f"middle_{l}",
            [((count, D), f32), ((own, D), f32), ((count, D), bf16), ((count, D), bf16), ((count, D), bf16), ((count, D), bf16)]
            + [((own, D), f32)] + [((own, D), bf16)] * 3,
            where, table, *outs, wp[l], x, wf[l], wo[l],
            scratch=[pltpu.VMEM((TP, count, PW), bf16)], flops=6 * count * D * D,
        )
        if l + 1 < LAYERS:
            total = y0
            for k, y in ((1, y1), (2, y2), (3, y3)):
                total = total + chip_swap(y, k).astype(f32)
        saved.append((x, x_own, normed, q, kv, other, keys, lse, wide, heads, mid, mid_own, normed2, slope, act, unit))
        if l + 1 < LAYERS:
            next_mixed, total = lax.optimization_barrier((next_mixed, total))
            state = (mid, *share(total.astype(bf16)))
            prepared, wq[l + 1] = arrange(next_mixed, D, 3 * PW)
    last_parts = [y0, y1, y2, y3]

    copies = devices // (2 * TP)
    halves = [((copies * TP, shard, 2 * D), bf16)] * 2

    def reduce_copies(keep, got):
        total = (keep.astype(f32) + got.astype(f32)).astype(bf16)
        return lax.psum_scatter(total, COPIES, scatter_dimension=0, tiled=True)

    def by_owner(sums):
        return [sums[0]] + [chip_swap(sums[k], k) for k in range(1, TP)]

    line = ((8, D), f32)
    parts = [((own, D), f32)] + [((own, D), bf16)] * 3
    g_own = g_low
    sums = [None] * LAYERS
    for l in reversed(range(LAYERS)):
        x, x_own, normed, q, kv, other, keys, lse, wide, heads, mid, mid_own, normed2, slope, act, unit = saved[l]
        g_up, y0, y1, y2, y3 = launch(
            feed_back_kernel, f"feed_back_{l}", [((count, D), bf16)] + parts,
            where, *pieces, slope, wo[l], wf[l], flops=4 * count * D * D,
        )
        got = [chip_swap(y, k) for k, y in ((3, y3), (2, y2), (1, y1))][::-1]
        keep, give, b_fc_sum, norm2_sum = launch(
            feed_weights_kernel, f"feed_weights_{l}", halves + [line, line],
            where, normed2, g_up, act, *pieces, mid, y0, y1, y2, y3,
            scratch=[pltpu.VMEM((devices, shard, 2 * D), bf16)], flops=4 * count * D * D,
        )
        if l + 1 == LAYERS:
            got, keep, give = lax.optimization_barrier((got, keep, give))
        else:
            got, keep, give, mixed, output = lax.optimization_barrier((got, keep, give, mixed, output))
        give = swap(give, "c")
        g_own, g_low, b_proj_sum = launch(
            norm_back_kernel(l, 4), f"norm2_back_{l}", [((own, D), f32), ((own, D), bf16), line],
            where, mid_own, g_own, table, y0, *got,
        )
        give, g_low = lax.optimization_barrier((give, g_low))
        feed = reduce_copies(keep, give)
        pieces = share(g_low)
        if l + 1 == LAYERS:
            last_parts, pieces[1] = lax.optimization_barrier((last_parts, pieces[1]))
            total = last_parts[0]
            for k in range(1, TP):
                total = total + chip_swap(last_parts[k], k).astype(f32)
            meanwhile = (mid_own + total + table[8 * l + 1 : 8 * l + 2]).astype(bf16)
        if many:
            g_attn = jnp.concatenate(pieces, 0)
            mine = lax.dynamic_slice_in_dim(wp[l], p * PW, PW, 0)
            dq, dkv = attend_back(q, keys, mask, lse, dot(g_attn, mine, NT).astype(bf16))
            dkv = lax.psum_scatter(dkv, "g", scatter_dimension=0, tiled=True).reshape(2, count, 2 * PW)
            dkv, give = (lax.dynamic_index_in_dim(dkv, i, 0, keepdims=False) for i in (c, 1 - c))
            give = give.astype(bf16)
        else:
            dq, dkv, give = launch(
                attend_back_kernel, f"attend_back_{l}",
                [((count, PW), bf16), ((count, 2 * PW), f32), ((count, 2 * PW), bf16)],
                where, q, kv, other, wide, lse, wp[l], *pieces,
                scratch=[pltpu.VMEM((count, PW), f32), pltpu.VMEM((count, PW), bf16), pltpu.VMEM((count, PW), bf16)]
                + [pltpu.VMEM((2 * count, PW), bf16)] * 2 + [pltpu.VMEM((count, PW), f32)]
                + [pltpu.VMEM((2 * count, PW), f32)] * 2,
                flops=10 * count * 2 * count * PW,
            )
        more = swap(give, "c")
        if l > 0:
            more, output = lax.optimization_barrier((more, meanwhile))
            output = back_to_blocks(output)
        sums[l] = (b_proj_sum, norm2_sum, b_fc_sum)
        if l > 0:
            g_qkv, y0, y1, y2, y3 = launch(
                leave_kernel, f"leave_{l}", [((count, 3 * PW), bf16)] + parts,
                where, dq, dkv, more, wq[l], flops=2 * count * D * 3 * PW,
            )
            got = [chip_swap(y, k) for k, y in ((3, y3), (2, y2), (1, y1))][::-1]
            keep, give, b_qkv_sum, norm1_sum = launch(
                mixed_weights_kernel, f"mixed_weights_{l}", [((copies * TP, shard, D), bf16)] * 2 + [line, line],
                where, normed, g_qkv, heads, *pieces, x, y0, y1, y2, y3,
                scratch=[pltpu.VMEM((devices, shard, D), bf16)], flops=4 * count * D * D,
            )
            got, keep, give, feed_last = lax.optimization_barrier((got, keep, give, feed))
            give = swap(give, "c")
            sums[l] = sums[l] + (norm1_sum, b_qkv_sum)
        else:
            keep, give, y0, y1, y2, y3 = launch(
                leave_last_kernel, "leave_last", [((copies * TP, shard, D + 128), bf16)] * 2 + parts,
                where, dq, dkv, more, wq[l], *unit, normed, heads, *pieces, *sums[0], *sums[1],
                scratch=[pltpu.VMEM((devices, shard, D + 128), bf16), pltpu.VMEM((128, D), f32),
                         pltpu.VMEM((devices, shard, 128), f32), pltpu.VMEM((count, 3 * PW), bf16)],
                flops=6 * count * D * D,
            )
            give, feed = lax.optimization_barrier((give, feed))
            last = (keep.astype(f32) + swap(give, "c").astype(f32)).astype(bf16)
            got = [chip_swap(y, k) for k, y in ((3, y3), (2, y2), (1, y1))][::-1]
            last = after(last, got[0])
            reduced = by_owner(after(jnp.concatenate([feed, feed_last, mixed], 2), last))
            last = lax.all_to_all(last, ("h", "g", "x", "f"), 0, 0, tiled=True)
        g_own, g_low, _ = launch(
            norm_back_kernel(l, 2), f"norm1_back_{l}", [((own, D), f32), ((own, D), bf16), line],
            where, x_own, g_own, table, y0, *got,
        )
        if l > 0:
            give, g_low = lax.optimization_barrier((give, g_low))
            mixed = reduce_copies(keep, give)
            pieces = share(g_low)
    g_low, reduced[1] = lax.optimization_barrier((g_low, reduced[1]))
    grad_tokens = back_to_blocks(g_low).astype(f32)
    d_wf, d_wo = launch(
        finish_feed_kernel, "finish_feed", [((LAYERS, shard, ff), f32), ((LAYERS, TP, shard, D), f32)],
        where, *reduced,
        scratch=[pltpu.VMEM((TP, shard, 2 * D), bf16)],
    )
    d_wo = d_wo.reshape(w_out.shape)
    d_wq, d_wp, d_b_proj, d_b_out, d_g1, d_s1, d_g2, d_s2, d_b_qv, d_b_fc = launch(
        finish_mixed_kernel, "finish_mixed",
        [((LAYERS, shard, 3 * D), f32), ((LAYERS, shard, D), f32)] + [(item.shape, f32) for item in smalls],
        where, last, *reduced, scratch=[pltpu.VMEM((LAYERS, TP, shard, D), f32), pltpu.VMEM((128, 128), f32)],
    )
    return (output, grad_tokens, d_wq, d_b_qv, d_wp, d_b_proj, d_g1, d_s1, d_g2, d_s2, d_wf, d_b_fc, d_wo, d_b_out)


def solution(mesh):
    ctx, pair = mesh.shape["ctx"], mesh.shape["fsdp"]
    view = Mesh(mesh.devices.reshape(4, ctx // 16, 2, 2, pair), ALL)
    along = ("h", "g", "x", "c")
    token = P("f", along, None)
    matrix = P(None, ALL, None)
    line = P(None, ALL)
    in_specs = (token, matrix, line, matrix, line, line, line, line, line, matrix, line, matrix, line, token)
    out_specs = (token, token, matrix, line, matrix, line, line, line, line, line, matrix, line, matrix, line)
    return jax.shard_map(body, mesh=view, in_specs=in_specs, out_specs=out_specs, check_vma=False)
```

```python
import functools
import math

import jax
import jax.numpy as jnp
from jax import lax
from jax.experimental import pallas as pl
from jax.experimental.pallas import tpu as pltpu
from jax.sharding import Mesh, PartitionSpec as P

D = 768
H = 12
HD = 64
LAYERS = 2
TP = 4
PH = H // TP
PW = PH * HD
EPS = 1e-05
ROOT = math.sqrt(2.0 / math.pi)
bf16 = jnp.bfloat16
f32 = jnp.float32

ALL = ("h", "g", "x", "c", "f")
COPIES = ("h", "g")
SLOTS = 12


def dot(a, b, dims=((1,), (0,)), precision=None):
    return lax.dot_general(a, b, (dims, ((), ())), preferred_element_type=f32, precision=precision)


NT = ((1,), (1,))
TN = ((0,), (0,))


def swap(value, axis, mask=1):
    names = (axis,) if isinstance(axis, str) else axis
    size = math.prod(lax.axis_size(name) for name in names)
    return lax.ppermute(value, axis, [(i, i ^ mask) for i in range(size)])


def chip_swap(value, mask):
    return swap(value, ("x", "f"), mask % 2 * 2 + mask // 2)


def after(value, event):
    return lax.optimization_barrier((value, event))[0]


def share(own):
    far = [chip_swap(own, k) for k in reversed(range(1, TP))]
    return [own] + far[::-1]


def launch(kernel, name, outs, scalars, *args, scratch=(), flops=0):
    shapes = [jax.ShapeDtypeStruct(shape, kind) for shape, kind in outs]
    moved = sum(a.size * a.dtype.itemsize for a in args) + sum(math.prod(o.shape) * o.dtype.itemsize for o in shapes)
    return pl.pallas_call(
        kernel,
        name=name,
        out_shape=shapes,
        in_specs=[pl.BlockSpec(memory_space=pltpu.SMEM)] + [pl.BlockSpec(memory_space=pltpu.VMEM)] * len(args),
        out_specs=[pl.BlockSpec(memory_space=pltpu.VMEM)] * len(shapes),
        scratch_shapes=list(scratch),
        cost_estimate=pl.CostEstimate(flops=flops, bytes_accessed=moved, transcendentals=0),
        compiler_params=pltpu.CompilerParams(vmem_limit_bytes=56 * 1024 * 1024),
    )(scalars, *args)


def unit_rows(values):
    center = values - jnp.mean(values, -1, keepdims=True)
    scale = lax.rsqrt(jnp.mean(center * center, -1, keepdims=True) + EPS)
    return center * scale, scale


def interleave(shard):
    block = D // 2
    per = block // (TP * shard)
    row = lax.broadcasted_iota(jnp.int32, (block, block), 0)
    col = lax.broadcasted_iota(jnp.int32, (block, block), 1)
    chip, rest = lax.div(row, per * shard), lax.rem(row, per * shard)
    target = lax.div(rest, shard) * (TP * shard) + chip * shard + lax.rem(rest, shard)
    return (col == target).astype(bf16)


def first_pieces_kernel(where, w_qkv, w_proj, *refs):
    small, outs, (proj, lines, cols) = refs[:8], refs[8 : 8 + TP], refs[8 + TP :]
    p = where[1]
    shard = cols.shape[1]
    lines[...] = jnp.zeros_like(lines)
    at = 0
    for l in range(LAYERS):
        for item in small:
            for first in range(0, item.shape[1], shard):
                lines[at : at + 1, :shard] = item[l : l + 1, first : first + shard].astype(f32)
                at += 1
    columns = lines[...].T[:shard, :HD]
    for q in range(TP):
        parts = [w_qkv[0, :, j * D + q * PW : j * D + (q + 1) * PW].astype(f32) for j in range(3)]
        cols[q] = jnp.concatenate(parts + [columns], 1).astype(bf16)
        proj[q] = w_proj[0, :, q * PW : (q + 1) * PW]
    for k, out in enumerate(outs):
        out[...] = cols[jnp.bitwise_xor(p, k)]


def layer_pieces_kernel(where, w_fc, w_out, w_proj, w_qkv, *refs):
    outs, (cols,) = refs[:TP], refs[TP:]
    p = where[1]
    shard = w_proj.shape[1]
    block = D // 2
    order = interleave(shard)
    for l in range(LAYERS):
        fc = [dot(w_fc[l, :, b * block : (b + 1) * block], order, NT) for b in range(w_fc.shape[2] // block)]
        for q in range(TP):
            lanes = slice(q * block // TP, (q + 1) * block // TP)
            cols[q, :, l * D : (l + 1) * D] = jnp.concatenate([item[:, lanes] for item in fc], 1).astype(bf16)
    for q in range(TP):
        parts = [w_qkv[1, :, j * D + q * PW : j * D + (q + 1) * PW] for j in range(3)]
        cols[q, :, LAYERS * D :] = jnp.concatenate(parts + [jnp.zeros((shard, HD), bf16)], 1)
    for k, out in enumerate(outs):
        q = jnp.bitwise_xor(p, k)
        for l in range(LAYERS):
            out[:, 2 * l * D : (2 * l + 1) * D] = cols[q, :, l * D : (l + 1) * D]
            out[:, (2 * l + 1) * D : (2 * l + 2) * D] = w_out[l, q]
        out[:, 2 * LAYERS * D : (2 * LAYERS + 1) * D] = w_proj[1]
        out[:, (2 * LAYERS + 1) * D :] = cols[q, :, LAYERS * D :]


def arrange_first_kernel(sizes):
    def kernel(where, got, w_first, table, columns, blocks):
        h, p, c = where[0], where[1], where[2]
        devices, shard = w_first.shape[:2]
        groups = sizes["g"]
        columns[...] = jnp.zeros_like(columns)
        for d in range(devices):
            rest, fi = divmod(d, 2)
            rest, ci = divmod(rest, 2)
            rest, xi = divmod(rest, 2)
            hi, gi = divmod(rest, groups)
            copy = (jnp.bitwise_xor(c, ci) * sizes["h"] + jnp.bitwise_xor(h, hi)) * groups + gi
            one = got[copy * TP + jnp.bitwise_xor(p, 2 * fi + xi)].astype(f32)
            w_first[d] = one[:, : 3 * PW].astype(bf16)
            columns[d * shard : (d + 1) * shard, :HD] = one[:, 3 * PW : 3 * PW + HD]
            blocks[d] = one[:, 3 * PW : 3 * PW + HD]
        lines = columns[...].T
        per = PW // (2 * shard)
        for l in range(LAYERS):
            base = SLOTS * l
            table[8 * l : 8 * l + 6, :] = lines[base : base + 6]
            parts = []
            for first in (0, devices // 2):
                for j in range(per):
                    block = blocks[first + p * per + j]
                    parts += [block[:, base + 6 : base + 7], block[:, base + 7 : base + 8]]
                if first == 0:
                    parts.append(jnp.zeros((PW, 1), f32))
            parts.append(jnp.zeros((D - 3 * PW, 1), f32))
            bias = jnp.broadcast_to(jnp.concatenate(parts, 0), (D, 128)).T
            table[8 * l + 6 : 8 * l + 7, :] = bias[0:1]
            row = lines[base + 8 : base + 9]
            for q in range(1, TP):
                row = jnp.where(p == q, lines[base + 8 + q : base + 9 + q], row)
            table[8 * l + 7 : 8 * l + 8, :] = row

    return kernel


def by_core(c, own, oth, work):
    @pl.when(c == 0)
    def _():
        work((own, oth))

    @pl.when(c != 0)
    def _():
        work((oth, own))


def arrange_proj_kernel(sizes):
    def kernel(where, own, oth, out):
        h, p, c = where[0], where[1], where[2]

        def work(cores):
            for d in range(out.shape[0]):
                rest, fi = divmod(d, 2)
                rest, ci = divmod(rest, 2)
                rest, xi = divmod(rest, 2)
                hi, gi = divmod(rest, sizes["g"])
                k = jnp.bitwise_xor(p, 2 * fi + xi)
                place = (jnp.bitwise_xor(h, hi) * sizes["g"] + gi) * TP
                out[d] = jnp.concatenate([cores[ci][k, place + q] for q in range(TP)], 1)

        by_core(c, own, oth, work)

    return kernel


def finish_feed_kernel(where, *refs):
    pieces, (wf_out, wo_out, cols) = refs[:TP], refs[TP:]
    p = where[1]
    shard = wf_out.shape[1]
    block = D // 2
    order = interleave(shard)
    for l in range(LAYERS):
        for k in range(TP):
            cols[jnp.bitwise_xor(p, k)] = pieces[k][:, 2 * D * l : 2 * D * (l + 1)]
        fc = [cols[q, :, :D].astype(f32) for q in range(TP)]
        for b in range(wf_out.shape[2] // block):
            lanes = slice(b * block // TP, (b + 1) * block // TP)
            joined = jnp.concatenate([item[:, lanes] for item in fc], 1).astype(bf16)
            wf_out[l, :, b * block : (b + 1) * block] = dot(joined, order)
        for q in range(TP):
            wo_out[l, q] = cols[q, :, D:].astype(f32)


def finish_mixed_kernel(where, last, m0, m1, m2, m3, wq_out, wp_out, *refs):
    small_outs, (cols, square) = refs[:8], refs[8:]
    p = where[1]
    shard = wq_out.shape[1]
    columns = jnp.zeros((shard, 128), f32)
    for q in range(TP):
        total = jnp.zeros((shard, D + 128), f32)
        for copy in range(last.shape[0] // TP):
            total = total + last[(copy * 2 + q % 2) * 2 + q // 2].astype(f32)
        columns = columns + total[:, D:]
        cols[0, q] = total[:, :D]
    for k, m in enumerate((m0, m1, m2, m3)):
        cols[1, jnp.bitwise_xor(p, k)] = m[:, 2 * D * LAYERS :].astype(f32)
    for l in range(LAYERS):
        for j in range(3):
            wq_out[l, :, j * D : (j + 1) * D] = jnp.concatenate(
                [cols[l, q, :, j * PW : (j + 1) * PW] for q in range(TP)], 1
            )
        wp_out[l] = jnp.concatenate([cols[l, q, :, 3 * PW :] for q in range(TP)], 1)
    square[...] = jnp.zeros_like(square)
    square[:shard, :] = columns
    lines = square[...].T
    at = 0
    for l in range(LAYERS):
        for out in small_outs:
            for first in range(0, out.shape[1], shard):
                out[l : l + 1, first : first + shard] = lines[at : at + 1, :shard]
                at += 1


def enter_kernel(first, index):
    def kernel(where, table, *refs):
        if first:
            *inputs, wq, x_out, xo_out, n_out, q_out, kv_out, u_out = refs
        else:
            mid, *inputs, wq, x_out, xo_out, n_out, q_out, kv_out = refs
        t = table
        gain, shift, bias = (t[8 * index + i : 8 * index + i + 1, :] for i in (2, 3, 6))
        rows = n_out.shape[0] // TP
        for k in range(TP):
            at = slice(k * rows, (k + 1) * rows)
            x = inputs[k][...].astype(f32)
            if not first:
                x = mid[at, :] + x + t[8 * (index - 1) + 1 : 8 * (index - 1) + 2, :]
            x_out[at, :] = x
            if k == 0:
                xo_out[...] = x
            unit, _ = unit_rows(x)
            n_out[at, :] = (unit * gain + shift).astype(bf16)
            if first:
                u_out[at, :] = unit.astype(bf16)
        got = (dot(n_out[...], wq[...]) + bias[:, : 3 * PW]).astype(bf16)
        kv_out[...] = got[:, PW:]
        q_out[...] = got[:, :PW]

    return kernel


def tile_rows(p, t, size):
    return pl.multiple_of((jnp.bitwise_xor(t % TP, p) * 2 + t // TP) * size, size)


def mask_of(c, chunk, size):
    a = lax.broadcasted_iota(jnp.int32, (chunk, 2 * chunk), 0)
    b = lax.broadcasted_iota(jnp.int32, (chunk, 2 * chunk), 1)
    ahead = lax.div(b - chunk, size) < lax.div(a, size) + c
    return jnp.where(b < chunk, b - a, jnp.where(ahead, 0, 1)) <= 0


def by_position(p, count, q_ref, own_ref, oth_ref, qn, kc, vc):
    size = count // (2 * TP)
    for t in range(2 * TP):
        at = pl.ds(tile_rows(p, t, size), size)
        qn[t * size : (t + 1) * size, :] = q_ref[at, :]
        for source, first in ((own_ref, 0), (oth_ref, 2)):
            here = slice((t // 2 * 4 + first + t % 2) * size, (t // 2 * 4 + first + t % 2 + 1) * size)
            both = source[at, :]
            kc[here, :] = both[:, :PW]
            vc[here, :] = both[:, PW:]


def attend_kernel(where, q_ref, own_ref, oth_ref, out_ref, lse_ref, wide_ref, qn, kc, vc):
    p, c = where[1], where[2]
    count = q_ref.shape[0]
    size = count // (2 * TP)
    chunk = 2 * size
    by_position(p, count, q_ref, own_ref, oth_ref, qn, kc, vc)
    allowed = mask_of(c, chunk, size)
    for j in range(count // chunk):
        rows = slice(j * chunk, (j + 1) * chunk)
        past, last = slice(0, 2 * j * chunk), slice(2 * j * chunk, 2 * (j + 1) * chunk)
        outs = []
        for h in range(PH):
            lanes = slice(h * HD, (h + 1) * HD)
            q = qn[rows, lanes]
            scores = [jnp.where(allowed, dot(q, kc[last, lanes], NT) * 0.125, -1e30)]
            if j > 0:
                scores.append(dot(q, kc[past, lanes], NT) * 0.125)
            top = functools.reduce(jnp.maximum, [jnp.max(v, -1, keepdims=True) for v in scores])
            weights = [jnp.exp(v - top) for v in scores]
            total = sum(jnp.sum(v, -1, keepdims=True) for v in weights)
            out = dot(weights[0].astype(bf16), vc[last, lanes])
            if j > 0:
                out = out + dot(weights[1].astype(bf16), vc[past, lanes])
            outs.append(out / total)
            lse_ref[rows, h : h + 1] = top + jnp.log(total)
        out = jnp.concatenate(outs, 1)
        wide_ref[rows, :] = out
        low = out.astype(bf16)
        for t in (2 * j, 2 * j + 1):
            out_ref[pl.ds(tile_rows(p, t, size), size), :] = low[(t - 2 * j) * size : (t - 2 * j + 1) * size]


def middle_kernel(index):
    def kernel(where, table, o0, o1, o2, o3, wp, x, wf, wo, mid_out, mo_out, heads_out, n_out, slope_out, act_out, y0, y1, y2, y3, got):
        p = where[1]
        t = table
        b_proj, gain, shift, b_up = (t[8 * index + i : 8 * index + i + 1, :] for i in (0, 4, 5, 7))
        rows = x.shape[0] // TP
        for k, o in enumerate((o0, o1, o2, o3)):
            for m in range(TP):
                got[k, m * rows : (m + 1) * rows, :] = o[(m ^ k) * rows : ((m ^ k) + 1) * rows, :]
        heads_out[...] = jnp.concatenate([got[jnp.bitwise_xor(p, q)] for q in range(TP)], 1)
        for m, y in enumerate((y0, y1, y2, y3)):
            at = slice(m * rows, (m + 1) * rows)
            mid = x[at, :] + dot(heads_out[at, :], wp[...]) + b_proj
            mid_out[at, :] = mid
            if m == 0:
                mo_out[...] = mid
            unit, _ = unit_rows(mid)
            n_out[at, :] = (unit * gain + shift).astype(bf16)
        up = dot(n_out[...], wf[...]) + b_up
        square = up * up
        bent = jnp.tanh(ROOT * up * (1.0 + 0.044715 * square))
        half = 0.5 * (1.0 + bent)
        act_out[...] = (up * half).astype(bf16)
        slope_out[...] = (half + up * half * (1.0 - bent) * (ROOT * (1.0 + 3 * 0.044715 * square))).astype(bf16)
        for m, y in ((3, y3), (2, y2), (1, y1), (0, y0)):
            at = slice(m * rows, (m + 1) * rows)
            y[...] = dot(act_out[at, :], wo[...]).astype(y.dtype)

    return kernel


def part_sums(parts, values, acc):
    acc[...] = jnp.zeros(acc.shape, f32)
    rows = parts[0].shape[0]
    for k, part in enumerate(parts):
        unit, _ = unit_rows(values[k * rows : (k + 1) * rows, :])
        part = part[...].astype(f32)
        acc[0:1, :] += jnp.sum(part * unit, 0, keepdims=True)
        acc[1:2, :] += jnp.sum(part, 0, keepdims=True)


def feed_back_kernel(where, g0, g1, g2, g3, slope, wo, wf, gu_out, y0, y1, y2, y3):
    rows = g0.shape[0]
    for k, (g, y) in enumerate(((g0, y0), (g1, y1), (g2, y2), (g3, y3))):
        at = slice(k * rows, (k + 1) * rows)
        g_up = (slope[at, :].astype(f32) * dot(g[...], wo[...], NT)).astype(bf16)
        gu_out[at, :] = g_up
        y[...] = dot(g_up, wf[...], NT).astype(y.dtype)


def norm_back_kernel(index, which):
    def kernel(where, value, grad, table, r0, r1, r2, r3, g_out, low_out, sum_out):
        gain = table[8 * index + which : 8 * index + which + 1, :]
        unit, scale = unit_rows(value[...])
        cot = r0[...].astype(f32) + r1[...].astype(f32) + r2[...].astype(f32) + r3[...].astype(f32)
        inner = cot * gain
        moved = scale * (
            inner - jnp.mean(inner, -1, keepdims=True) - unit * jnp.mean(inner * unit, -1, keepdims=True)
        )
        total = grad[...].astype(f32) + moved
        g_out[...] = total
        low = total.astype(bf16)
        low_out[...] = low
        sum_out[...] = jnp.zeros(sum_out.shape, f32)
        sum_out[0:1, :] = jnp.sum(low.astype(f32), 0, keepdims=True)

    return kernel


def attend_back_kernel(where, q_ref, own_ref, oth_ref, wide_ref, lse_ref, wp, g0, g1, g2, g3, dq_ref, down_ref, doth_ref, local, gn, qn, kc, vc, dqn, dkc, dvc):
    p, c = where[1], where[2]
    count = q_ref.shape[0]
    size = count // (2 * TP)
    chunk = 2 * size
    rows_of = g0.shape[0]
    by_position(p, count, q_ref, own_ref, oth_ref, qn, kc, vc)
    mine = wp[pl.ds(pl.multiple_of(p * PW, PW), PW), :]
    for k, g in enumerate((g0, g1, g2, g3)):
        local[k * rows_of : (k + 1) * rows_of, :] = dot(g[...], mine, NT)
    for t in range(2 * TP):
        gn[t * size : (t + 1) * size, :] = local[pl.ds(tile_rows(p, t, size), size), :].astype(bf16)
    product = gn[...].astype(f32) * wide_ref[...]
    delta = [jnp.sum(product[:, h * HD : (h + 1) * HD], -1, keepdims=True) for h in range(PH)]
    allowed = mask_of(c, chunk, size)
    dqn[...] = jnp.zeros_like(dqn)
    for b in range(count // chunk):
        rows, keys = slice(b * chunk, count), slice(2 * b * chunk, 2 * (b + 1) * chunk)
        dqs, dks, dvs = [], [], []
        for h in range(PH):
            lanes = slice(h * HD, (h + 1) * HD)
            q, g, k = qn[rows, lanes], gn[rows, lanes], kc[keys, lanes]
            scores = dot(q, k, NT) * 0.125 - lse_ref[rows, h : h + 1]
            first = jnp.where(allowed, scores[:chunk], -1e30)
            if b + 1 < count // chunk:
                first = jnp.concatenate([first, scores[chunk:]], 0)
            probs = jnp.exp(first)
            grad = dot(g, vc[keys, lanes], NT)
            ds = (probs * (grad - delta[h][b * chunk :])).astype(bf16)
            dqs.append(dot(ds, k))
            dks.append(dot(ds, q, TN))
            dvs.append(dot(probs.astype(bf16), g, TN))
        dqn[rows, :] += jnp.concatenate(dqs, 1)
        dkc[keys, :] = jnp.concatenate(dks, 1) * 0.125
        dvc[keys, :] = jnp.concatenate(dvs, 1)
    for t in range(2 * TP):
        at = pl.ds(tile_rows(p, t, size), size)
        for out, first in ((doth_ref, 2), (down_ref, 0)):
            here = slice((t // 2 * 4 + first + t % 2) * size, (t // 2 * 4 + first + t % 2 + 1) * size)
            out[at, :] = jnp.concatenate([dkc[here, :], dvc[here, :]], 1).astype(out.dtype)
        dq_ref[at, :] = (dqn[t * size : (t + 1) * size, :] * 0.125).astype(bf16)


def leave_kernel(where, dq, dkv, more, wq, gq_out, y0, y1, y2, y3):
    gq_out[:, :PW] = dq[...]
    gq_out[:, PW:] = (dkv[...].astype(f32) + more[...].astype(f32)).astype(bf16)
    rows = y0.shape[0]
    for k, y in ((3, y3), (2, y2), (1, y1), (0, y0)):
        y[...] = dot(gq_out[k * rows : (k + 1) * rows, :], wq[...], NT).astype(y.dtype)


def arrange_kernel(widths):
    def kernel(where, own, oth, *outs):
        p, c = where[1], where[2]

        def work(cores):
            for d in range(outs[0].shape[0]):
                rest, f = divmod(d, 2)
                rest, core = divmod(rest, 2)
                copy, x = divmod(rest, 2)
                block = copy * TP + jnp.bitwise_xor(2 * f + x, p)
                at = 0
                for out, width in zip(outs, widths):
                    out[d] = cores[core][block, :, at : at + width]
                    at += width

        by_core(c, own, oth, work)

    return kernel


def scatter_blocks(where, blocks, keep, give):
    p, c = where[1], where[2]
    for i in range(keep.shape[0]):
        copy, k = divmod(i, TP)
        chip = jnp.bitwise_xor(p, k)
        for out, core in ((keep, c), (give, 1 - c)):
            out[i] = blocks[((copy * 2 + lax.rem(chip, 2)) * 2 + core) * 2 + lax.div(chip, 2)]


def feed_weights_kernel(where, normed, g_up, act, g0, g1, g2, g3, mid, y0, y1, y2, y3, keep, give, b_out, sums, blocks):
    part_sums((y0, y1, y2, y3), mid, sums)
    sums[2:3, :] = jnp.sum(g0[...].astype(f32), 0, keepdims=True)
    b_out[...] = jnp.zeros(b_out.shape, f32)
    b_out[0:1, :] = jnp.sum(g_up[...].astype(f32), 0, keepdims=True)
    width = normed.shape[1]
    shard = keep.shape[1]
    g = jnp.concatenate([g0[...], g1[...], g2[...], g3[...]], 0)
    for at, (a, b) in ((0, (normed, g_up[...])), (width, (act, g))):
        value = dot(a[...], b, TN)
        for d in range(blocks.shape[0]):
            blocks[d, :, at : at + width] = value[d * shard : (d + 1) * shard].astype(bf16)
    scatter_blocks(where, blocks, keep, give)


def mixed_weights(where, normed, g_qkv, heads, g_attn):
    p = where[1]
    value = dot(normed[...], g_qkv[...], TN)
    whole = dot(heads[...], jnp.concatenate([g[...] for g in g_attn], 0), TN)
    mine = whole[:, :PW]
    for q in range(1, TP):
        mine = jnp.where(p == q, whole[:, q * PW : (q + 1) * PW], mine)
    return jnp.concatenate([value, mine], 1)


def mixed_weights_kernel(where, normed, g_qkv, heads, g0, g1, g2, g3, x, y0, y1, y2, y3, keep, give, b_out, sums, blocks):
    part_sums((y0, y1, y2, y3), x, sums)
    b_out[...] = jnp.zeros(b_out.shape, f32)
    b_out[0:1, : 3 * PW] = jnp.sum(g_qkv[...].astype(f32), 0, keepdims=True)
    value = mixed_weights(where, normed, g_qkv, heads, (g0, g1, g2, g3))
    shard = blocks.shape[1]
    for d in range(blocks.shape[0]):
        blocks[d] = value[d * shard : (d + 1) * shard].astype(bf16)
    scatter_blocks(where, blocks, keep, give)


def leave_last_kernel(where, dq, dkv, more_keys, wq, unit, normed, heads, g0, g1, g2, g3, *refs):
    sums, refs = refs[: 5 * LAYERS - 2], refs[5 * LAYERS - 2 :]
    keep, give, y0, y1, y2, y3, blocks, lines, more, g_qkv = refs
    leave_kernel(where, dq, dkv, more_keys, wq, g_qkv, y0, y1, y2, y3)
    part = jnp.concatenate([y[...].astype(f32) for y in (y0, y1, y2, y3)], 0)
    norm1_first = [jnp.sum(part * unit[...].astype(f32), 0, keepdims=True), jnp.sum(part, 0, keepdims=True)]
    b_qkv = jnp.sum(g_qkv[...].astype(f32), 0, keepdims=True)
    p, c = where[1], where[2]
    devices, shard = blocks.shape[:2]
    per = PW // (2 * shard)
    lines[...] = jnp.zeros_like(lines)
    more[...] = jnp.zeros_like(more)
    for l in range(LAYERS):
        b_proj, norm2, fc = sums[3 * l : 3 * l + 3]
        if l == 0:
            (gain, shift), qkv = norm1_first, jnp.concatenate([b_qkv, jnp.zeros((1, D - 3 * PW), f32)], 1)
        else:
            gain, shift, qkv = sums[6][0:1, :], sums[6][1:2, :], sums[7][0:1, :]
        base = SLOTS * l
        rows = (b_proj[0:1, :], norm2[2:3, :], gain, shift, norm2[0:1, :], norm2[1:2, :])
        for i, row in enumerate(rows):
            lines[base + i : base + i + 1, :] = row
        for q in range(TP):
            lines[base + 8 + q : base + 9 + q, :] = jnp.where(p == q, fc[0:1, :], 0.0)
        bias = jnp.broadcast_to(qkv, (128, D)).T
        for first, start in ((0, 0), (devices // 2, 2 * PW)):
            for j in range(2 * per):
                lane = base + 6 + j % 2
                more[first + p * per + j // 2, :, lane : lane + 1] = bias[
                    start + j * shard : start + (j + 1) * shard, 0:1
                ]
    columns = lines[...].T
    value = mixed_weights(where, normed, g_qkv, heads, (g0, g1, g2, g3))
    for d in range(devices):
        at = slice(d * shard, (d + 1) * shard)
        blocks[d] = jnp.concatenate([value[at], columns[at] + more[d]], 1).astype(bf16)
    for i in range(keep.shape[0]):
        rest, f = divmod(i, 2)
        keep[i] = blocks[(rest * 2 + c) * 2 + f]
        give[i] = blocks[(rest * 2 + 1 - c) * 2 + f]


def attend(q, keys_values, mask):
    k, v = keys_values[:, :PW], keys_values[:, PW:]
    q, k, v = (item.reshape(-1, PH, HD) for item in (q, k, v))
    scores = jnp.einsum("qhe,khe->hqk", q, k, preferred_element_type=f32) * 0.125
    scores = jnp.where(mask, scores, -1e30)
    top = jnp.max(scores, -1, keepdims=True)
    weights = jnp.exp(scores - top)
    total = jnp.sum(weights, -1, keepdims=True)
    out = jnp.einsum("hqk,khe->qhe", (weights / total).astype(bf16), v, preferred_element_type=f32)
    return out.reshape(-1, PW).astype(bf16), top + jnp.log(total)


def attend_back(q, keys_values, mask, log_total, grad_out):
    k, v = keys_values[:, :PW], keys_values[:, PW:]
    q, k, v, g = (item.reshape(-1, PH, HD) for item in (q, k, v, grad_out))
    scores = jnp.einsum("qhe,khe->hqk", q, k, preferred_element_type=f32) * 0.125
    probs = jnp.where(mask, jnp.exp(scores - log_total), 0.0)
    grad_probs = jnp.einsum("qhe,khe->hqk", g, v, preferred_element_type=f32)
    delta = jnp.sum(probs * grad_probs, -1, keepdims=True)
    grad_scores = (probs * (grad_probs - delta)).astype(bf16)
    dq = 0.125 * jnp.einsum("hqk,khe->qhe", grad_scores, k, preferred_element_type=f32)
    dk = 0.125 * jnp.einsum("hqk,qhe->khe", grad_scores, q, preferred_element_type=f32)
    dv = jnp.einsum("hqk,qhe->khe", probs.astype(bf16), g, preferred_element_type=f32)
    dkv = jnp.concatenate([dk.reshape(-1, PW), dv.reshape(-1, PW)], 1)
    return dq.reshape(-1, PW).astype(bf16), dkv


def body(tokens, w_qkv, b_qv, w_proj, b_proj, ln1_gain, ln1_bias, ln2_gain, ln2_bias, w_fc, b_fc, w_out, b_out, d_out):
    size = {name: lax.axis_size(name) for name in ALL}
    devices = math.prod(size.values())
    rows = tokens.shape[1]
    shard = w_qkv.shape[1]
    ff = w_fc.shape[2]
    h, g, x_at, c, f = (lax.axis_index(name) for name in ALL)
    p = 2 * f + x_at
    where = jnp.stack([h, p, c, g, f]).astype(jnp.int32)
    many = size["g"] > 1

    homes = [(a, b) for a in range(size["h"]) for b in range(size["f"])]
    outward = [
        [(a * 2 + b, (2 * ((a // 2 + turn) % 2) + b) * 2 + a % 2) for a, b in homes] for turn in range(2)
    ]

    def both_ways(value, low, moves):
        sent = [lax.dynamic_index_in_dim(value, i, 0, keepdims=False) for i in (low, 1 - low)]
        return [lax.ppermute(item, ("h", "f"), move) for item, move in zip(sent, moves)]

    def own_sequence(value):
        one, two = both_ways(value, h // 2, outward)
        both = jnp.where(h // 2 == 0, jnp.stack([one, two]), jnp.stack([two, one]))
        return [both[:, i].reshape(-1, D) for i in range(2)]

    def back_to_blocks(value):
        moves = [[(b, a) for a, b in move] for move in outward]
        one, two = both_ways(value.reshape(2, rows, -1), h // 2, moves)
        return jnp.where(h // 2 == 0, jnp.stack([one, two]), jnp.stack([two, one]))

    smalls = (b_proj, b_out, ln1_gain, ln1_bias, ln2_gain, ln2_bias, b_qv, b_fc)
    by_part = w_out.reshape(LAYERS, TP, shard, D)

    def plane(pieces):
        return jnp.stack([pieces[0]] + [chip_swap(pieces[k], k) for k in range(1, TP)])

    def fetch(pieces):
        return lax.all_gather(pieces, COPIES, axis=0, tiled=True)

    def arrange(own, *widths):
        return [
            item.reshape(D, -1)
            for item in launch(
                arrange_kernel(widths), "arrange", [((devices, shard, width), bf16) for width in widths],
                where, own, swap(own, "c"),
            )
        ]

    *first, proj = launch(
        first_pieces_kernel, "first_pieces",
        [((shard, 3 * PW + HD), bf16)] * TP + [((TP, shard, PW), bf16)], where, w_qkv, w_proj, *smalls,
        scratch=[pltpu.VMEM((128, 128), f32), pltpu.VMEM((TP, shard, 3 * PW + HD), bf16)],
    )
    feed = launch(
        layer_pieces_kernel, "layer_pieces", [((shard, (2 * LAYERS + 1) * D + 3 * PW + HD), bf16)] * TP,
        where, w_fc, by_part, w_proj, w_qkv, scratch=[pltpu.VMEM((TP, shard, LAYERS * D + 3 * PW + HD), bf16)],
    )
    x_own, g_low = own_sequence(jnp.stack([tokens, d_out], 1))
    feed, first, x_own, g_low = lax.optimization_barrier((feed, first, x_own, g_low))
    first, feed, x_own = lax.optimization_barrier((plane(first), feed, x_own))
    feed = [feed[0]] + [chip_swap(feed[k], k) for k in range(1, TP)]
    first = after(jnp.concatenate([first, proj], 2), feed[1])
    if many:
        first = lax.all_gather(first, "g", axis=0, tiled=True)
    first = jnp.concatenate([first] + [swap(first, "h", k) for k in range(1, size["h"])], 0)

    def part_of(start, stop):
        return jnp.stack([item[:, start:stop] for item in feed])

    next_feed, next_mixed = part_of(2 * D, 4 * D), part_of(4 * D, feed[0].shape[1])
    feed = part_of(0, 2 * D)
    x_pieces = share(after(x_own, feed))
    feed = fetch(feed)
    proj = after(first[:, :, 3 * PW + HD :], x_pieces)
    proj = [proj] + [chip_swap(proj, k) for k in range(1, TP)]
    first = jnp.concatenate([first, swap(first, "c")], 0)
    wq, table = launch(
        arrange_first_kernel(size), "arrange_first",
        [((devices, shard, 3 * PW), bf16), ((LAYERS * 8, D), f32)], where, first, flops=1 << 34,
        scratch=[pltpu.VMEM((D, 128), f32), pltpu.VMEM((devices, shard, HD), f32)],
    )
    wq = [wq.reshape(D, 3 * PW), None]
    wf, wo, wp = [None] * LAYERS, [None] * LAYERS, [None] * LAYERS
    count = TP * x_pieces[0].shape[0]
    own = count // TP
    if many:
        second = jnp.arange(2)[None, :, None]
        inside = jnp.arange(rows)[None, None, :]
        chip = p ^ jnp.arange(TP)[:, None, None]

        def positions(group, core):
            place = (chip // 2 + 2 * second) * size["g"] + group
            return (((place * 2 + chip % 2) * 2 + core) * rows + inside).reshape(-1)

        q_pos = positions(g, c)
        k_pos = jnp.concatenate([positions(gi, core) for gi in range(size["g"]) for core in (0, 1)])
        mask = (k_pos[None, :] <= q_pos[:, None])[None]

    def all_keys(kv, other):
        both = jnp.where(c == 0, jnp.stack([kv, other]), jnp.stack([other, kv])).reshape(-1, kv.shape[1])
        return lax.all_gather(both, "g", axis=0, tiled=True)

    saved = []
    state = tuple(x_pieces)
    for l in range(LAYERS):
        x, x_own, normed, q, kv, *unit = launch(
            enter_kernel(l == 0, l), f"enter_{l}",
            [((count, D), f32), ((own, D), f32), ((count, D), bf16), ((count, PW), bf16), ((count, 2 * PW), bf16)]
            + [((count, D), bf16)] * (l == 0),
            where, table, *state, wq[l], flops=2 * count * D * 3 * PW,
        )
        other = swap(kv, "c")
        if many:
            keys = all_keys(kv, other)
            out, lse = attend(q, keys, mask)
            wide = None
        else:
            keys = None
            out, lse, wide = launch(
                attend_kernel, f"attend_{l}", [((count, PW), bf16), ((count, PH), f32), ((count, PW), f32)],
                where, q, kv, other,
                scratch=[pltpu.VMEM((count, PW), bf16)] + [pltpu.VMEM((2 * count, PW), bf16)] * 2,
                flops=4 * count * 2 * count * PW,
            )
        if l == 0:
            next_mixed, next_feed = fetch(next_mixed), fetch(next_feed)
        if l == 0:
            out, proj = lax.optimization_barrier((out, proj))
        outs = share(out)
        if l == 0:
            proj = jnp.stack(proj)
            (proj,) = launch(
                arrange_proj_kernel(size), "arrange_proj", [((devices, shard, D), bf16)],
                where, proj, swap(proj, "c"),
            )
            prepared = *arrange(after(feed, out), D, D), proj.reshape(D, D)
        if l + 1 == LAYERS:
            pieces = share(after(g_low, outs[1]))
            prepared = *arrange(after(next_feed, out), D, D), prepared
        wf[l], wo[l], wp[l] = prepared
        mid, mid_own, heads, normed2, slope, act, y0, y1, y2, y3 = launch(
            middle_kernel(l), f"middle_{l}",
            [((count, D), f32), ((own, D), f32), ((count, D), bf16), ((count, D), bf16), ((count, D), bf16), ((count, D), bf16)]
            + [((own, D), bf16)] * 4,
            where, table, *outs, wp[l], x, wf[l], wo[l],
            scratch=[pltpu.VMEM((TP, count, PW), bf16)], flops=6 * count * D * D,
        )
        if l + 1 < LAYERS:
            total = y0.astype(f32)
            for k, y in ((1, y1), (2, y2), (3, y3)):
                total = total + chip_swap(y, k).astype(f32)
        saved.append((x, x_own, normed, q, kv, other, keys, lse, wide, heads, mid, mid_own, normed2, slope, act, unit))
        if l + 1 < LAYERS:
            next_mixed, total = lax.optimization_barrier((next_mixed, total))
            state = (mid, *share(total.astype(bf16)))
            prepared, wq[l + 1] = arrange(next_mixed, D, 3 * PW)
    last_parts = [y0, y1, y2, y3]

    copies = devices // (2 * TP)
    halves = [((copies * TP, shard, 2 * D), bf16)] * 2

    def reduce_copies(keep, got):
        total = (keep.astype(f32) + got.astype(f32)).astype(bf16)
        return lax.psum_scatter(total, COPIES, scatter_dimension=0, tiled=True)

    def by_owner(sums):
        return [sums[0]] + [chip_swap(sums[k], k) for k in range(1, TP)]

    line = ((8, D), f32)
    parts = [((own, D), bf16)] * 4
    g_own = g_low
    sums = [None] * LAYERS
    for l in reversed(range(LAYERS)):
        x, x_own, normed, q, kv, other, keys, lse, wide, heads, mid, mid_own, normed2, slope, act, unit = saved[l]
        g_up, y0, y1, y2, y3 = launch(
            feed_back_kernel, f"feed_back_{l}", [((count, D), bf16)] + parts,
            where, *pieces, slope, wo[l], wf[l], flops=4 * count * D * D,
        )
        got = [chip_swap(y, k) for k, y in ((3, y3), (2, y2), (1, y1))][::-1]
        keep, give, b_fc_sum, norm2_sum = launch(
            feed_weights_kernel, f"feed_weights_{l}", halves + [line, line],
            where, normed2, g_up, act, *pieces, mid, y0, y1, y2, y3,
            scratch=[pltpu.VMEM((devices, shard, 2 * D), bf16)], flops=4 * count * D * D,
        )
        if l + 1 == LAYERS:
            got, keep, give = lax.optimization_barrier((got, keep, give))
        else:
            got, keep, give, mixed, output = lax.optimization_barrier((got, keep, give, mixed, output))
        give = swap(give, "c")
        g_own, g_low, b_proj_sum = launch(
            norm_back_kernel(l, 4), f"norm2_back_{l}", [((own, D), f32), ((own, D), bf16), line],
            where, mid_own, g_own, table, y0, *got,
        )
        give, g_low = lax.optimization_barrier((give, g_low))
        feed = reduce_copies(keep, give)
        pieces = share(g_low)
        if l + 1 == LAYERS:
            last_parts, pieces[1] = lax.optimization_barrier((last_parts, pieces[1]))
            total = last_parts[0].astype(f32)
            for k in range(1, TP):
                total = total + chip_swap(last_parts[k], k).astype(f32)
            meanwhile = (mid_own + total + table[8 * l + 1 : 8 * l + 2]).astype(bf16)
        if many:
            g_attn = jnp.concatenate(pieces, 0)
            mine = lax.dynamic_slice_in_dim(wp[l], p * PW, PW, 0)
            dq, dkv = attend_back(q, keys, mask, lse, dot(g_attn, mine, NT).astype(bf16))
            dkv = lax.psum_scatter(dkv, "g", scatter_dimension=0, tiled=True).reshape(2, count, 2 * PW)
            dkv, give = (lax.dynamic_index_in_dim(dkv, i, 0, keepdims=False) for i in (c, 1 - c))
            give = give.astype(bf16)
        else:
            dq, dkv, give = launch(
                attend_back_kernel, f"attend_back_{l}",
                [((count, PW), bf16)] + [((count, 2 * PW), bf16)] * 2,
                where, q, kv, other, wide, lse, wp[l], *pieces,
                scratch=[pltpu.VMEM((count, PW), f32), pltpu.VMEM((count, PW), bf16), pltpu.VMEM((count, PW), bf16)]
                + [pltpu.VMEM((2 * count, PW), bf16)] * 2 + [pltpu.VMEM((count, PW), f32)]
                + [pltpu.VMEM((2 * count, PW), f32)] * 2,
                flops=10 * count * 2 * count * PW,
            )
        more = swap(give, "c")
        if l > 0:
            more, output = lax.optimization_barrier((more, meanwhile))
            output = back_to_blocks(output)
        sums[l] = (b_proj_sum, norm2_sum, b_fc_sum)
        if l > 0:
            g_qkv, y0, y1, y2, y3 = launch(
                leave_kernel, f"leave_{l}", [((count, 3 * PW), bf16)] + parts,
                where, dq, dkv, more, wq[l], flops=2 * count * D * 3 * PW,
            )
            got = [chip_swap(y, k) for k, y in ((3, y3), (2, y2), (1, y1))][::-1]
            keep, give, b_qkv_sum, norm1_sum = launch(
                mixed_weights_kernel, f"mixed_weights_{l}", [((copies * TP, shard, D), bf16)] * 2 + [line, line],
                where, normed, g_qkv, heads, *pieces, x, y0, y1, y2, y3,
                scratch=[pltpu.VMEM((devices, shard, D), bf16)], flops=4 * count * D * D,
            )
            got, keep, give, feed_last = lax.optimization_barrier((got, keep, give, feed))
            give = swap(give, "c")
            sums[l] = sums[l] + (norm1_sum, b_qkv_sum)
        else:
            keep, give, y0, y1, y2, y3 = launch(
                leave_last_kernel, "leave_last", [((copies * TP, shard, D + 128), bf16)] * 2 + parts,
                where, dq, dkv, more, wq[l], *unit, normed, heads, *pieces, *sums[0], *sums[1],
                scratch=[pltpu.VMEM((devices, shard, D + 128), bf16), pltpu.VMEM((128, D), f32),
                         pltpu.VMEM((devices, shard, 128), f32), pltpu.VMEM((count, 3 * PW), bf16)],
                flops=6 * count * D * D,
            )
            give, feed = lax.optimization_barrier((give, feed))
            last = (keep.astype(f32) + swap(give, "c").astype(f32)).astype(bf16)
            got = [chip_swap(y, k) for k, y in ((3, y3), (2, y2), (1, y1))][::-1]
            last = after(last, got[0])
            reduced = by_owner(after(jnp.concatenate([feed, feed_last, mixed], 2), last))
            last = lax.all_to_all(last, ("h", "g", "x", "f"), 0, 0, tiled=True)
        g_own, g_low, _ = launch(
            norm_back_kernel(l, 2), f"norm1_back_{l}", [((own, D), f32), ((own, D), bf16), line],
            where, x_own, g_own, table, y0, *got,
        )
        if l > 0:
            give, g_low = lax.optimization_barrier((give, g_low))
            mixed = reduce_copies(keep, give)
            pieces = share(g_low)
    g_low, reduced[1] = lax.optimization_barrier((g_low, reduced[1]))
    grad_tokens = back_to_blocks(g_low).astype(f32)
    d_wf, d_wo = launch(
        finish_feed_kernel, "finish_feed", [((LAYERS, shard, ff), f32), ((LAYERS, TP, shard, D), f32)],
        where, *reduced,
        scratch=[pltpu.VMEM((TP, shard, 2 * D), bf16)],
    )
    d_wo = d_wo.reshape(w_out.shape)
    d_wq, d_wp, d_b_proj, d_b_out, d_g1, d_s1, d_g2, d_s2, d_b_qv, d_b_fc = launch(
        finish_mixed_kernel, "finish_mixed",
        [((LAYERS, shard, 3 * D), f32), ((LAYERS, shard, D), f32)] + [(item.shape, f32) for item in smalls],
        where, last, *reduced, scratch=[pltpu.VMEM((LAYERS, TP, shard, D), f32), pltpu.VMEM((128, 128), f32)],
    )
    return (output, grad_tokens, d_wq, d_b_qv, d_wp, d_b_proj, d_g1, d_s1, d_g2, d_s2, d_wf, d_b_fc, d_wo, d_b_out)


def solution(mesh):
    ctx, pair = mesh.shape["ctx"], mesh.shape["fsdp"]
    view = Mesh(mesh.devices.reshape(4, ctx // 16, 2, 2, pair), ALL)
    along = ("h", "g", "x", "c")
    token = P("f", along, None)
    matrix = P(None, ALL, None)
    line = P(None, ALL)
    in_specs = (token, matrix, line, matrix, line, line, line, line, line, matrix, line, matrix, line, token)
    out_specs = (token, token, matrix, line, matrix, line, line, line, line, line, matrix, line, matrix, line)
    return jax.shard_map(body, mesh=view, in_specs=in_specs, out_specs=out_specs, check_vma=False)
```
